128 devices in a mesh: group: 8 (over x_hi, z), helper: 16 (over y, x_lo, core).
Axes of the slice: x: 4 (x_hi: 2, x_lo: 2; x = x_hi * 2 + x_lo), y: 4, z: 4, core: 2. Of those that a mesh axis runs over, the one named last changes fastest.
Arguments:
- embeddings: float32 [8, 8192, 1024], P('group', 'helper'), may hold values from -420 to 420
- sizes: int32 [8], replicated, may hold values from 4096 to 8192, as said below
- ranks: int32 [8, 8192], P('group', 'helper'), may hold values from 0 to 8191, each once within a row
Outputs:
- within: float32 [8, 8192], P('group', 'helper')
- adjacent: float32 [8, 8192], P('group', 'helper')
The draws below stay inside these ranges and needn't reach their ends.
Inputs may be any that keep to these rules, and one draw needn't show every extreme that they name: `sizes`: real rows fill the leading positions of a cluster; at least one cluster is full. Each cluster's ranks are a permutation.
All inputs are finite; a program needn't handle non-finite values.
Results may differ from the reference program's by a relative error of at most 0.00046.
Values may be sent and summed in bfloat16 or wider, within the bound.
No kernel may reach another device: no remote copies, remote signals or barrier semaphores. Data moves between devices by JAX's collectives and lax.ppermute only.
A program may use at most 128 MiB of HBM per device.

```python
import math
import jax
import jax.numpy as jnp
from jax import lax

D = 1024
R_DEV = 512
CLUSTERS = 8
CAP = 8192
N_HELPER = 16


def draw_sizes(key, part):
    key = jax.random.fold_in(key, 11)
    first, second = jax.random.split(key)
    counts = jax.random.randint(first, (CLUSTERS,), CAP // 2, CAP + 1)
    chosen = jax.random.randint(second, (), 0, CLUSTERS)
    return jnp.where(jnp.arange(CLUSTERS) == chosen, CAP, counts).astype(jnp.int32)


def draw_embeddings(key, part):
    key = jax.random.fold_in(key, 23)
    keys = jax.random.split(key, 7)
    base = jnp.clip(jax.random.normal(keys[0], (CLUSTERS, CAP, D), jnp.float32), -6.0, 6.0)
    source_in = jax.random.randint(keys[1], (CLUSTERS, CAP, 1), 0, CAP)
    source_next = jax.random.randint(keys[2], (CLUSTERS, CAP, 1), 0, CAP)
    weight_in = jax.random.uniform(keys[3], (CLUSTERS, CAP, 1), jnp.float32, 0.5, 3.0)
    weight_in = weight_in * (jax.random.uniform(keys[4], (CLUSTERS, CAP, 1)) < 0.5)
    weight_next = jax.random.uniform(keys[5], (CLUSTERS, CAP, 1), jnp.float32, 0.5, 3.0)
    weight_next = weight_next * (jax.random.uniform(keys[6], (CLUSTERS, CAP, 1)) < 0.3)
    partner = jnp.take_along_axis(base, source_in, axis=1)
    neighbour = jnp.take_along_axis(jnp.roll(base, -1, axis=0), source_next, axis=1)
    values = base + weight_in * partner + weight_next * neighbour
    return values.astype(jnp.float32)


def setup_inputs(seed: int = 0) -> dict:
    key_of = jax.random.split(jax.random.key(seed), 4)
    embeddings = draw_embeddings(jax.random.fold_in(key_of[3], 71), 0)
    sizes = draw_sizes(jax.random.fold_in(key_of[3], 71), 0)
    ranks = jax.vmap(lambda own: jax.random.permutation(own, CAP))(jax.random.split(key_of[2], CLUSTERS)).reshape((CLUSTERS, CAP)).astype(jnp.int32)
    return {"embeddings": embeddings, "sizes": sizes, "ranks": ranks}


def normalize(values):
    scale = lax.rsqrt(lax.optimization_barrier(jnp.mean(values * values, axis=-1, keepdims=True)) + 1e-06) / math.sqrt(D)
    return (values * scale).astype(jnp.bfloat16)

def reference(embeddings, sizes, ranks):
    unit = normalize(embeddings).astype(jnp.float32)
    position = jnp.arange(CAP, dtype=jnp.int32)
    real = position[None, :] < sizes[:, None]
    next_unit = jnp.roll(unit, -1, axis=0)
    next_real = jnp.roll(real, -1, axis=0)

    def one_cluster(items):
        keys, key_real, key_rank, other, other_real = items
        blocks = (keys.reshape(N_HELPER, R_DEV, D), key_rank.reshape(N_HELPER, R_DEV), key_real.reshape(N_HELPER, R_DEV))

        def one_block(block):
            queries, query_rank, query_real = block
            scores = jnp.dot(queries, keys.T, precision=lax.Precision.HIGHEST)
            usable = (key_rank[None, :] < query_rank[:, None]) & key_real[None, :]
            best = lax.optimization_barrier(jnp.max(jnp.where(usable, scores, -1.0), axis=1))
            best = jnp.where(query_real, best, 0.0)
            across = jnp.dot(queries, other.T, precision=lax.Precision.HIGHEST)
            nearest = lax.optimization_barrier(jnp.max(jnp.where(other_real[None, :], across, -1.0), axis=1))
            nearest = jnp.where(query_real, nearest, 0.0)
            return (best, nearest)
        best, nearest = lax.map(one_block, blocks)
        return (best.reshape(CAP), nearest.reshape(CAP))
    within, adjacent = lax.map(one_cluster, (unit, real, ranks, next_unit, next_real))
    return (within.astype(jnp.float32), adjacent.astype(jnp.float32))
```

```python
import functools
import math

import jax
import jax.numpy as jnp
from jax import lax
from jax.experimental import pallas as pl
from jax.experimental.pallas import tpu as pltpu
from jax.sharding import PartitionSpec as P

D = 1024
HALF = 256
EXTRA = 8
PAY = HALF + EXTRA
BASE = 64
FAR = 8192.0
LOW = -4.0
AXES = ("group", "helper")
VMEM = pl.BlockSpec(memory_space=pltpu.VMEM)


def place(index):
    group, helper = divmod(index, 16)
    return {
        "part": group // 4,
        "z": group % 4,
        "row": helper // 4,
        "col": (helper // 2) % 2,
        "core": helper % 2,
    }


def number(at):
    return (at["part"] * 4 + at["z"]) * 16 + at["row"] * 4 + at["col"] * 2 + at["core"]


def pairs(col=0, row=0, core=0, cluster=0):
    out = []
    for source in range(128):
        at = place(source)
        step = at["part"] * 4 + at["z"] + cluster
        flip = 1 if step // 4 != at["part"] else 0
        at["part"], at["z"] = (step // 4) % 2, step % 4
        at["col"] = (at["col"] + col + flip) % 2
        at["row"] = (at["row"] + row) % 4
        at["core"] = (at["core"] + core) % 2
        out.append((source, number(at)))
    return out


def send(value, **shift):
    return lax.ppermute(value, AXES, pairs(**shift))


def inner(keys, queries):
    return lax.dot_general(
        keys, queries, (((1,), (1,)), ((), ())), preferred_element_type=jnp.float32
    )


def pack_kernel(left_ref, rows_ref, rank_ref, pay_ref):
    half = pl.program_id(0)
    rows = rows_ref[...]
    scale = lax.rsqrt(jnp.mean(rows * rows, axis=-1, keepdims=True) + 1e-06) / math.sqrt(D)
    pay_ref[0, :HALF, :] = (rows * scale).astype(jnp.bfloat16)
    rank = rank_ref[...]
    position = lax.broadcasted_iota(jnp.int32, (1, HALF), 1) + half * HALF
    real = position < left_ref[0]
    high = jnp.where(real, rank // BASE, int(FAR) // BASE).astype(jnp.float32)
    low = jnp.where(real, rank % BASE, 0).astype(jnp.float32)
    both = jnp.concatenate([high, low, jnp.zeros((1, D - 2 * HALF), jnp.float32)], axis=1)
    pay_ref[0, HALF:, :] = jnp.broadcast_to(both, (EXTRA, D)).astype(jnp.bfloat16)


def packed(rows, ranks, left):
    return pl.pallas_call(
        pack_kernel,
        grid=(2,),
        in_specs=[
            pl.BlockSpec(memory_space=pltpu.SMEM),
            pl.BlockSpec((HALF, D), lambda i: (i, 0)),
            pl.BlockSpec((1, HALF), lambda i: (0, i)),
        ],
        out_specs=pl.BlockSpec((1, PAY, D), lambda i: (i, 0, 0)),
        out_shape=jax.ShapeDtypeStruct((2, PAY, D), jnp.bfloat16),
        name="pack",
        compiler_params=pltpu.CompilerParams(vmem_limit_bytes=16 * 2**20),
        cost_estimate=pl.CostEstimate(flops=4 * 512 * D, bytes_accessed=3 * 2**20, transcendentals=512),
    )(left, rows, ranks)


def rank_row(tail):
    tail = tail[0:1, :].astype(jnp.float32)
    return tail[:, :HALF] * BASE + tail[:, HALF:]


def rank_column(tail):
    return jnp.transpose(jnp.broadcast_to(rank_row(tail), (128, HALF)))


def score_kernel(jobs, row_of, key_of, count, *refs):
    ins, row_ref, key_ref = refs[:count], refs[count], refs[count + 1]

    def halves(index):
        ref = ins[index]
        if len(ref.shape) == 2:
            return [ref]
        return [ref.at[0], ref.at[1]]

    rows = [jnp.full((1, HALF), LOW, jnp.float32) for _ in range(row_ref.shape[0])]
    for job, (kind, keys, queries) in enumerate(jobs):
        views = [view for q in queries for view in halves(q)]
        if kind != "next":
            q_rank = [rank_row(view[HALF:, : 2 * HALF]) for view in views]

        def tile(view, slot, best, kind=kind, views=views):
            best = list(best)
            key = view[:HALF, :]
            if kind != "prev":
                k_rank = rank_column(view[HALF:, : 2 * HALF])
            side = jnp.full((HALF, 128), LOW, jnp.float32)
            for i, query in enumerate(views):
                scores = inner(key, query[:HALF, :])
                parts = []
                for c in range(0, HALF, 128):
                    piece = scores[:, c : c + 128]
                    if kind == "next":
                        parts.append(jnp.where(k_rank < FAR, piece, LOW))
                    elif kind == "prev":
                        side = jnp.maximum(side, jnp.where(q_rank[i][:, c : c + 128] < FAR, piece, LOW))
                    else:
                        earlier = k_rank < q_rank[i][:, c : c + 128]
                        parts.append(jnp.where(earlier, piece, LOW))
                        if kind == "pair":
                            side = jnp.maximum(side, jnp.where(earlier, LOW, piece))
                if parts:
                    top = [jnp.max(part, axis=0, keepdims=True) for part in parts]
                    best[i] = jnp.maximum(best[i], jnp.concatenate(top, axis=1))
            if slot is not None:
                key_ref[slot] = jnp.max(jnp.transpose(side), axis=0, keepdims=True)
            return best

        places = [row_of(job, i) for i in range(len(views))]
        best = [rows[p] if p is not None else jnp.zeros((1, HALF), jnp.float32) for p in places]
        first = key_of(job)
        flat = [k for k in keys if len(ins[k].shape) == 2]
        deep = [k for k in keys if len(ins[k].shape) == 3]
        for n, k in enumerate(flat):
            best = tile(ins[k], None if first is None else first + n, best)
        if deep:

            def step(h, best):
                for n, k in enumerate(deep):
                    slot = None if first is None else first + 2 * n + h
                    best = tile(ins[k].at[h], slot, best)
                return tuple(best)

            best = lax.fori_loop(0, 2, step, tuple(best))
        for p, value in zip(places, best):
            if p is not None:
                rows[p] = value
    for p, value in enumerate(rows):
        row_ref[p : p + 1, :] = value


def score(name, arrays, jobs, n_rows, row_of, n_keys, key_of):
    dots = 0
    size = lambda k: HALF * (2 if arrays[k].ndim == 3 else 1)
    for _, keys, queries in jobs:
        dots += 2 * D * sum(size(k) for k in keys) * sum(size(q) for q in queries)
    return pl.pallas_call(
        functools.partial(score_kernel, jobs, row_of, key_of, len(arrays)),
        in_specs=[VMEM] * len(arrays),
        out_specs=[VMEM, VMEM],
        out_shape=[
            jax.ShapeDtypeStruct((max(n_rows, 1), HALF), jnp.float32),
            jax.ShapeDtypeStruct((max(n_keys, 1), 1, HALF), jnp.float32),
        ],
        name=name,
        compiler_params=pltpu.CompilerParams(vmem_limit_bytes=32 * 2**20),
        cost_estimate=pl.CostEstimate(
            flops=dots, bytes_accessed=sum(2 * a.size for a in arrays), transcendentals=0
        ),
    )(*arrays)


def pick_count(sizes, which):
    return jnp.sum(jnp.where(jnp.arange(sizes.shape[0]) == which, sizes, 0))


def on_device(embeddings, sizes, ranks):
    rows = embeddings.shape[1]
    clusters = lax.axis_size("group")
    group_index = lax.axis_index("group")
    helper_index = lax.axis_index("helper")
    count = pick_count(sizes, group_index)
    left = count - helper_index * rows
    own = packed(embeddings[0], ranks, left[None])

    ownx = send(own, core=1)
    b03 = send(own, row=1)
    b10 = send(own, col=1)
    nxt = send(own, cluster=-1)
    b01a = send(own[0], row=-1)
    b01b = send(own[1], row=-1)
    prva = send(b01a, cluster=1)
    b13a = send(b03[0], col=1)
    b13b = send(b10[1], row=1)
    prvb = send(b01b, cluster=1)
    b01ax = send(b01a, core=1)
    b01bx = send(b01b, core=1)
    nxtx = send(nxt, core=1)
    prvax = send(prva, core=1)
    prvbx = send(prvb, core=1)

    row_self, _ = score("self", [own, ownx], [("self", [0, 1], [0])], 2, lambda j, i: i, 0, lambda j: None)
    row_own, key_own = score(
        "own", [own, ownx, b01a, b01b, b10], [("pair", [0, 1], [2, 3, 4])], 4, lambda j, i: i, 4, lambda j: 0
    )
    row_nxt, _ = score(
        "next", [nxt, nxtx, own, b01a, b01b, b03, b10], [("next", [0, 1], [2, 3, 4, 5, 6])],
        8, lambda j, i: i, 0, lambda j: None,
    )
    row_one, key_one = score(
        "one", [b01a, b01b, b01ax, b01bx, b03], [("pair", [0, 1, 2, 3], [4])], 2, lambda j, i: i, 4, lambda j: 0
    )
    _, key_prv = score(
        "prev", [prva, prvax, b03, b10], [("prev", [0, 1], [2, 3])], 0, lambda j, i: None, 2, lambda j: 0
    )
    row_last, key_last = score(
        "last",
        [own, ownx, b01a, b01b, b01ax, b01bx, nxt, nxtx, prva, prvax, b13a, b13b],
        [
            ("pair", [0, 1], [10, 11]),
            ("pair", [2, 3, 4, 5], [10, 11]),
            ("next", [6, 7], [10, 11]),
            ("prev", [8, 9], [10, 11]),
        ],
        4, lambda j, i: (i, i, 2 + i, None)[j], 10, lambda j: (0, 4, None, 8)[j],
    )
    _, key_end = score(
        "end", [prvb, prvbx, b03, b10, b13a, b13b], [("prev", [0, 1], [2, 3, 4, 5])],
        0, lambda j, i: None, 2, lambda j: 0,
    )

    key_own, key_one, key_prv = key_own[:, 0], key_one[:, 0], key_prv[:, 0]
    key_last, key_end = key_last[:, 0], key_end[:, 0]
    key_own = jnp.maximum(key_own, key_last[:4])
    key_one = jnp.maximum(key_one, key_last[4:8])
    key_prv = jnp.maximum(key_prv, key_last[8:10])

    back_01 = send(jnp.concatenate([row_own[:2], row_nxt[2:4]]), row=1)
    back_03 = send(jnp.concatenate([row_one, row_nxt[4:6]]), row=-1)
    back_10 = send(jnp.concatenate([row_own[2:4], row_nxt[6:8]]), col=1)
    back_13 = send(row_last, col=1, row=-1)
    back_own = send(key_own[2:], core=1)
    back_one = send(key_one[:2], row=1)
    back_onex = send(key_one[2:], row=1, core=1)
    back_prv = send(jnp.concatenate([key_prv[:1], key_end[:1]]), cluster=-1, row=1)
    back_prvx = send(jnp.concatenate([key_prv[1:], key_end[1:]]), cluster=-1, row=1, core=1)

    def largest(*values):
        return functools.reduce(jnp.maximum, values).reshape(1, rows)

    within = largest(
        row_self, key_own[:2], back_own, back_01[:2], back_03[:2], back_10[:2], back_13[:2], back_one, back_onex
    )
    adjacent = largest(row_nxt[:2], back_01[2:], back_03[2:], back_10[2:], back_13[2:], back_prv, back_prvx)
    next_count = pick_count(sizes, (group_index + 1) % clusters)
    adjacent = jnp.where(next_count < rows * lax.axis_size("helper"), jnp.maximum(adjacent, -1.0), adjacent)
    real = (jnp.arange(rows, dtype=jnp.int32) < left)[None, :]
    within = jnp.where(real, jnp.maximum(within, -1.0), 0.0)
    return (within, jnp.where(real, adjacent, 0.0))


def solution(mesh):
    in_specs = (P("group", "helper", None), P(), P("group", "helper"))
    out_specs = (P("group", "helper"), P("group", "helper"))
    return jax.shard_map(
        on_device, mesh=mesh, in_specs=in_specs, out_specs=out_specs, check_vma=False
    )
```

```python
import functools
import math

import jax
import jax.numpy as jnp
from jax import lax
from jax.experimental import pallas as pl
from jax.experimental.pallas import tpu as pltpu
from jax.sharding import PartitionSpec as P

D = 1024
HALF = 256
EXTRA = 8
PAY = HALF + EXTRA
BASE = 64
FAR = 8192.0
LOW = -4.0
AXES = ("group", "helper")
VMEM = pl.BlockSpec(memory_space=pltpu.VMEM)
SMEM = pl.BlockSpec(memory_space=pltpu.SMEM)


def place(index):
    group, helper = divmod(index, 16)
    return {
        "part": group // 4,
        "z": group % 4,
        "row": helper // 4,
        "col": (helper // 2) % 2,
        "core": helper % 2,
    }


def number(at):
    return (at["part"] * 4 + at["z"]) * 16 + at["row"] * 4 + at["col"] * 2 + at["core"]


def pairs(col=0, row=0, core=0, cluster=0):
    out = []
    for source in range(128):
        at = place(source)
        step = at["part"] * 4 + at["z"] + cluster
        flip = 1 if step // 4 != at["part"] else 0
        at["part"], at["z"] = (step // 4) % 2, step % 4
        at["col"] = (at["col"] + col + flip) % 2
        at["row"] = (at["row"] + row) % 4
        at["core"] = (at["core"] + core) % 2
        out.append((source, number(at)))
    return out


def send(name, value, **shift):
    with jax.named_scope(name):
        return lax.ppermute(value, AXES, pairs(**shift))


def after(value, *others):
    return lax.optimization_barrier((value, *others))[0]


def inner(keys, queries):
    return lax.dot_general(
        keys, queries, (((1,), (1,)), ((), ())), preferred_element_type=jnp.float32
    )


PARTS = 4


def own_count(sizes_ref, step=0):
    return sizes_ref[lax.rem(lax.axis_index("group") + step, lax.axis_size("group"))]


def pack_kernel(sizes_ref, rows_hbm, rank_ref, pay_ref, a_ref, b_ref, rows_ref, sem):
    part = 2 * HALF // PARTS
    copies = [
        pltpu.make_async_copy(rows_hbm.at[pl.ds(i * part, part)], rows_ref.at[pl.ds(i * part, part)], sem.at[i])
        for i in range(PARTS)
    ]
    for copy in copies:
        copy.start()
    left = own_count(sizes_ref) - lax.axis_index("helper") * 2 * HALF
    for half, half_ref in enumerate((a_ref, b_ref)):
        rank = rank_ref[:, half * HALF : (half + 1) * HALF]
        position = lax.broadcasted_iota(jnp.int32, (1, HALF), 1) + half * HALF
        real = position < left
        high = jnp.where(real, rank // BASE, int(FAR) // BASE).astype(jnp.float32)
        low = jnp.where(real, rank % BASE, 0).astype(jnp.float32)
        both = jnp.concatenate([high, low, jnp.zeros((1, D - 2 * HALF), jnp.float32)], axis=1)
        tail = jnp.broadcast_to(both, (EXTRA, D)).astype(jnp.bfloat16)
        pay_ref[half, HALF:, :] = tail
        half_ref[HALF:, :] = tail
    for i, copy in enumerate(copies):
        copy.wait()
        half, at = divmod(i * part, HALF)
        rows = rows_ref[i * part : (i + 1) * part, :]
        scale = lax.rsqrt(jnp.mean(rows * rows, axis=-1, keepdims=True) + 1e-06) / math.sqrt(D)
        unit = (rows * scale).astype(jnp.bfloat16)
        pay_ref[half, at : at + part, :] = unit
        (a_ref, b_ref)[half][at : at + part, :] = unit


def packed(rows, ranks, sizes):
    half = jax.ShapeDtypeStruct((PAY, D), jnp.bfloat16)
    return pl.pallas_call(
        pack_kernel,
        in_specs=[SMEM, pl.BlockSpec(memory_space=pltpu.HBM), VMEM],
        out_specs=[VMEM] * 3,
        out_shape=[jax.ShapeDtypeStruct((2, PAY, D), jnp.bfloat16), half, half],
        scratch_shapes=[pltpu.VMEM((2 * HALF, D), jnp.float32), pltpu.SemaphoreType.DMA((PARTS,))],
        name="pack",
        compiler_params=pltpu.CompilerParams(vmem_limit_bytes=16 * 2**20),
        cost_estimate=pl.CostEstimate(flops=4 * 512 * D, bytes_accessed=4 * 2**20, transcendentals=512),
    )(sizes, rows, ranks)


def rank_row(tail):
    tail = tail[0:1, :].astype(jnp.float32)
    return tail[:, :HALF] * BASE + tail[:, HALF:]


def rank_column(tail):
    return jnp.transpose(jnp.broadcast_to(rank_row(tail), (128, HALF)))


def split(ref):
    return [ref.at[0], ref.at[1]]


def tops(scores):
    return jnp.max(scores.reshape(HALF // 8, 8, 128), axis=0)


def pieces(scores):
    return [scores[:, c : c + 128] for c in range(0, HALF, 128)]


def keep(row_ref, places, best):
    for at, value in zip(places, best):
        value = jnp.max(value, axis=0, keepdims=True)
        row_ref[at : at + 1, :] = jnp.maximum(row_ref[at : at + 1, :], value)


def lowest(queries):
    return [jnp.full((8, HALF), LOW, jnp.float32) for _ in queries]


def pair_job(row_ref, ranks, keys, queries, q_at, k_at):
    q_rank = [rank_row(query[HALF:, : 2 * HALF]) for query in queries]
    best, sides = lowest(queries), []
    for n, key_ref in enumerate(keys):
        key, k_rank, side = key_ref[:HALF, :], ranks[n][...], None
        for i, query in enumerate(queries):
            parts = []
            for c, piece in enumerate(pieces(inner(key, query[:HALF, :]))):
                earlier = k_rank < q_rank[i][:, c * 128 : c * 128 + 128]
                parts.append(tops(jnp.where(earlier, piece, LOW)))
                if k_at is not None:
                    other = jnp.where(earlier, LOW, piece)
                    side = other if side is None else jnp.maximum(side, other)
            best[i] = jnp.maximum(best[i], jnp.concatenate(parts, axis=1))
        sides.append(side)
    keep(row_ref, q_at, best)
    if k_at is not None:
        keep(row_ref, k_at, [jnp.transpose(side) for side in sides])


def real_job(row_ref, limits, keys, queries, q_at):
    best = lowest(queries)
    for n, key_ref in enumerate(keys):
        key = key_ref[:HALF, :]
        real = lax.broadcasted_iota(jnp.int32, (HALF, 128), 0) < limits[n]
        for i, query in enumerate(queries):
            parts = [tops(jnp.where(real, piece, LOW)) for piece in pieces(inner(key, query[:HALF, :]))]
            best[i] = jnp.maximum(best[i], jnp.concatenate(parts, axis=1))
    keep(row_ref, q_at, best)


def put_ranks(rank_ref, halves):
    for n, half in enumerate(halves):
        rank_ref[n] = rank_column(half[HALF:, : 2 * HALF])


def rank_shape(halves):
    return jax.ShapeDtypeStruct((halves, HALF, 128), jnp.float32)


def kernel_call(name, body, tasks, rows, sizes, arrays, extra_out=()):
    n = len(arrays)

    def kernel(*refs):
        sizes_ref, rows_in, ins = refs[0], refs[1], refs[2 : 2 + n]
        row_ref, extra = refs[2 + n], refs[3 + n :]
        row_ref[...] = rows_in[...]
        body(row_ref, sizes_ref, *ins, *extra)

    out = pl.pallas_call(
        kernel,
        in_specs=[SMEM, VMEM] + [VMEM] * n,
        out_specs=[VMEM] * (1 + len(extra_out)),
        out_shape=[jax.ShapeDtypeStruct((N_ROWS, HALF), jnp.float32), *extra_out],
        name=name,
        compiler_params=pltpu.CompilerParams(vmem_limit_bytes=14 * 2**20),
        cost_estimate=pl.CostEstimate(flops=int(tasks * 1024), bytes_accessed=1024, transcendentals=0),
    )(sizes, rows, *arrays)
    return out if extra_out else out[0]


W00, A00, KOWN, W03, A03, W10, A10 = 0, 2, 4, 6, 8, 10, 12
W13, A13, W01, A01, K01, PRV, KOWNX, K01X, PRVX = 14, 16, 18, 20, 22, 24, 26, 28, 30
N_ROWS = 32


def both(at):
    return [at, at + 1]


def real_rows(sizes_ref, col, row, other=0, cluster=0):
    helper = lax.axis_index("helper")
    flip = jnp.where(lax.axis_index("group") % 4 == 3, cluster, 0)
    row = (helper // 4 + row) % 4
    col = (helper // 2 + col + flip) % 2
    start = own_count(sizes_ref, cluster) - (row * 4 + col * 2 + (helper + other) % 2) * 2 * HALF
    return [start, start - HALF]


def self_kernel(row_ref, sizes_ref, own, ownx, ranks):
    keys = split(own) + split(ownx)
    put_ranks(ranks, keys)
    row_ref[...] = jnp.full(row_ref.shape, LOW, jnp.float32)
    pair_job(row_ref, [ranks.at[n] for n in range(4)], keys, split(own), both(W00), None)


def own_job(row_ref, own, ownx, ranks, queries, places):
    keys = split(own) + split(ownx)
    pair_job(row_ref, [ranks.at[n] for n in range(4)], keys, queries, places, both(KOWN) + both(KOWNX))


def first_kernel(row_ref, sizes_ref, own, ownx, ranks, b01a):
    own_job(row_ref, own, ownx, ranks, [b01a], [W01])


def bundle_kernel(b01a, b01b, nxt, prva, bundle):
    for n, half in enumerate([nxt.at[0], nxt.at[1], b01a, b01b, prva]):
        bundle[n] = half[...]


def middle_job(row_ref, sizes_ref, own, b01a, b01b, b03, b10, nxt, one, prv, ranks, core):
    queries = [*split(own), b01a, b01b, *split(b03), *split(b10)]
    real_job(
        row_ref, real_rows(sizes_ref, 0, 0, core, 1), nxt, queries, both(A00) + both(A01) + both(A03) + both(A10)
    )
    put_ranks(ranks, one)
    pair_job(row_ref, [ranks.at[0], ranks.at[1]], one, split(b03), both(W03), both((K01, K01X)[core]))
    limits = real_rows(sizes_ref, 0, -1) + real_rows(sizes_ref, 1, 0)
    real_job(row_ref, limits, split(b03) + split(b10), [prv], [(PRV, PRVX)[core]])


def same_kernel(row_ref, sizes_ref, own, ownx, own_ranks, b01a, b01b, b03, b10, nxt, prva, ranks):
    own_job(row_ref, own, ownx, own_ranks, [b01b, *split(b10)], [W01 + 1, W10, W10 + 1])
    middle_job(row_ref, sizes_ref, own, b01a, b01b, b03, b10, split(nxt), [b01a, b01b], prva, ranks, 0)


def cross_kernel(row_ref, sizes_ref, own, b01a, b01b, b03, b10, cross, ranks):
    nxt, one = [cross.at[0], cross.at[1]], [cross.at[2], cross.at[3]]
    middle_job(row_ref, sizes_ref, own, b01a, b01b, b03, b10, nxt, one, cross.at[4], ranks, 1)


def last_kernel(row_ref, sizes_ref, own, ownx, ranks, b01a, b01b, ranks1, ranks1x, nxt, prva, cross, b13a, b13b):
    b13 = [b13a, b13b]
    own_job(row_ref, own, ownx, ranks, b13, both(W13))
    one_ranks = [ranks1.at[0], ranks1.at[1], ranks1x.at[0], ranks1x.at[1]]
    keys = [b01a, b01b, cross.at[2], cross.at[3]]
    pair_job(row_ref, one_ranks, keys, b13, both(W13), both(K01) + both(K01X))
    limits = real_rows(sizes_ref, 0, 0, 0, 1) + real_rows(sizes_ref, 0, 0, 1, 1)
    real_job(row_ref, limits, [*split(nxt), cross.at[0], cross.at[1]], b13, both(A13))
    real_job(row_ref, real_rows(sizes_ref, 1, -1), b13, [prva, cross.at[4]], [PRV, PRVX])


def end_kernel(row_ref, sizes_ref, b03, b10, b13a, b13b, prvb, prvbx):
    limits = real_rows(sizes_ref, 1, -1) + real_rows(sizes_ref, 0, -1) + real_rows(sizes_ref, 1, 0)
    real_job(row_ref, limits, [b13a, b13b, *split(b03), *split(b10)], [prvb, prvbx], [PRV + 1, PRVX + 1])


def gather_kernel(rows_ref, swapped_ref, side_ref, own_ref, to03_ref, to01_ref, prv_ref):
    own_ref[...] = rows_ref[W00 : W00 + 6, :]
    own_ref[KOWN : KOWN + 2, :] = jnp.maximum(rows_ref[KOWN : KOWN + 2, :], swapped_ref[0:2, :])
    to03_ref[...] = jnp.maximum(rows_ref[W03 : W03 + 4, :], side_ref[4:8, :])
    to01_ref[...] = rows_ref[W01 : W01 + 6, :]
    to01_ref[4:6, :] = jnp.maximum(rows_ref[K01 : K01 + 2, :], swapped_ref[2:4, :])
    prv_ref[...] = jnp.maximum(rows_ref[PRV : PRV + 2, :], swapped_ref[4:6, :])


def final_kernel(sizes_ref, own, side, b03, b01, bprv, within_ref, adjacent_ref):
    left = own_count(sizes_ref) - lax.axis_index("helper") * 2 * HALF
    next_full = own_count(sizes_ref, 1) >= 2 * HALF * lax.axis_size("helper")
    for h in range(2):
        row = lambda ref, at: ref[at + h : at + h + 1, :]
        within = [row(own, W00), row(own, KOWN), row(side, 0), row(b03, 0), row(b01, 0), row(b01, 4)]
        adjacent = [row(own, A00), row(side, 2), row(b03, 2), row(b01, 2), row(bprv, 0)]
        within = functools.reduce(jnp.maximum, within)
        adjacent = functools.reduce(jnp.maximum, adjacent)
        adjacent = jnp.maximum(adjacent, jnp.where(next_full, LOW, -1.0))
        real = lax.broadcasted_iota(jnp.int32, (1, HALF), 1) + h * HALF < left
        within_ref[:, h * HALF : (h + 1) * HALF] = jnp.where(real, jnp.maximum(within, -1.0), 0.0)
        adjacent_ref[:, h * HALF : (h + 1) * HALF] = jnp.where(real, adjacent, 0.0)


def small_call(name, body, shapes, smem, arrays):
    return pl.pallas_call(
        body,
        in_specs=[SMEM] * smem + [VMEM] * (len(arrays) - smem),
        out_specs=[VMEM] * len(shapes),
        out_shape=[jax.ShapeDtypeStruct(shape, jnp.float32) for shape in shapes],
        name=name,
        compiler_params=pltpu.CompilerParams(vmem_limit_bytes=2 * 2**20),
    )(*arrays)


def on_device(embeddings, sizes, ranks):
    rows = embeddings.shape[1]
    own, own_a, own_b = packed(embeddings[0], ranks, sizes)

    b01a = send("b01a", own_a, row=-1)
    b10 = send("b10", own, col=1)
    b03 = send("b03", own, row=1)
    nxt = send("nxt", own, cluster=-1)
    ownx = send("ownx", own, core=1)
    b01b = send("b01b", after(own_b, ownx), row=-1)
    empty = jnp.zeros((N_ROWS, HALF), jnp.float32)
    state, own_ranks = kernel_call("self", self_kernel, 1, empty, sizes, [own, ownx], [rank_shape(4)])
    prva = send("prva", after(b01a, state), cluster=1)
    state = kernel_call("first", first_kernel, 0.5, state, sizes, [own, ownx, own_ranks, b01a])

    b03, b10, nxt, b01b, prva, state = lax.optimization_barrier((b03, b10, nxt, b01b, prva, state))
    b13a = send("b13a", b03[0], col=1)
    b13b = send("b13b", b10[1], row=1)
    prvb = send("prvb", b01b, cluster=1)
    bundle = pl.pallas_call(
        bundle_kernel,
        in_specs=[VMEM] * 4,
        out_specs=VMEM,
        out_shape=jax.ShapeDtypeStruct((5, PAY, D), jnp.bfloat16),
        name="bundle",
        compiler_params=pltpu.CompilerParams(vmem_limit_bytes=8 * 2**20),
    )(b01a, b01b, nxt, prva)
    cross = send("cross", bundle, core=1)
    state, ranks1 = kernel_call(
        "same", same_kernel, 4.5, state, sizes,
        [own, ownx, own_ranks, b01a, b01b, b03, b10, nxt, prva], [rank_shape(2)],
    )
    state, ranks1x = kernel_call(
        "cross", cross_kernel, 3, state, sizes, [own, b01a, b01b, b03, b10, cross], [rank_shape(2)]
    )
    prvbx = send("prvbx", after(prvb, state), core=1)
    state = kernel_call(
        "last", last_kernel, 3.5, state, sizes,
        [own, ownx, own_ranks, b01a, b01b, ranks1, ranks1x, nxt, prva, cross, b13a, b13b],
    )
    state = kernel_call("end", end_kernel, 1.5, state, sizes, [b03, b10, b13a, b13b, prvb, prvbx])

    swapped = send("swapped", state[KOWNX : KOWNX + 6], core=1)
    side = send("side", state[W10 : W10 + 8], col=1)
    shapes = [(6, HALF), (4, HALF), (6, HALF), (2, HALF)]
    kept, to_03, to_01, to_prv = small_call("gather", gather_kernel, shapes, 0, [state, swapped, side])
    back_03 = send("back_03", to_03, row=-1)
    back_01 = send("back_01", to_01, row=1)
    back_prv = send("back_prv", to_prv, cluster=-1, row=1)
    return tuple(
        small_call("final", final_kernel, [(1, rows)] * 2, 1, [sizes, kept, side, back_03, back_01, back_prv])
    )


def solution(mesh):
    in_specs = (P("group", "helper", None), P(), P("group", "helper"))
    out_specs = (P("group", "helper"), P("group", "helper"))
    return jax.shard_map(
        on_device, mesh=mesh, in_specs=in_specs, out_specs=out_specs, check_vma=False
    )
```

```python
import functools
import math

import jax
import jax.numpy as jnp
from jax import lax
from jax.experimental import pallas as pl
from jax.experimental.pallas import tpu as pltpu
from jax.sharding import PartitionSpec as P

D = 1024
HALF = 256
EXTRA = 8
PAY = HALF + EXTRA
BASE = 64
FAR = 8192.0
LOW = -4.0
AXES = ("group", "helper")
VMEM = pl.BlockSpec(memory_space=pltpu.VMEM)
SMEM = pl.BlockSpec(memory_space=pltpu.SMEM)


def place(index):
    group, helper = divmod(index, 16)
    return {
        "part": group // 4,
        "z": group % 4,
        "row": helper // 4,
        "col": (helper // 2) % 2,
        "core": helper % 2,
    }


def number(at):
    return (at["part"] * 4 + at["z"]) * 16 + at["row"] * 4 + at["col"] * 2 + at["core"]


def pairs(col=0, row=0, core=0, cluster=0):
    out = []
    for source in range(128):
        at = place(source)
        step = at["part"] * 4 + at["z"] + cluster
        flip = 1 if step // 4 != at["part"] else 0
        at["part"], at["z"] = (step // 4) % 2, step % 4
        at["col"] = (at["col"] + col + flip) % 2
        at["row"] = (at["row"] + row) % 4
        at["core"] = (at["core"] + core) % 2
        out.append((source, number(at)))
    return out


def send(name, value, **shift):
    with jax.named_scope(name):
        return lax.ppermute(value, AXES, pairs(**shift))


def after(value, *others):
    return lax.optimization_barrier((value, *others))[0]


def inner(keys, queries):
    return lax.dot_general(
        keys, queries, (((1,), (1,)), ((), ())), preferred_element_type=jnp.float32
    )


PARTS = 4
PACK_MIB = 60
LONG = 10**8


def own_count(sizes_ref, step=0):
    return sizes_ref[lax.rem(lax.axis_index("group") + step, lax.axis_size("group"))]


def pack_kernel(sizes_hbm, rows_hbm, rank_hbm, pay_ref, a_ref, b_ref, rows_ref, rank_ref, sizes_ref, sem):
    part = 2 * HALF // PARTS
    copies = [
        pltpu.make_async_copy(rows_hbm.at[pl.ds(i * part, part)], rows_ref.at[pl.ds(i * part, part)], sem.at[i])
        for i in range(PARTS)
    ]
    rank_copy = pltpu.make_async_copy(rank_hbm, rank_ref, sem.at[PARTS])
    sizes_copy = pltpu.make_async_copy(sizes_hbm, sizes_ref, sem.at[PARTS + 1])
    for copy in [*copies, rank_copy, sizes_copy]:
        copy.start()
    for i, copy in enumerate(copies):
        copy.wait()
        half, at = divmod(i * part, HALF)
        rows = rows_ref[i * part : (i + 1) * part, :]
        scale = lax.rsqrt(jnp.mean(rows * rows, axis=-1, keepdims=True) + 1e-06) / math.sqrt(D)
        unit = (rows * scale).astype(jnp.bfloat16)
        pay_ref[half, at : at + part, :] = unit
        (a_ref, b_ref)[half][at : at + part, :] = unit
    rank_copy.wait()
    sizes_copy.wait()
    left = own_count(sizes_ref) - lax.axis_index("helper") * 2 * HALF
    for half, half_ref in enumerate((a_ref, b_ref)):
        rank = rank_ref[:, half * HALF : (half + 1) * HALF]
        position = lax.broadcasted_iota(jnp.int32, (1, HALF), 1) + half * HALF
        real = position < left
        high = jnp.where(real, rank // BASE, int(FAR) // BASE).astype(jnp.float32)
        low = jnp.where(real, rank % BASE, 0).astype(jnp.float32)
        both = jnp.concatenate([high, low, jnp.zeros((1, D - 2 * HALF), jnp.float32)], axis=1)
        tail = jnp.broadcast_to(both, (EXTRA, D)).astype(jnp.bfloat16)
        pay_ref[half, HALF:, :] = tail
        half_ref[HALF:, :] = tail


def packed(rows, ranks, sizes):
    half = jax.ShapeDtypeStruct((PAY, D), jnp.bfloat16)
    return pl.pallas_call(
        pack_kernel,
        in_specs=[pl.BlockSpec(memory_space=pltpu.HBM)] * 3,
        out_specs=[VMEM] * 3,
        out_shape=[jax.ShapeDtypeStruct((2, PAY, D), jnp.bfloat16), half, half],
        scratch_shapes=[
            pltpu.VMEM((2 * HALF, D), jnp.float32),
            pltpu.VMEM((1, 2 * HALF), jnp.int32),
            pltpu.SMEM(sizes.shape, jnp.int32),
            pltpu.SemaphoreType.DMA((PARTS + 2,)),
        ],
        name="pack",
        compiler_params=pltpu.CompilerParams(vmem_limit_bytes=PACK_MIB * 2**20),
        cost_estimate=pl.CostEstimate(flops=4 * 512 * D, bytes_accessed=4 * 2**20, transcendentals=512),
    )(sizes, rows, ranks)


def rank_row(tail):
    tail = tail[0:1, :].astype(jnp.float32)
    return tail[:, :HALF] * BASE + tail[:, HALF:]


def rank_column(tail):
    return jnp.transpose(jnp.broadcast_to(rank_row(tail), (128, HALF)))


def split(ref):
    return [ref.at[0], ref.at[1]]


def tops(scores):
    return jnp.max(scores.reshape(HALF // 8, 8, 128), axis=0)


def pieces(scores):
    return [scores[:, c : c + 128] for c in range(0, HALF, 128)]


def keep(row_ref, places, best):
    for at, value in zip(places, best):
        value = jnp.max(value, axis=0, keepdims=True)
        row_ref[at : at + 1, :] = jnp.maximum(row_ref[at : at + 1, :], value)


def lowest(queries):
    return [jnp.full((8, HALF), LOW, jnp.float32) for _ in queries]


ALL = lambda k, q: True
SHARE = {(0, 0), (1, 0), (1, 1), (2, 0), (2, 1), (3, 1)}


def pair_job(row_ref, ranks, keys, queries, q_at, k_at, wanted=ALL):
    q_rank = [rank_row(query[HALF:, : 2 * HALF]) for query in queries]
    best, sides = lowest(queries), []
    for n, key_ref in enumerate(keys):
        key, k_rank, side = key_ref[:HALF, :], ranks[n][...], None
        for i, query in enumerate(queries):
            if not wanted(n, i):
                continue
            parts = []
            for c, piece in enumerate(pieces(inner(key, query[:HALF, :]))):
                earlier = k_rank < q_rank[i][:, c * 128 : c * 128 + 128]
                parts.append(tops(jnp.where(earlier, piece, LOW)))
                if k_at is not None:
                    other = jnp.where(earlier, LOW, piece)
                    side = other if side is None else jnp.maximum(side, other)
            best[i] = jnp.maximum(best[i], jnp.concatenate(parts, axis=1))
        sides.append(side)
    keep(row_ref, q_at, best)
    if k_at is not None:
        keep(row_ref, k_at, [jnp.transpose(side) for side in sides])


def real_job(row_ref, limits, keys, queries, q_at):
    best = lowest(queries)
    for n, key_ref in enumerate(keys):
        key = key_ref[:HALF, :]
        real = lax.broadcasted_iota(jnp.int32, (HALF, 128), 0) < limits[n]
        for i, query in enumerate(queries):
            parts = [tops(jnp.where(real, piece, LOW)) for piece in pieces(inner(key, query[:HALF, :]))]
            best[i] = jnp.maximum(best[i], jnp.concatenate(parts, axis=1))
    keep(row_ref, q_at, best)


def put_ranks(rank_ref, halves):
    for n, half in enumerate(halves):
        rank_ref[n] = rank_column(half[HALF:, : 2 * HALF])


def rank_shape(halves):
    return jax.ShapeDtypeStruct((halves, HALF, 128), jnp.float32)


def kernel_call(name, body, tasks, rows, sizes, arrays, extra_out=()):
    n = len(arrays)

    def kernel(*refs):
        sizes_ref, rows_in, ins = refs[0], refs[1], refs[2 : 2 + n]
        row_ref, extra = refs[2 + n], refs[3 + n :]
        row_ref[...] = rows_in[...]
        body(row_ref, sizes_ref, *ins, *extra)

    out = pl.pallas_call(
        kernel,
        in_specs=[SMEM, VMEM] + [VMEM] * n,
        out_specs=[VMEM] * (1 + len(extra_out)),
        out_shape=[jax.ShapeDtypeStruct((N_ROWS, HALF), jnp.float32), *extra_out],
        name=name,
        compiler_params=pltpu.CompilerParams(vmem_limit_bytes=14 * 2**20),
        cost_estimate=pl.CostEstimate(flops=int(tasks * 1024), bytes_accessed=1024, transcendentals=0),
    )(sizes, rows, *arrays)
    return out if extra_out else out[0]


W00, A00, KOWN, W03, A03, W10, A10 = 0, 2, 4, 6, 8, 10, 12
W13, A13, W01, A01, K01, PRV, KOWNX, K01X, PRVX = 14, 16, 18, 20, 22, 24, 26, 28, 30
N_ROWS = 40


def both(at):
    return [at, at + 1]


def real_rows(sizes_ref, col, row, other=0, cluster=0):
    helper = lax.axis_index("helper")
    flip = jnp.where(lax.axis_index("group") % 4 == 3, cluster, 0)
    row = (helper // 4 + row) % 4
    col = (helper // 2 + col + flip) % 2
    start = own_count(sizes_ref, cluster) - (row * 4 + col * 2 + (helper + other) % 2) * 2 * HALF
    return [start, start - HALF]


def self_kernel(row_ref, sizes_ref, own, ownx, ranks):
    keys = split(own) + split(ownx)
    put_ranks(ranks, keys)
    row_ref[...] = jnp.full(row_ref.shape, LOW, jnp.float32)
    pair_job(row_ref, [ranks.at[n] for n in range(4)], keys, split(own), both(W00), None)


def own_job(row_ref, own, ownx, ranks, queries, places, wanted=ALL):
    keys = split(own) + split(ownx)
    pair_job(row_ref, [ranks.at[n] for n in range(4)], keys, queries, places, both(KOWN) + both(KOWNX), wanted)


def first_kernel(row_ref, sizes_ref, own, ownx, ranks, b01a):
    own_job(row_ref, own, ownx, ranks, [b01a], [W01])


def bundle_kernel(b01a, b01b, nxt, prva, bundle):
    for n, half in enumerate([nxt.at[0], nxt.at[1], b01a, b01b, prva]):
        bundle[n] = half[...]


def same_kernel(row_ref, sizes_ref, own, ownx, own_ranks, b01a, b01b, b03, b10, nxt, prva, ranks):
    places = [W01 + 1, W10, W10 + 1]
    own_job(row_ref, own, ownx, own_ranks, [b01b, *split(b10)], places, lambda k, q: q == 0 or (k, q - 1) in SHARE)
    queries = [*split(own), b01a, b01b, *split(b03), *split(b10)]
    places = both(A00) + both(A01) + both(A03) + both(A10)
    real_job(row_ref, real_rows(sizes_ref, 0, 0, 0, 1), split(nxt), queries, places)
    put_ranks(ranks, [b01a, b01b])
    pair_job(
        row_ref, [ranks.at[0], ranks.at[1]], [b01a, b01b], split(b03), both(W03), both(K01),
        lambda k, q: (k, q) in SHARE,
    )
    limits = real_rows(sizes_ref, 0, -1) + real_rows(sizes_ref, 1, 0)
    real_job(row_ref, limits, split(b03) + split(b10), [prva], [PRV])


def last_kernel(row_ref, sizes_ref, own, ownx, ranks, b01a, b01b, ranks1, nxt, prva, b13a, b13b):
    b13 = [b13a, b13b]
    own_job(row_ref, own, ownx, ranks, b13, both(W13))
    pair_job(
        row_ref, [ranks1.at[0], ranks1.at[1]], [b01a, b01b], b13, both(W13), both(K01), lambda k, q: (k, q) in SHARE
    )
    real_job(row_ref, real_rows(sizes_ref, 0, 0, 0, 1), split(nxt), b13, both(A13))
    real_job(row_ref, real_rows(sizes_ref, 1, -1), b13, [prva], [PRV])


def cross_kernel(row_ref, sizes_ref, own, b01a, b01b, b03, b10, b13a, b13b, cross):
    b13 = [b13a, b13b]
    queries = [*split(own), b01a, b01b, *split(b03), *split(b10), *b13]
    places = both(A00) + both(A01) + both(A03) + both(A10) + both(A13)
    real_job(row_ref, real_rows(sizes_ref, 0, 0, 1, 1), [cross.at[0], cross.at[1]], queries, places)
    one = [cross.at[2], cross.at[3]]
    ranks = [rank_column(half[HALF:, : 2 * HALF]) for half in one]
    queries = split(b03) + b13
    pair_job(
        row_ref, ranks, one, queries, both(W03) + both(W13), both(K01X), lambda k, q: (2 + k, q % 2) in SHARE
    )
    limits = real_rows(sizes_ref, 0, -1) + real_rows(sizes_ref, 1, 0) + real_rows(sizes_ref, 1, -1)
    real_job(row_ref, limits, split(b03) + split(b10) + b13, [cross.at[4]], [PRVX])


def end_kernel(row_ref, sizes_ref, b03, b10, b13a, b13b, prvb, prvbx):
    limits = real_rows(sizes_ref, 1, -1) + real_rows(sizes_ref, 0, -1) + real_rows(sizes_ref, 1, 0)
    real_job(row_ref, limits, [b13a, b13b, *split(b03), *split(b10)], [prvb, prvbx], [PRV + 1, PRVX + 1])


def gather_kernel(sizes_ref, rows_ref, swapped_ref, side_ref, kept_ref, to03_ref, to01_ref):
    left = own_count(sizes_ref) - lax.axis_index("helper") * 2 * HALF
    floor = jnp.where(own_count(sizes_ref, 1) >= 2 * HALF * lax.axis_size("helper"), LOW, -1.0)
    for h in range(2):
        row = lambda ref, at: ref[at + h : at + h + 1, :]
        real = lax.broadcasted_iota(jnp.int32, (1, HALF), 1) + h * HALF < left
        within = jnp.maximum(row(rows_ref, W00), row(rows_ref, KOWN))
        within = jnp.maximum(jnp.maximum(within, row(swapped_ref, 0)), jnp.maximum(row(side_ref, 0), -1.0))
        adjacent = jnp.maximum(jnp.maximum(row(rows_ref, A00), row(side_ref, 2)), floor)
        kept_ref[h : h + 1, :] = within
        kept_ref[2 + h : 3 + h, :] = adjacent
        kept_ref[4 + h : 5 + h, :] = jnp.where(real, 1.0, 0.0)
    kept_ref[6:8, :] = jnp.zeros((2, HALF), jnp.float32)
    to03_ref[...] = jnp.maximum(rows_ref[W03 : W03 + 4, :], side_ref[4:8, :])
    to01_ref[...] = rows_ref[W01 : W01 + 6, :]
    to01_ref[4:6, :] = jnp.maximum(rows_ref[K01 : K01 + 2, :], swapped_ref[2:4, :])


def final_kernel(kept, b03, b01, bprv, bprvx, within_ref, adjacent_ref):
    for h in range(2):
        row = lambda ref, at: ref[at + h : at + h + 1, :]
        within = [row(kept, 0), row(b03, 0), row(b01, 0), row(b01, 4)]
        adjacent = [row(kept, 2), row(b03, 2), row(b01, 2), row(bprv, 0), row(bprvx, 0)]
        real = row(kept, 4) > 0
        place = slice(h * HALF, (h + 1) * HALF)
        within_ref[:, place] = jnp.where(real, functools.reduce(jnp.maximum, within), 0.0)
        adjacent_ref[:, place] = jnp.where(real, functools.reduce(jnp.maximum, adjacent), 0.0)


def small_call(name, body, shapes, smem, arrays):
    return pl.pallas_call(
        body,
        in_specs=[SMEM] * smem + [VMEM] * (len(arrays) - smem),
        out_specs=[VMEM] * len(shapes),
        out_shape=[jax.ShapeDtypeStruct(shape, jnp.float32) for shape in shapes],
        name=name,
        compiler_params=pltpu.CompilerParams(vmem_limit_bytes=2 * 2**20),
    )(*arrays)


def on_device(embeddings, sizes, ranks):
    rows = embeddings.shape[1]
    own, own_a, own_b = packed(embeddings[0], ranks, sizes)

    b01a = send("b01a", own_a, row=-1)
    b03 = send("b03", own, row=1)
    nxt = send("nxt", own, cluster=-1)
    b10 = send("b10", own, col=1)
    ownx = send("ownx", own, core=1)
    b01b = send("b01b", after(own_b, ownx), row=-1)
    empty = jnp.zeros((N_ROWS, HALF), jnp.float32)
    state, own_ranks = kernel_call("self", self_kernel, 1, empty, sizes, [own, ownx], [rank_shape(4)])
    prva = send("prva", after(b01a, state), cluster=1)
    state = kernel_call("first", first_kernel, 0.5, state, sizes, [own, ownx, own_ranks, b01a])

    b03, b10, state = lax.optimization_barrier((b03, b10, state))
    nxt, b01b, prva, state = lax.optimization_barrier((nxt, b01b, prva, state))
    b13a = send("b13a", b03[0], col=1)
    b13b = send("b13b", b10[1], row=1)
    prvb = send("prvb", b01b, cluster=1)
    bundle = pl.pallas_call(
        bundle_kernel,
        in_specs=[VMEM] * 4,
        out_specs=VMEM,
        out_shape=jax.ShapeDtypeStruct((5, PAY, D), jnp.bfloat16),
        name="bundle",
        compiler_params=pltpu.CompilerParams(vmem_limit_bytes=8 * 2**20),
    )(b01a, b01b, nxt, prva)
    cross = send("cross", bundle, core=1)
    state, ranks1 = kernel_call(
        "same", same_kernel, 4.5, state, sizes,
        [own, ownx, own_ranks, b01a, b01b, b03, b10, nxt, prva], [rank_shape(2)],
    )
    state = kernel_call(
        "last", last_kernel, LONG, state, sizes,
        [own, ownx, own_ranks, b01a, b01b, ranks1, nxt, prva, b13a, b13b],
    )
    prvbx = send("prvbx", after(prvb, state), core=1)
    state = kernel_call(
        "cross", cross_kernel, 4, state, sizes, [own, b01a, b01b, b03, b10, b13a, b13b, cross]
    )

    swapped = send("swapped", state[KOWNX : KOWNX + 4], core=1)
    side = send("side", state[W10 : W10 + 8], col=1)
    state = kernel_call("end", end_kernel, 1.5, state, sizes, [b03, b10, b13a, b13b, prvb, prvbx])
    shapes = [(8, HALF), (4, HALF), (6, HALF)]
    kept, to_03, to_01 = small_call("gather", gather_kernel, shapes, 1, [sizes, state, swapped, side])
    back_03 = send("back_03", to_03, row=-1)
    back_01 = send("back_01", to_01, row=1)
    back_prv = send("back_prv", state[PRV : PRV + 8], cluster=-1, row=1)
    back_prvx = send("back_prvx", state[PRVX : PRVX + 8], cluster=-1, row=1, core=1)
    arrays = [kept, back_03, back_01, back_prv, back_prvx]
    return tuple(small_call("final", final_kernel, [(1, rows)] * 2, 0, arrays))


def solution(mesh):
    in_specs = (P("group", "helper", None), P(), P("group", "helper"))
    out_specs = (P("group", "helper"), P("group", "helper"))
    return jax.shard_map(
        on_device, mesh=mesh, in_specs=in_specs, out_specs=out_specs, check_vma=False
    )
```

```python
import functools
import math

import jax
import jax.numpy as jnp
from jax import lax
from jax.experimental import pallas as pl
from jax.experimental.pallas import tpu as pltpu
from jax.sharding import PartitionSpec as P

D = 1024
HALF = 256
EXTRA = 8
PAY = HALF + EXTRA
BASE = 64
FAR = 8192.0
LOW = -4.0
AXES = ("group", "helper")
VMEM = pl.BlockSpec(memory_space=pltpu.VMEM)
SMEM = pl.BlockSpec(memory_space=pltpu.SMEM)


def place(index):
    group, helper = divmod(index, 16)
    return {
        "part": group // 4,
        "z": group % 4,
        "row": helper // 4,
        "col": (helper // 2) % 2,
        "core": helper % 2,
    }


def number(at):
    return (at["part"] * 4 + at["z"]) * 16 + at["row"] * 4 + at["col"] * 2 + at["core"]


def pairs(col=0, row=0, core=0, cluster=0):
    out = []
    for source in range(128):
        at = place(source)
        step = at["part"] * 4 + at["z"] + cluster
        flip = 1 if step // 4 != at["part"] else 0
        at["part"], at["z"] = (step // 4) % 2, step % 4
        at["col"] = (at["col"] + col + flip) % 2
        at["row"] = (at["row"] + row) % 4
        at["core"] = (at["core"] + core) % 2
        out.append((source, number(at)))
    return out


def send(name, value, **shift):
    with jax.named_scope(name):
        return lax.ppermute(value, AXES, pairs(**shift))


def after(value, *others):
    return lax.optimization_barrier((value, *others))[0]


def inner(keys, queries):
    return lax.dot_general(
        keys, queries, (((1,), (1,)), ((), ())), preferred_element_type=jnp.float32
    )


PARTS = 4
PACK_MIB = 60
LONG = 10**8


def own_count(sizes_ref, step=0):
    return sizes_ref[lax.rem(lax.axis_index("group") + step, lax.axis_size("group"))]


def pack_kernel(sizes_hbm, rows_hbm, rank_hbm, pay_ref, a_ref, b_ref, rows_ref, rank_ref, sizes_ref, sem):
    part = 2 * HALF // PARTS
    copies = [
        pltpu.make_async_copy(rows_hbm.at[pl.ds(i * part, part)], rows_ref.at[pl.ds(i * part, part)], sem.at[i])
        for i in range(PARTS)
    ]
    rank_copy = pltpu.make_async_copy(rank_hbm, rank_ref, sem.at[PARTS])
    sizes_copy = pltpu.make_async_copy(sizes_hbm, sizes_ref, sem.at[PARTS + 1])
    for copy in [*copies, rank_copy, sizes_copy]:
        copy.start()
    for i, copy in enumerate(copies):
        copy.wait()
        half, at = divmod(i * part, HALF)
        rows = rows_ref[i * part : (i + 1) * part, :]
        scale = lax.rsqrt(jnp.mean(rows * rows, axis=-1, keepdims=True) + 1e-06) / math.sqrt(D)
        unit = (rows * scale).astype(jnp.bfloat16)
        pay_ref[half, at : at + part, :] = unit
        (a_ref, b_ref)[half][at : at + part, :] = unit
    rank_copy.wait()
    sizes_copy.wait()
    left = own_count(sizes_ref) - lax.axis_index("helper") * 2 * HALF
    for half, half_ref in enumerate((a_ref, b_ref)):
        rank = rank_ref[:, half * HALF : (half + 1) * HALF]
        position = lax.broadcasted_iota(jnp.int32, (1, HALF), 1) + half * HALF
        real = position < left
        high = jnp.where(real, rank // BASE, int(FAR) // BASE).astype(jnp.float32)
        low = jnp.where(real, rank % BASE, 0).astype(jnp.float32)
        both = jnp.concatenate([high, low, jnp.zeros((1, D - 2 * HALF), jnp.float32)], axis=1)
        tail = jnp.broadcast_to(both, (EXTRA, D)).astype(jnp.bfloat16)
        pay_ref[half, HALF:, :] = tail
        half_ref[HALF:, :] = tail


def packed(rows, ranks, sizes):
    half = jax.ShapeDtypeStruct((PAY, D), jnp.bfloat16)
    return pl.pallas_call(
        pack_kernel,
        in_specs=[pl.BlockSpec(memory_space=pltpu.HBM)] * 3,
        out_specs=[VMEM] * 3,
        out_shape=[jax.ShapeDtypeStruct((2, PAY, D), jnp.bfloat16), half, half],
        scratch_shapes=[
            pltpu.VMEM((2 * HALF, D), jnp.float32),
            pltpu.VMEM((1, 2 * HALF), jnp.int32),
            pltpu.SMEM(sizes.shape, jnp.int32),
            pltpu.SemaphoreType.DMA((PARTS + 2,)),
        ],
        name="pack",
        compiler_params=pltpu.CompilerParams(vmem_limit_bytes=PACK_MIB * 2**20),
        cost_estimate=pl.CostEstimate(flops=4 * 512 * D, bytes_accessed=4 * 2**20, transcendentals=512),
    )(sizes, rows, ranks)


def rank_row(tail):
    tail = tail[0:1, :].astype(jnp.float32)
    return tail[:, :HALF] * BASE + tail[:, HALF:]


def rank_column(tail):
    return jnp.transpose(jnp.broadcast_to(rank_row(tail), (128, HALF)))


def split(ref):
    return [ref.at[0], ref.at[1]]


def tops(scores):
    return jnp.max(scores.reshape(HALF // 8, 8, 128), axis=0)


def pieces(scores):
    return [scores[:, c : c + 128] for c in range(0, HALF, 128)]


def keep(row_ref, places, best):
    for at, value in zip(places, best):
        value = jnp.max(value, axis=0, keepdims=True)
        row_ref[at : at + 1, :] = jnp.maximum(row_ref[at : at + 1, :], value)


def lowest(queries):
    return [jnp.full((8, HALF), LOW, jnp.float32) for _ in queries]


ALL = lambda k, q: True
SHARE = {(0, 0), (1, 0), (1, 1), (2, 0), (2, 1), (3, 1)}


def pair_job(row_ref, ranks, keys, queries, q_at, k_at, wanted=ALL):
    q_rank = [rank_row(query[HALF:, : 2 * HALF]) for query in queries]
    best, sides = lowest(queries), []
    for n, key_ref in enumerate(keys):
        key, k_rank, side = key_ref[:HALF, :], ranks[n][...], None
        for i, query in enumerate(queries):
            if not wanted(n, i):
                continue
            parts = []
            for c, piece in enumerate(pieces(inner(key, query[:HALF, :]))):
                earlier = k_rank < q_rank[i][:, c * 128 : c * 128 + 128]
                parts.append(tops(jnp.where(earlier, piece, LOW)))
                if k_at is not None:
                    other = jnp.where(earlier, LOW, piece)
                    side = other if side is None else jnp.maximum(side, other)
            best[i] = jnp.maximum(best[i], jnp.concatenate(parts, axis=1))
        sides.append(side)
    keep(row_ref, q_at, best)
    if k_at is not None:
        keep(row_ref, k_at, [jnp.transpose(side) for side in sides])


def real_job(row_ref, limits, keys, queries, q_at):
    best = lowest(queries)
    for n, key_ref in enumerate(keys):
        key = key_ref[:HALF, :]
        real = lax.broadcasted_iota(jnp.int32, (HALF, 128), 0) < limits[n]
        for i, query in enumerate(queries):
            parts = [tops(jnp.where(real, piece, LOW)) for piece in pieces(inner(key, query[:HALF, :]))]
            best[i] = jnp.maximum(best[i], jnp.concatenate(parts, axis=1))
    keep(row_ref, q_at, best)


def put_ranks(rank_ref, halves):
    for n, half in enumerate(halves):
        rank_ref[n] = rank_column(half[HALF:, : 2 * HALF])


def rank_shape(halves):
    return jax.ShapeDtypeStruct((halves, HALF, 128), jnp.float32)


def kernel_call(name, body, tasks, rows, sizes, arrays, extra_out=()):
    n = len(arrays)

    def kernel(*refs):
        sizes_ref, rows_in, ins = refs[0], refs[1], refs[2 : 2 + n]
        row_ref, extra = refs[2 + n], refs[3 + n :]
        row_ref[...] = rows_in[...]
        body(row_ref, sizes_ref, *ins, *extra)

    out = pl.pallas_call(
        kernel,
        in_specs=[SMEM, VMEM] + [VMEM] * n,
        out_specs=[VMEM] * (1 + len(extra_out)),
        out_shape=[jax.ShapeDtypeStruct((N_ROWS, HALF), jnp.float32), *extra_out],
        name=name,
        compiler_params=pltpu.CompilerParams(vmem_limit_bytes=14 * 2**20),
        cost_estimate=pl.CostEstimate(flops=int(tasks * 1024), bytes_accessed=1024, transcendentals=0),
    )(sizes, rows, *arrays)
    return out if extra_out else out[0]


W00, A00, KOWN, W03, A03, W10, A10 = 0, 2, 4, 6, 8, 10, 12
W13, A13, W01, A01, K01, PRV, KOWNX, K01X, PRVX = 14, 16, 18, 20, 22, 24, 26, 28, 30
REAL, FLOOR = 32, 34
N_ROWS = 40


def both(at):
    return [at, at + 1]


def real_rows(sizes_ref, col, row, other=0, cluster=0):
    helper = lax.axis_index("helper")
    flip = jnp.where(lax.axis_index("group") % 4 == 3, cluster, 0)
    row = (helper // 4 + row) % 4
    col = (helper // 2 + col + flip) % 2
    start = own_count(sizes_ref, cluster) - (row * 4 + col * 2 + (helper + other) % 2) * 2 * HALF
    return [start, start - HALF]


def self_kernel(row_ref, sizes_ref, own, ownx, ranks):
    keys = split(own) + split(ownx)
    put_ranks(ranks, keys)
    row_ref[...] = jnp.full(row_ref.shape, LOW, jnp.float32)
    left = own_count(sizes_ref) - lax.axis_index("helper") * 2 * HALF
    for h in range(2):
        position = lax.broadcasted_iota(jnp.int32, (1, HALF), 1) + h * HALF
        row_ref[REAL + h : REAL + h + 1, :] = jnp.where(position < left, 1.0, 0.0)
    floor = jnp.where(own_count(sizes_ref, 1) < 2 * HALF * lax.axis_size("helper"), -1.0, LOW)
    row_ref[FLOOR : FLOOR + 1, :] = jnp.full((1, HALF), floor, jnp.float32)
    pair_job(row_ref, [ranks.at[n] for n in range(4)], keys, split(own), both(W00), None)


def own_job(row_ref, own, ownx, ranks, queries, places, wanted=ALL):
    keys = split(own) + split(ownx)
    pair_job(row_ref, [ranks.at[n] for n in range(4)], keys, queries, places, both(KOWN) + both(KOWNX), wanted)


def first_kernel(row_ref, sizes_ref, own, ownx, ranks, b01a):
    own_job(row_ref, own, ownx, ranks, [b01a], [W01])


def bundle_kernel(b01a, b01b, nxt, prva, bundle):
    for n, half in enumerate([nxt.at[0], nxt.at[1], b01a, b01b, prva]):
        bundle[n] = half[...]


def same_kernel(row_ref, sizes_ref, own, ownx, own_ranks, b01a, b01b, b03, b10, nxt, prva, ranks):
    places = [W01 + 1, W10, W10 + 1]
    own_job(row_ref, own, ownx, own_ranks, [b01b, *split(b10)], places, lambda k, q: q == 0 or (k, q - 1) in SHARE)
    queries = [*split(own), b01a, b01b, *split(b03), *split(b10)]
    places = both(A00) + both(A01) + both(A03) + both(A10)
    real_job(row_ref, real_rows(sizes_ref, 0, 0, 0, 1), split(nxt), queries, places)
    put_ranks(ranks, [b01a, b01b])
    pair_job(
        row_ref, [ranks.at[0], ranks.at[1]], [b01a, b01b], split(b03), both(W03), both(K01),
        lambda k, q: (k, q) in SHARE,
    )
    limits = real_rows(sizes_ref, 0, -1) + real_rows(sizes_ref, 1, 0)
    real_job(row_ref, limits, split(b03) + split(b10), [prva], [PRV])


def last_kernel(row_ref, sizes_ref, own, ownx, ranks, b01a, b01b, ranks1, nxt, prva, b13a, b13b):
    b13 = [b13a, b13b]
    own_job(row_ref, own, ownx, ranks, b13, both(W13))
    pair_job(
        row_ref, [ranks1.at[0], ranks1.at[1]], [b01a, b01b], b13, both(W13), both(K01), lambda k, q: (k, q) in SHARE
    )
    real_job(row_ref, real_rows(sizes_ref, 0, 0, 0, 1), split(nxt), b13, both(A13))
    real_job(row_ref, real_rows(sizes_ref, 1, -1), b13, [prva], [PRV])


def cross_kernel(row_ref, sizes_ref, own, b01a, b01b, b03, b10, b13a, b13b, cross, prvbx):
    b13 = [b13a, b13b]
    queries = [*split(own), b01a, b01b, *split(b03), *split(b10), *b13]
    places = both(A00) + both(A01) + both(A03) + both(A10) + both(A13)
    real_job(row_ref, real_rows(sizes_ref, 0, 0, 1, 1), [cross.at[0], cross.at[1]], queries, places)
    one = [cross.at[2], cross.at[3]]
    ranks = [rank_column(half[HALF:, : 2 * HALF]) for half in one]
    queries = split(b03) + b13
    pair_job(
        row_ref, ranks, one, queries, both(W03) + both(W13), both(K01X), lambda k, q: (2 + k, q % 2) in SHARE
    )
    limits = real_rows(sizes_ref, 0, -1) + real_rows(sizes_ref, 1, 0) + real_rows(sizes_ref, 1, -1)
    real_job(row_ref, limits, split(b03) + split(b10) + b13, [cross.at[4], prvbx], both(PRVX))


def end_kernel(row_ref, sizes_ref, b03, b10, b13a, b13b, prvb):
    limits = real_rows(sizes_ref, 1, -1) + real_rows(sizes_ref, 0, -1) + real_rows(sizes_ref, 1, 0)
    real_job(row_ref, limits, [b13a, b13b, *split(b03), *split(b10)], [prvb], [PRV + 1])


def gather_kernel(rows_ref, swapped_ref, side_ref, kept_ref, to03_ref, to01_ref, prv_ref):
    within = jnp.maximum(rows_ref[W00 : W00 + 2, :], rows_ref[KOWN : KOWN + 2, :])
    within = jnp.maximum(within, jnp.maximum(swapped_ref[0:2, :], side_ref[0:2, :]))
    kept_ref[0:2, :] = jnp.maximum(within, -1.0)
    kept_ref[2:4, :] = jnp.maximum(jnp.maximum(rows_ref[A00 : A00 + 2, :], side_ref[2:4, :]), rows_ref[FLOOR : FLOOR + 1, :])
    kept_ref[4:6, :] = rows_ref[REAL : REAL + 2, :]
    kept_ref[6:8, :] = rows_ref[REAL : REAL + 2, :]
    to03_ref[...] = jnp.maximum(rows_ref[W03 : W03 + 4, :], side_ref[4:8, :])
    to01_ref[0:4, :] = rows_ref[W01 : W01 + 4, :]
    to01_ref[4:6, :] = jnp.maximum(rows_ref[K01 : K01 + 2, :], swapped_ref[2:4, :])
    prv_ref[0:2, :] = jnp.maximum(rows_ref[PRV : PRV + 2, :], swapped_ref[4:6, :])
    prv_ref[2:8, :] = rows_ref[0:6, :]


def final_kernel(kept, b03, b01, bprv, within_ref, adjacent_ref):
    for h in range(2):
        row = lambda ref, at: ref[at + h : at + h + 1, :]
        within = [row(kept, 0), row(b03, 0), row(b01, 0), row(b01, 4)]
        adjacent = [row(kept, 2), row(b03, 2), row(b01, 2), row(bprv, 0)]
        real = row(kept, 4) > 0
        place = slice(h * HALF, (h + 1) * HALF)
        within_ref[:, place] = jnp.where(real, functools.reduce(jnp.maximum, within), 0.0)
        adjacent_ref[:, place] = jnp.where(real, functools.reduce(jnp.maximum, adjacent), 0.0)


def small_call(name, body, shapes, arrays):
    return pl.pallas_call(
        body,
        in_specs=[VMEM] * len(arrays),
        out_specs=[VMEM] * len(shapes),
        out_shape=[jax.ShapeDtypeStruct(shape, jnp.float32) for shape in shapes],
        name=name,
        compiler_params=pltpu.CompilerParams(vmem_limit_bytes=2 * 2**20),
    )(*arrays)


def on_device(embeddings, sizes, ranks):
    rows = embeddings.shape[1]
    own, own_a, own_b = packed(embeddings[0], ranks, sizes)

    b01a = send("b01a", own_a, row=-1)
    b03 = send("b03", own, row=1)
    nxt = send("nxt", own, cluster=-1)
    b10 = send("b10", own, col=1)
    ownx = send("ownx", own, core=1)
    b01b = send("b01b", after(own_b, ownx), row=-1)
    empty = jnp.zeros((N_ROWS, HALF), jnp.float32)
    state, own_ranks = kernel_call("self", self_kernel, 1, empty, sizes, [own, ownx], [rank_shape(4)])
    prva = send("prva", after(b01a, state), cluster=1)
    state = kernel_call("first", first_kernel, 0.5, state, sizes, [own, ownx, own_ranks, b01a])

    prvb = send("prvb", after(b01b, state), cluster=1)
    b03, b10, state = lax.optimization_barrier((b03, b10, state))
    nxt, b01b, prva, state = lax.optimization_barrier((nxt, b01b, prva, state))
    b13a = send("b13a", b03[0], col=1)
    b13b = send("b13b", b10[1], row=1)
    bundle = pl.pallas_call(
        bundle_kernel,
        in_specs=[VMEM] * 4,
        out_specs=VMEM,
        out_shape=jax.ShapeDtypeStruct((5, PAY, D), jnp.bfloat16),
        name="bundle",
        compiler_params=pltpu.CompilerParams(vmem_limit_bytes=8 * 2**20),
    )(b01a, b01b, nxt, prva)
    cross = send("cross", bundle, core=1)
    state, ranks1 = kernel_call(
        "same", same_kernel, 4.5, state, sizes,
        [own, ownx, own_ranks, b01a, b01b, b03, b10, nxt, prva], [rank_shape(2)],
    )
    prvb, state = lax.optimization_barrier((prvb, state))
    state = kernel_call(
        "last", last_kernel, LONG, state, sizes,
        [own, ownx, own_ranks, b01a, b01b, ranks1, nxt, prva, b13a, b13b],
    )
    prvbx = send("prvbx", prvb, core=1)
    state = kernel_call(
        "cross", cross_kernel, 4, state, sizes, [own, b01a, b01b, b03, b10, b13a, b13b, cross, prvbx]
    )

    swapped = send("swapped", state[KOWNX : KOWNX + 6], core=1)
    side = send("side", state[W10 : W10 + 8], col=1)
    state = kernel_call("end", end_kernel, 1, state, sizes, [b03, b10, b13a, b13b, prvb])
    shapes = [(8, HALF), (4, HALF), (6, HALF), (8, HALF)]
    kept, to_03, to_01, to_prv = small_call("gather", gather_kernel, shapes, [state, swapped, side])
    back_prv = send("back_prv", to_prv, cluster=-1, row=1)
    back_01 = send("back_01", to_01, row=1)
    back_03 = send("back_03", to_03, row=-1)
    return tuple(small_call("final", final_kernel, [(1, rows)] * 2, [kept, back_03, back_01, back_prv]))


def solution(mesh):
    in_specs = (P("group", "helper", None), P(), P("group", "helper"))
    out_specs = (P("group", "helper"), P("group", "helper"))
    return jax.shard_map(
        on_device, mesh=mesh, in_specs=in_specs, out_specs=out_specs, check_vma=False
    )
```

```python
import functools
import math

import jax
import jax.numpy as jnp
from jax import lax
from jax.experimental import pallas as pl
from jax.experimental.pallas import tpu as pltpu
from jax.sharding import PartitionSpec as P

D = 1024
HALF = 256
EXTRA = 8
PAY = HALF + EXTRA
BASE = 64
FAR = 8192.0
LOW = -4.0
AXES = ("group", "helper")
VMEM = pl.BlockSpec(memory_space=pltpu.VMEM)
SMEM = pl.BlockSpec(memory_space=pltpu.SMEM)


def place(index):
    group, helper = divmod(index, 16)
    return {
        "part": group // 4,
        "z": group % 4,
        "row": helper // 4,
        "col": (helper // 2) % 2,
        "core": helper % 2,
    }


def number(at):
    return (at["part"] * 4 + at["z"]) * 16 + at["row"] * 4 + at["col"] * 2 + at["core"]


def pairs(col=0, row=0, core=0, cluster=0):
    out = []
    for source in range(128):
        at = place(source)
        step = at["part"] * 4 + at["z"] + cluster
        flip = 1 if step // 4 != at["part"] else 0
        at["part"], at["z"] = (step // 4) % 2, step % 4
        at["col"] = (at["col"] + col + flip) % 2
        at["row"] = (at["row"] + row) % 4
        at["core"] = (at["core"] + core) % 2
        out.append((source, number(at)))
    return out


def send(name, value, **shift):
    with jax.named_scope(name):
        return lax.ppermute(value, AXES, pairs(**shift))


def after(value, *others):
    return lax.optimization_barrier((value, *others))[0]


def inner(keys, queries):
    return lax.dot_general(
        keys, queries, (((1,), (1,)), ((), ())), preferred_element_type=jnp.float32
    )


PARTS = 4
PACK_MIB = 60
LONG = 10**8


def own_count(sizes_ref, step=0):
    return sizes_ref[lax.rem(lax.axis_index("group") + step, lax.axis_size("group"))]


def pack_kernel(sizes_hbm, rows_hbm, rank_hbm, pay_ref, a_ref, b_ref, rows_ref, rank_ref, sizes_ref, sem):
    part = 2 * HALF // PARTS
    copies = [
        pltpu.make_async_copy(rows_hbm.at[pl.ds(i * part, part)], rows_ref.at[pl.ds(i * part, part)], sem.at[i])
        for i in range(PARTS)
    ]
    rank_copy = pltpu.make_async_copy(rank_hbm, rank_ref, sem.at[PARTS])
    sizes_copy = pltpu.make_async_copy(sizes_hbm, sizes_ref, sem.at[PARTS + 1])
    for copy in [*copies, rank_copy, sizes_copy]:
        copy.start()
    for i, copy in enumerate(copies):
        copy.wait()
        half, at = divmod(i * part, HALF)
        rows = rows_ref[i * part : (i + 1) * part, :]
        scale = lax.rsqrt(jnp.mean(rows * rows, axis=-1, keepdims=True) + 1e-06) / math.sqrt(D)
        unit = (rows * scale).astype(jnp.bfloat16)
        pay_ref[half, at : at + part, :] = unit
        (a_ref, b_ref)[half][at : at + part, :] = unit
    rank_copy.wait()
    sizes_copy.wait()
    left = own_count(sizes_ref) - lax.axis_index("helper") * 2 * HALF
    for half, half_ref in enumerate((a_ref, b_ref)):
        rank = rank_ref[:, half * HALF : (half + 1) * HALF]
        position = lax.broadcasted_iota(jnp.int32, (1, HALF), 1) + half * HALF
        real = position < left
        high = jnp.where(real, rank // BASE, int(FAR) // BASE).astype(jnp.float32)
        low = jnp.where(real, rank % BASE, 0).astype(jnp.float32)
        both = jnp.concatenate([high, low, jnp.zeros((1, D - 2 * HALF), jnp.float32)], axis=1)
        tail = jnp.broadcast_to(both, (EXTRA, D)).astype(jnp.bfloat16)
        pay_ref[half, HALF:, :] = tail
        half_ref[HALF:, :] = tail


def packed(rows, ranks, sizes):
    half = jax.ShapeDtypeStruct((PAY, D), jnp.bfloat16)
    return pl.pallas_call(
        pack_kernel,
        in_specs=[pl.BlockSpec(memory_space=pltpu.HBM)] * 3,
        out_specs=[VMEM] * 3,
        out_shape=[jax.ShapeDtypeStruct((2, PAY, D), jnp.bfloat16), half, half],
        scratch_shapes=[
            pltpu.VMEM((2 * HALF, D), jnp.float32),
            pltpu.VMEM((1, 2 * HALF), jnp.int32),
            pltpu.SMEM(sizes.shape, jnp.int32),
            pltpu.SemaphoreType.DMA((PARTS + 2,)),
        ],
        name="pack",
        compiler_params=pltpu.CompilerParams(vmem_limit_bytes=PACK_MIB * 2**20),
        cost_estimate=pl.CostEstimate(flops=4 * 512 * D, bytes_accessed=4 * 2**20, transcendentals=512),
    )(sizes, rows, ranks)


def rank_row(tail):
    tail = tail[0:1, :].astype(jnp.float32)
    return tail[:, :HALF] * BASE + tail[:, HALF:]


def rank_column(tail):
    return jnp.transpose(jnp.broadcast_to(rank_row(tail), (128, HALF)))


def split(ref):
    return [ref.at[0], ref.at[1]]


def tops(scores):
    return jnp.max(scores.reshape(HALF // 8, 8, 128), axis=0)


def pieces(scores):
    return [scores[:, c : c + 128] for c in range(0, HALF, 128)]


def keep(row_ref, places, best):
    for at, value in zip(places, best):
        value = jnp.max(value, axis=0, keepdims=True)
        row_ref[at : at + 1, :] = jnp.maximum(row_ref[at : at + 1, :], value)


def lowest(queries):
    return [jnp.full((8, HALF), LOW, jnp.float32) for _ in queries]


ALL = lambda k, q: True
SHARE = {(0, 0), (1, 0), (1, 1), (2, 0), (2, 1), (3, 1)}


def pair_job(row_ref, ranks, keys, queries, q_at, k_at, wanted=ALL):
    q_rank = [rank_row(query[HALF:, : 2 * HALF]) for query in queries]
    best, sides = lowest(queries), []
    for n, key_ref in enumerate(keys):
        key, k_rank, side = key_ref[:HALF, :], ranks[n][...], None
        for i, query in enumerate(queries):
            if not wanted(n, i):
                continue
            parts = []
            for c, piece in enumerate(pieces(inner(key, query[:HALF, :]))):
                earlier = k_rank < q_rank[i][:, c * 128 : c * 128 + 128]
                parts.append(tops(jnp.where(earlier, piece, LOW)))
                if k_at is not None:
                    other = jnp.where(earlier, LOW, piece)
                    side = other if side is None else jnp.maximum(side, other)
            best[i] = jnp.maximum(best[i], jnp.concatenate(parts, axis=1))
        if side is not None:
            sides.append((k_at[n], side))
    keep(row_ref, q_at, best)
    for at, side in sides:
        keep(row_ref, [at], [jnp.transpose(side)])


def real_job(row_ref, limits, keys, queries, q_at):
    best = lowest(queries)
    position = lax.broadcasted_iota(jnp.int32, (HALF, 128), 0).astype(jnp.float32)
    for n, key_ref in enumerate(keys):
        key = key_ref[:HALF, :]
        real = position < row_ref[limits[n] : limits[n] + 1, :128]
        for i, query in enumerate(queries):
            parts = [tops(jnp.where(real, piece, LOW)) for piece in pieces(inner(key, query[:HALF, :]))]
            best[i] = jnp.maximum(best[i], jnp.concatenate(parts, axis=1))
    keep(row_ref, q_at, best)


def put_ranks(rank_ref, halves):
    for n, half in enumerate(halves):
        rank_ref[n] = rank_column(half[HALF:, : 2 * HALF])


def rank_shape(halves):
    return jax.ShapeDtypeStruct((halves, HALF, 128), jnp.float32)


def kernel_call(name, body, tasks, rows, arrays, extra_out=(), scalars=()):
    n = len(arrays) + len(scalars)

    def kernel(rows_in, *refs):
        row_ref = refs[n]
        row_ref[...] = rows_in[...]
        body(row_ref, *refs[:n], *refs[n + 1 :])

    out = pl.pallas_call(
        kernel,
        in_specs=[VMEM] * (1 + len(arrays)) + [SMEM] * len(scalars),
        out_specs=[VMEM] * (1 + len(extra_out)),
        out_shape=[jax.ShapeDtypeStruct((N_ROWS, HALF), jnp.float32), *extra_out],
        name=name,
        compiler_params=pltpu.CompilerParams(vmem_limit_bytes=14 * 2**20),
        cost_estimate=pl.CostEstimate(flops=int(tasks * 1024), bytes_accessed=1024, transcendentals=0),
    )(rows, *arrays, *scalars)
    return out if extra_out else out[0]


W00, A00, KOWN, W03, A03, W10, A10 = 0, 2, 4, 6, 8, 10, 12
W13, A13, W01, A01, K01, PRV, KOWNX, K01X, PRVX = 14, 16, 18, 20, 22, 24, 26, 28, 30
REAL, FLOOR = 32, 34
L_NXT, L_NXTX, L_03, L_10, L_13 = 40, 42, 44, 46, 48
N_ROWS = 56


def both(at):
    return [at, at + 1]


def real_rows(sizes_ref, col, row, other=0, cluster=0):
    helper = lax.axis_index("helper")
    flip = jnp.where(lax.axis_index("group") % 4 == 3, cluster, 0)
    row = (helper // 4 + row) % 4
    col = (helper // 2 + col + flip) % 2
    start = own_count(sizes_ref, cluster) - (row * 4 + col * 2 + (helper + other) % 2) * 2 * HALF
    return [start, start - HALF]


def self_kernel(row_ref, own, ownx, sizes_ref, ranks):
    keys = split(own) + split(ownx)
    put_ranks(ranks, keys)
    row_ref[...] = jnp.full(row_ref.shape, LOW, jnp.float32)
    left = own_count(sizes_ref) - lax.axis_index("helper") * 2 * HALF
    for h in range(2):
        position = lax.broadcasted_iota(jnp.int32, (1, HALF), 1) + h * HALF
        row_ref[REAL + h : REAL + h + 1, :] = jnp.where(position < left, 1.0, 0.0)
    floor = jnp.where(own_count(sizes_ref, 1) < 2 * HALF * lax.axis_size("helper"), -1.0, LOW)
    row_ref[FLOOR : FLOOR + 1, :] = jnp.full((1, HALF), floor, jnp.float32)
    limits = [(L_NXT, real_rows(sizes_ref, 0, 0, 0, 1)), (L_NXTX, real_rows(sizes_ref, 0, 0, 1, 1))]
    limits += [(L_03, real_rows(sizes_ref, 0, -1)), (L_10, real_rows(sizes_ref, 1, 0)), (L_13, real_rows(sizes_ref, 1, -1))]
    for at, counts in limits:
        for h, count in enumerate(counts):
            row_ref[at + h : at + h + 1, :] = jnp.full((1, HALF), count, jnp.int32).astype(jnp.float32)
    pair_job(row_ref, [ranks.at[n] for n in range(4)], keys, split(own), both(W00), None)


def own_job(row_ref, own, ownx, ranks, queries, places, wanted=ALL):
    keys = split(own) + split(ownx)
    pair_job(row_ref, [ranks.at[n] for n in range(4)], keys, queries, places, both(KOWN) + both(KOWNX), wanted)


def first_kernel(row_ref, own, ownx, ranks, b01a):
    own_job(row_ref, own, ownx, ranks, [b01a], [W01])


def bundle_kernel(b01a, b01b, nxt, prva, bundle):
    for n, half in enumerate([nxt.at[0], nxt.at[1], b01a, b01b, prva]):
        bundle[n] = half[...]


def same_kernel(row_ref, own, ownx, own_ranks, b01a, b01b, b03, b10, nxt, prva, ranks):
    places = [W01 + 1, W10, W10 + 1]
    own_job(row_ref, own, ownx, own_ranks, [b01b, *split(b10)], places, lambda k, q: q == 0 or (k, q - 1) in SHARE)
    queries = [*split(own), b01a, b01b, *split(b03), *split(b10)]
    places = both(A00) + both(A01) + both(A03) + both(A10)
    real_job(row_ref, both(L_NXT), split(nxt), queries, places)
    put_ranks(ranks, [b01a, b01b])
    pair_job(
        row_ref, [ranks.at[0], ranks.at[1]], [b01a, b01b], split(b03), both(W03), both(K01),
        lambda k, q: (k, q) in SHARE,
    )
    limits = both(L_03) + both(L_10)
    real_job(row_ref, limits, split(b03) + split(b10), [prva], [PRV])


def half_kernel(h, row_ref, own, ownx, ranks, b01a, b01b, ranks1, nxt, prva, b13):
    own_job(row_ref, own, ownx, ranks, [b13], [W13 + h])
    pair_job(
        row_ref, [ranks1.at[0], ranks1.at[1]], [b01a, b01b], [b13], [W13 + h], both(K01), lambda k, q: (k, h) in SHARE
    )
    real_job(row_ref, both(L_NXT), split(nxt), [b13], [A13 + h])
    real_job(row_ref, [L_13 + h], [b13], [prva], [PRV])


def cross_kernel(row_ref, b03, b10, b13a, b13b, cross, prvbx):
    b13 = [b13a, b13b]
    real_job(row_ref, both(L_NXTX), [cross.at[0], cross.at[1]], split(b10) + b13, both(A10) + both(A13))
    one = [cross.at[2], cross.at[3]]
    ranks = [rank_column(half[HALF:, : 2 * HALF]) for half in one]
    pair_job(
        row_ref, ranks, one, split(b03) + b13, both(W03) + both(W13), both(K01X),
        lambda k, q: (2 + k, q % 2) in SHARE,
    )
    limits = both(L_03) + both(L_10) + both(L_13)
    real_job(row_ref, limits, split(b03) + split(b10) + b13, [cross.at[4], prvbx], both(PRVX))


def end_kernel(row_ref, own, b01a, b01b, b03, b10, b13a, b13b, cross, prvb):
    queries = [*split(own), b01a, b01b, *split(b03)]
    real_job(row_ref, both(L_NXTX), [cross.at[0], cross.at[1]], queries, both(A00) + both(A01) + both(A03))
    limits = both(L_13) + both(L_03) + both(L_10)
    real_job(row_ref, limits, [b13a, b13b, *split(b03), *split(b10)], [prvb], [PRV + 1])


def gather_kernel(rows_ref, swapped_ref, side_ref, kept_ref, to03_ref, to01_ref, prv_ref):
    within = jnp.maximum(rows_ref[W00 : W00 + 2, :], rows_ref[KOWN : KOWN + 2, :])
    within = jnp.maximum(within, jnp.maximum(swapped_ref[0:2, :], side_ref[0:2, :]))
    kept_ref[0:2, :] = jnp.maximum(within, -1.0)
    kept_ref[2:4, :] = jnp.maximum(jnp.maximum(rows_ref[A00 : A00 + 2, :], side_ref[2:4, :]), rows_ref[FLOOR : FLOOR + 1, :])
    kept_ref[4:6, :] = rows_ref[REAL : REAL + 2, :]
    kept_ref[6:8, :] = rows_ref[REAL : REAL + 2, :]
    to03_ref[...] = jnp.maximum(rows_ref[W03 : W03 + 4, :], side_ref[4:8, :])
    to01_ref[0:4, :] = rows_ref[W01 : W01 + 4, :]
    to01_ref[4:6, :] = jnp.maximum(rows_ref[K01 : K01 + 2, :], swapped_ref[2:4, :])
    prv_ref[0:2, :] = jnp.maximum(rows_ref[PRV : PRV + 2, :], swapped_ref[4:6, :])
    prv_ref[2:8, :] = rows_ref[0:6, :]


def final_kernel(kept, b03, b01, bprv, within_ref, adjacent_ref):
    for h in range(2):
        row = lambda ref, at: ref[at + h : at + h + 1, :]
        within = [row(kept, 0), row(b03, 0), row(b01, 0), row(b01, 4)]
        adjacent = [row(kept, 2), row(b03, 2), row(b01, 2), row(bprv, 0)]
        real = row(kept, 4) > 0
        place = slice(h * HALF, (h + 1) * HALF)
        within_ref[:, place] = jnp.where(real, functools.reduce(jnp.maximum, within), 0.0)
        adjacent_ref[:, place] = jnp.where(real, functools.reduce(jnp.maximum, adjacent), 0.0)


def small_call(name, body, shapes, arrays):
    return pl.pallas_call(
        body,
        in_specs=[VMEM] * len(arrays),
        out_specs=[VMEM] * len(shapes),
        out_shape=[jax.ShapeDtypeStruct(shape, jnp.float32) for shape in shapes],
        name=name,
        compiler_params=pltpu.CompilerParams(vmem_limit_bytes=2 * 2**20),
    )(*arrays)


def on_device(embeddings, sizes, ranks):
    rows = embeddings.shape[1]
    own, own_a, own_b = packed(embeddings[0], ranks, sizes)

    b01a = send("b01a", own_a, row=-1)
    b03 = send("b03", own, row=1)
    nxt = send("nxt", own, cluster=-1)
    b10 = send("b10", own, col=1)
    ownx = send("ownx", own, core=1)
    b01b = send("b01b", after(own_b, ownx), row=-1)
    empty = jnp.zeros((N_ROWS, HALF), jnp.float32)
    state, own_ranks = kernel_call("self", self_kernel, 1, empty, [own, ownx], [rank_shape(4)], [sizes])
    prva = send("prva", after(b01a, state), cluster=1)
    state = kernel_call("first", first_kernel, 0.5, state, [own, ownx, own_ranks, b01a])

    prvb = send("prvb", after(b01b, state), cluster=1)
    b03, b10, state = lax.optimization_barrier((b03, b10, state))
    nxt, b01b, prva, state = lax.optimization_barrier((nxt, b01b, prva, state))
    b13a = send("b13a", b03[0], col=1)
    b13b = send("b13b", b10[1], row=1)
    bundle = pl.pallas_call(
        bundle_kernel,
        in_specs=[VMEM] * 4,
        out_specs=VMEM,
        out_shape=jax.ShapeDtypeStruct((5, PAY, D), jnp.bfloat16),
        name="bundle",
        compiler_params=pltpu.CompilerParams(vmem_limit_bytes=8 * 2**20),
    )(b01a, b01b, nxt, prva)
    cross = send("cross", bundle, core=1)
    state, ranks1 = kernel_call(
        "same", same_kernel, 4.5, state,
        [own, ownx, own_ranks, b01a, b01b, b03, b10, nxt, prva], [rank_shape(2)],
    )
    kept = [own, ownx, own_ranks, b01a, b01b, ranks1, nxt, prva]
    state = kernel_call("left", functools.partial(half_kernel, 0), 1, state, [*kept, b13a])
    prvb, state = lax.optimization_barrier((prvb, state))
    state = kernel_call("right", functools.partial(half_kernel, 1), LONG, state, [*kept, b13b])
    prvbx = send("prvbx", prvb, core=1)
    state = kernel_call(
        "cross", cross_kernel, 4, state, [b03, b10, b13a, b13b, cross, prvbx]
    )

    swapped = send("swapped", state[KOWNX : KOWNX + 6], core=1)
    side = send("side", state[W10 : W10 + 8], col=1)
    state = kernel_call("end", end_kernel, 1, state, [own, b01a, b01b, b03, b10, b13a, b13b, cross, prvb])
    shapes = [(8, HALF), (4, HALF), (6, HALF), (8, HALF)]
    kept, to_03, to_01, to_prv = small_call("gather", gather_kernel, shapes, [state, swapped, side])
    back_prv = send("back_prv", to_prv, cluster=-1, row=1)
    back_01 = send("back_01", to_01, row=1)
    back_03 = send("back_03", to_03, row=-1)
    return tuple(small_call("final", final_kernel, [(1, rows)] * 2, [kept, back_03, back_01, back_prv]))


def solution(mesh):
    in_specs = (P("group", "helper", None), P(), P("group", "helper"))
    out_specs = (P("group", "helper"), P("group", "helper"))
    return jax.shard_map(
        on_device, mesh=mesh, in_specs=in_specs, out_specs=out_specs, check_vma=False
    )
```

```python
import functools
import math

import jax
import jax.numpy as jnp
from jax import lax
from jax.experimental import pallas as pl
from jax.experimental.pallas import tpu as pltpu
from jax.sharding import PartitionSpec as P

D = 1024
HALF = 256
EXTRA = 8
PAY = HALF + EXTRA
BASE = 64
FAR = 8192.0
LOW = -4.0
AXES = ("group", "helper")
VMEM = pl.BlockSpec(memory_space=pltpu.VMEM)
SMEM = pl.BlockSpec(memory_space=pltpu.SMEM)


def place(index):
    group, helper = divmod(index, 16)
    return {
        "part": group // 4,
        "z": group % 4,
        "row": helper // 4,
        "col": (helper // 2) % 2,
        "core": helper % 2,
    }


def number(at):
    return (at["part"] * 4 + at["z"]) * 16 + at["row"] * 4 + at["col"] * 2 + at["core"]


def pairs(col=0, row=0, core=0, cluster=0):
    out = []
    for source in range(128):
        at = place(source)
        step = at["part"] * 4 + at["z"] + cluster
        flip = 1 if step // 4 != at["part"] else 0
        at["part"], at["z"] = (step // 4) % 2, step % 4
        at["col"] = (at["col"] + col + flip) % 2
        at["row"] = (at["row"] + row) % 4
        at["core"] = (at["core"] + core) % 2
        out.append((source, number(at)))
    return out


def send(name, value, **shift):
    with jax.named_scope(name):
        return lax.ppermute(value, AXES, pairs(**shift))


def after(value, *others):
    return lax.optimization_barrier((value, *others))[0]


def inner(keys, queries):
    return lax.dot_general(
        keys, queries, (((1,), (1,)), ((), ())), preferred_element_type=jnp.float32
    )


PARTS = 4
PACK_MIB = 56
LONG = 10**8


def own_count(sizes_ref, step=0):
    return sizes_ref[lax.rem(lax.axis_index("group") + step, lax.axis_size("group"))]


def pack_kernel(sizes_hbm, rows_hbm, rank_hbm, pay_hbm, a_hbm, b_hbm, rows_ref, rank_ref, pay_ref, sizes_ref, sem, out_sem):
    part = 2 * HALF // PARTS
    copies = [
        pltpu.make_async_copy(rows_hbm.at[pl.ds(i * part, part)], rows_ref.at[pl.ds(i * part, part)], sem.at[i])
        for i in range(PARTS)
    ]
    rank_copy = pltpu.make_async_copy(rank_hbm, rank_ref, sem.at[PARTS])
    sizes_copy = pltpu.make_async_copy(sizes_hbm, sizes_ref, sem.at[PARTS + 1])
    for copy in [rank_copy, sizes_copy, *copies]:
        copy.start()
    rank_copy.wait()
    sizes_copy.wait()
    left = own_count(sizes_ref) - lax.axis_index("helper") * 2 * HALF
    outs = []
    for half, half_hbm in enumerate((a_hbm, b_hbm)):
        rank = rank_ref[:, half * HALF : (half + 1) * HALF]
        position = lax.broadcasted_iota(jnp.int32, (1, HALF), 1) + half * HALF
        real = position < left
        high = jnp.where(real, rank // BASE, int(FAR) // BASE).astype(jnp.float32)
        low = jnp.where(real, rank % BASE, 0).astype(jnp.float32)
        row = jnp.concatenate([high, low, jnp.zeros((1, D - 2 * HALF), jnp.float32)], axis=1)
        pay_ref[half, HALF:, :] = jnp.broadcast_to(row, (EXTRA, D)).astype(jnp.bfloat16)
        for i in range(half * PARTS // 2, (half + 1) * PARTS // 2):
            copies[i].wait()
            rows = rows_ref[i * part : (i + 1) * part, :]
            scale = lax.rsqrt(jnp.mean(rows * rows, axis=-1, keepdims=True) + 1e-06) / math.sqrt(D)
            at = i * part - half * HALF
            pay_ref[half, at : at + part, :] = (rows * scale).astype(jnp.bfloat16)
        outs.append(pltpu.make_async_copy(pay_ref.at[half], pay_hbm.at[half], out_sem.at[2 * half]))
        outs.append(pltpu.make_async_copy(pay_ref.at[half], half_hbm, out_sem.at[2 * half + 1]))
        for out in outs[2 * half :]:
            out.start()
    for out in outs:
        out.wait()


def packed(rows, ranks, sizes):
    half = jax.ShapeDtypeStruct((PAY, D), jnp.bfloat16)
    return pl.pallas_call(
        pack_kernel,
        in_specs=[pl.BlockSpec(memory_space=pltpu.HBM)] * 3,
        out_specs=[pl.BlockSpec(memory_space=pltpu.HBM)] * 3,
        out_shape=[jax.ShapeDtypeStruct((2, PAY, D), jnp.bfloat16), half, half],
        scratch_shapes=[
            pltpu.VMEM((2 * HALF, D), jnp.float32),
            pltpu.VMEM((1, 2 * HALF), jnp.int32),
            pltpu.VMEM((2, PAY, D), jnp.bfloat16),
            pltpu.SMEM(sizes.shape, jnp.int32),
            pltpu.SemaphoreType.DMA((PARTS + 2,)),
            pltpu.SemaphoreType.DMA((4,)),
        ],
        name="pack",
        compiler_params=pltpu.CompilerParams(vmem_limit_bytes=PACK_MIB * 2**20),
        cost_estimate=pl.CostEstimate(flops=4 * 512 * D, bytes_accessed=4 * 2**20, transcendentals=512),
    )(sizes, rows, ranks)


def rank_row(tail):
    tail = tail[0:1, :].astype(jnp.float32)
    return tail[:, :HALF] * BASE + tail[:, HALF:]


def rank_column(tail):
    return jnp.transpose(jnp.broadcast_to(rank_row(tail), (128, HALF)))


def split(ref):
    return [ref.at[0], ref.at[1]]


def tops(scores):
    return jnp.max(scores.reshape(HALF // 8, 8, 128), axis=0)


def pieces(scores):
    return [scores[:, c : c + 128] for c in range(0, HALF, 128)]


def keep(row_ref, places, best):
    for at, value in zip(places, best):
        value = jnp.max(value, axis=0, keepdims=True)
        row_ref[at : at + 1, :] = jnp.maximum(row_ref[at : at + 1, :], value)


def lowest(queries):
    return [jnp.full((8, HALF), LOW, jnp.float32) for _ in queries]


ALL = lambda k, q: True
SHARE = {(0, 0), (1, 0), (1, 1), (2, 0), (2, 1), (3, 1)}


def pair_job(row_ref, ranks, keys, queries, q_at, k_at, wanted=ALL):
    q_rank = [rank_row(query[HALF:, : 2 * HALF]) for query in queries]
    best, sides = lowest(queries), []
    for n, key_ref in enumerate(keys):
        key, k_rank, side = key_ref[:HALF, :], ranks[n][...], None
        for i, query in enumerate(queries):
            if not wanted(n, i):
                continue
            parts = []
            for c, piece in enumerate(pieces(inner(key, query[:HALF, :]))):
                earlier = k_rank < q_rank[i][:, c * 128 : c * 128 + 128]
                parts.append(tops(jnp.where(earlier, piece, LOW)))
                if k_at is not None:
                    other = jnp.where(earlier, LOW, piece)
                    side = other if side is None else jnp.maximum(side, other)
            best[i] = jnp.maximum(best[i], jnp.concatenate(parts, axis=1))
        if side is not None:
            sides.append((k_at[n], side))
    keep(row_ref, q_at, best)
    for at, side in sides:
        keep(row_ref, [at], [jnp.transpose(side)])


def real_job(row_ref, limits, keys, queries, q_at):
    best = lowest(queries)
    position = lax.broadcasted_iota(jnp.int32, (HALF, 128), 0).astype(jnp.float32)
    for n, key_ref in enumerate(keys):
        key = key_ref[:HALF, :]
        real = position < row_ref[limits[n] : limits[n] + 1, :128]
        for i, query in enumerate(queries):
            parts = [tops(jnp.where(real, piece, LOW)) for piece in pieces(inner(key, query[:HALF, :]))]
            best[i] = jnp.maximum(best[i], jnp.concatenate(parts, axis=1))
    keep(row_ref, q_at, best)


def put_ranks(rank_ref, halves):
    for n, half in enumerate(halves):
        rank_ref[n] = rank_column(half[HALF:, : 2 * HALF])


def rank_shape(halves):
    return jax.ShapeDtypeStruct((halves, HALF, 128), jnp.float32)


def kernel_call(name, body, tasks, rows, arrays, extra_out=(), scalars=()):
    n = len(arrays) + len(scalars)

    def kernel(rows_in, *refs):
        row_ref = refs[n]
        row_ref[...] = rows_in[...]
        body(row_ref, *refs[:n], *refs[n + 1 :])

    out = pl.pallas_call(
        kernel,
        in_specs=[VMEM] * (1 + len(arrays)) + [SMEM] * len(scalars),
        out_specs=[VMEM] * (1 + len(extra_out)),
        out_shape=[jax.ShapeDtypeStruct((N_ROWS, HALF), jnp.float32), *extra_out],
        name=name,
        compiler_params=pltpu.CompilerParams(vmem_limit_bytes=14 * 2**20),
        cost_estimate=pl.CostEstimate(flops=int(tasks * 1024) if tasks == LONG else 0, bytes_accessed=0, transcendentals=0),
    )(rows, *arrays, *scalars)
    return out if extra_out else out[0]


W00, A00, KOWN, W03, A03, W10, A10 = 0, 2, 4, 6, 8, 10, 12
W13, A13, W01, A01, K01, PRV, KOWNX, K01X, PRVX = 14, 16, 18, 20, 22, 24, 26, 28, 30
REAL, FLOOR = 32, 34
L_NXT, L_NXTX, L_03, L_10, L_13 = 40, 42, 44, 46, 48
N_ROWS = 56


def both(at):
    return [at, at + 1]


def real_rows(sizes_ref, col, row, other=0, cluster=0):
    helper = lax.axis_index("helper")
    flip = jnp.where(lax.axis_index("group") % 4 == 3, cluster, 0)
    row = (helper // 4 + row) % 4
    col = (helper // 2 + col + flip) % 2
    start = own_count(sizes_ref, cluster) - (row * 4 + col * 2 + (helper + other) % 2) * 2 * HALF
    return [start, start - HALF]


def self_kernel(row_ref, own, ownx, sizes_ref, ranks):
    keys = split(own) + split(ownx)
    put_ranks(ranks, keys)
    row_ref[...] = jnp.full(row_ref.shape, LOW, jnp.float32)
    left = own_count(sizes_ref) - lax.axis_index("helper") * 2 * HALF
    for h in range(2):
        position = lax.broadcasted_iota(jnp.int32, (1, HALF), 1) + h * HALF
        row_ref[REAL + h : REAL + h + 1, :] = jnp.where(position < left, 1.0, 0.0)
    floor = jnp.where(own_count(sizes_ref, 1) < 2 * HALF * lax.axis_size("helper"), -1.0, LOW)
    row_ref[FLOOR : FLOOR + 1, :] = jnp.full((1, HALF), floor, jnp.float32)
    limits = [(L_NXT, real_rows(sizes_ref, 0, 0, 0, 1)), (L_NXTX, real_rows(sizes_ref, 0, 0, 1, 1))]
    limits += [(L_03, real_rows(sizes_ref, 0, -1)), (L_10, real_rows(sizes_ref, 1, 0)), (L_13, real_rows(sizes_ref, 1, -1))]
    for at, counts in limits:
        for h, count in enumerate(counts):
            row_ref[at + h : at + h + 1, :] = jnp.full((1, HALF), count, jnp.int32).astype(jnp.float32)
    pair_job(row_ref, [ranks.at[n] for n in range(4)], keys, split(own), both(W00), None)


def own_job(row_ref, own, ownx, ranks, queries, places, wanted=ALL):
    keys = split(own) + split(ownx)
    pair_job(row_ref, [ranks.at[n] for n in range(4)], keys, queries, places, both(KOWN) + both(KOWNX), wanted)


def first_kernel(row_ref, own, ownx, ranks, b01a):
    own_job(row_ref, own, ownx, ranks, [b01a], [W01])


def bundle_kernel(b01a, b01b, nxt, prva, bundle, nxta, nxtb):
    nxta[...] = nxt[0, :HALF, :]
    nxtb[...] = nxt[1, :HALF, :]
    for n, half in enumerate([b01a, b01b, prva]):
        bundle[n] = half[...]


def same_kernel(row_ref, own, ownx, own_ranks, b01a, b01b, b03, b10, nxt, prva, ranks):
    places = [W01 + 1, W10, W10 + 1]
    own_job(row_ref, own, ownx, own_ranks, [b01b, *split(b10)], places, lambda k, q: q == 0 or (k, q - 1) in SHARE)
    queries = [*split(own), b01a, b01b, *split(b03), *split(b10)]
    places = both(A00) + both(A01) + both(A03) + both(A10)
    real_job(row_ref, both(L_NXT), split(nxt), queries, places)
    put_ranks(ranks, [b01a, b01b])
    pair_job(
        row_ref, [ranks.at[0], ranks.at[1]], [b01a, b01b], split(b03), both(W03), both(K01),
        lambda k, q: (k, q) in SHARE,
    )
    limits = both(L_03) + both(L_10)
    real_job(row_ref, limits, split(b03) + split(b10), [prva], [PRV])


def half_kernel(h, row_ref, own, ownx, ranks, b01a, b01b, ranks1, nxt, prva, b13):
    own_job(row_ref, own, ownx, ranks, [b13], [W13 + h])
    pair_job(
        row_ref, [ranks1.at[0], ranks1.at[1]], [b01a, b01b], [b13], [W13 + h], both(K01), lambda k, q: (k, h) in SHARE
    )
    real_job(row_ref, both(L_NXT), split(nxt), [b13], [A13 + h])
    real_job(row_ref, [L_13 + h], [b13], [prva], [PRV])


def other_kernel(row_ref, own, b01a, b01b, b03, b10, nxtax, nxtbx):
    queries = [*split(own), b01a, b01b, *split(b03), *split(b10)]
    places = both(A00) + both(A01) + both(A03) + both(A10)
    real_job(row_ref, both(L_NXTX), [nxtax, nxtbx], queries, places)


def cross_kernel(row_ref, b03, b10, b13a, b13b, nxtax, nxtbx, cross, prvbx):
    b13 = [b13a, b13b]
    real_job(row_ref, both(L_NXTX), [nxtax, nxtbx], b13, both(A13))
    one = [cross.at[0], cross.at[1]]
    ranks = [rank_column(half[HALF:, : 2 * HALF]) for half in one]
    pair_job(
        row_ref, ranks, one, split(b03) + b13, both(W03) + both(W13), both(K01X),
        lambda k, q: (2 + k, q % 2) in SHARE,
    )
    limits = both(L_03) + both(L_10) + both(L_13)
    real_job(row_ref, limits, split(b03) + split(b10) + b13, [cross.at[2], prvbx], both(PRVX))


def end_kernel(row_ref, b03, b10, b13a, b13b, prvb):
    limits = both(L_13) + both(L_03) + both(L_10)
    real_job(row_ref, limits, [b13a, b13b, *split(b03), *split(b10)], [prvb], [PRV + 1])


def gather_kernel(rows_ref, swapped_ref, side_ref, kept_ref, to03_ref, to01_ref, prv_ref):
    within = jnp.maximum(rows_ref[W00 : W00 + 2, :], rows_ref[KOWN : KOWN + 2, :])
    within = jnp.maximum(within, jnp.maximum(swapped_ref[0:2, :], side_ref[0:2, :]))
    kept_ref[0:2, :] = jnp.maximum(within, -1.0)
    kept_ref[2:4, :] = jnp.maximum(jnp.maximum(rows_ref[A00 : A00 + 2, :], side_ref[2:4, :]), rows_ref[FLOOR : FLOOR + 1, :])
    kept_ref[4:6, :] = rows_ref[REAL : REAL + 2, :]
    kept_ref[6:8, :] = rows_ref[REAL : REAL + 2, :]
    to03_ref[...] = jnp.maximum(rows_ref[W03 : W03 + 4, :], side_ref[4:8, :])
    to01_ref[0:4, :] = rows_ref[W01 : W01 + 4, :]
    to01_ref[4:6, :] = jnp.maximum(rows_ref[K01 : K01 + 2, :], swapped_ref[2:4, :])
    prv_ref[0:2, :] = jnp.maximum(rows_ref[PRV : PRV + 2, :], swapped_ref[4:6, :])
    prv_ref[2:8, :] = rows_ref[0:6, :]


def final_kernel(kept, b03, b01, bprv, within_ref, adjacent_ref):
    for h in range(2):
        row = lambda ref, at: ref[at + h : at + h + 1, :]
        within = [row(kept, 0), row(b03, 0), row(b01, 0), row(b01, 4)]
        adjacent = [row(kept, 2), row(b03, 2), row(b01, 2), row(bprv, 0)]
        real = row(kept, 4) > 0
        place = slice(h * HALF, (h + 1) * HALF)
        within_ref[:, place] = jnp.where(real, functools.reduce(jnp.maximum, within), 0.0)
        adjacent_ref[:, place] = jnp.where(real, functools.reduce(jnp.maximum, adjacent), 0.0)


def small_call(name, body, shapes, arrays):
    return pl.pallas_call(
        body,
        in_specs=[VMEM] * len(arrays),
        out_specs=[VMEM] * len(shapes),
        out_shape=[jax.ShapeDtypeStruct(shape, jnp.float32) for shape in shapes],
        name=name,
        compiler_params=pltpu.CompilerParams(vmem_limit_bytes=2 * 2**20),
    )(*arrays)


def on_device(embeddings, sizes, ranks):
    rows = embeddings.shape[1]
    own, own_a, own_b = packed(embeddings[0], ranks, sizes)

    b01a = send("b01a", own_a, row=-1)
    b03 = send("b03", own, row=1)
    nxt = send("nxt", own, cluster=-1)
    b10 = send("b10", own, col=1)
    ownx = send("ownx", own, core=1)
    b01b = send("b01b", after(own_b, ownx), row=-1)
    empty = jnp.zeros((N_ROWS, HALF), jnp.float32)
    state, own_ranks = kernel_call("self", self_kernel, 1, empty, [own, ownx], [rank_shape(4)], [sizes])
    prva = send("prva", after(b01a, state), cluster=1)
    state = kernel_call("first", first_kernel, 0.5, state, [own, ownx, own_ranks, b01a])

    prvb = send("prvb", after(b01b, state), cluster=1)
    b03, b10, state = lax.optimization_barrier((b03, b10, state))
    nxt, b01b, prva, state = lax.optimization_barrier((nxt, b01b, prva, state))
    b13a = send("b13a", b03[0], col=1)
    b13b = send("b13b", b10[1], row=1)
    half = jax.ShapeDtypeStruct((HALF, D), jnp.bfloat16)
    bundle, nxta, nxtb = pl.pallas_call(
        bundle_kernel,
        in_specs=[VMEM] * 4,
        out_specs=[VMEM] * 3,
        out_shape=[jax.ShapeDtypeStruct((3, PAY, D), jnp.bfloat16), half, half],
        name="bundle",
        compiler_params=pltpu.CompilerParams(vmem_limit_bytes=8 * 2**20),
    )(b01a, b01b, nxt, prva)
    nxtax = send("nxtax", nxta, core=1)
    nxtbx = send("nxtbx", nxtb, core=1)
    state, ranks1 = kernel_call(
        "same", same_kernel, 4.5, state,
        [own, ownx, own_ranks, b01a, b01b, b03, b10, nxt, prva], [rank_shape(2)],
    )
    state = kernel_call("other", other_kernel, 0, state, [own, b01a, b01b, b03, b10, nxtax, nxtbx])
    cross = send("cross", after(bundle, state), core=1)
    kept = [own, ownx, own_ranks, b01a, b01b, ranks1, nxt, prva]
    state = kernel_call("left", functools.partial(half_kernel, 0), 1, state, [*kept, b13a])
    prvb, state = lax.optimization_barrier((prvb, state))
    state = kernel_call("right", functools.partial(half_kernel, 1), LONG, state, [*kept, b13b])
    prvbx = send("prvbx", prvb, core=1)
    state = kernel_call(
        "cross", cross_kernel, 4, state, [b03, b10, b13a, b13b, nxtax, nxtbx, cross, prvbx]
    )

    swapped = send("swapped", state[KOWNX : KOWNX + 6], core=1)
    side = send("side", state[W10 : W10 + 8], col=1)
    state = kernel_call("end", end_kernel, 1, state, [b03, b10, b13a, b13b, prvb])
    shapes = [(8, HALF), (4, HALF), (6, HALF), (8, HALF)]
    kept, to_03, to_01, to_prv = small_call("gather", gather_kernel, shapes, [state, swapped, side])
    back_prv = send("back_prv", to_prv, cluster=-1, row=1)
    back_01 = send("back_01", to_01, row=1)
    back_03 = send("back_03", to_03, row=-1)
    return tuple(small_call("final", final_kernel, [(1, rows)] * 2, [kept, back_03, back_01, back_prv]))


def solution(mesh):
    in_specs = (P("group", "helper", None), P(), P("group", "helper"))
    out_specs = (P("group", "helper"), P("group", "helper"))
    return jax.shard_map(
        on_device, mesh=mesh, in_specs=in_specs, out_specs=out_specs, check_vma=False
    )
```

```python
import functools
import math

import jax
import jax.numpy as jnp
from jax import lax
from jax.experimental import pallas as pl
from jax.experimental.pallas import tpu as pltpu
from jax.sharding import PartitionSpec as P

D = 1024
HALF = 256
EXTRA = 8
PAY = HALF + EXTRA
BASE = 64
FAR = 8192.0
LOW = -4.0
AXES = ("group", "helper")
VMEM = pl.BlockSpec(memory_space=pltpu.VMEM)
SMEM = pl.BlockSpec(memory_space=pltpu.SMEM)


def place(index):
    group, helper = divmod(index, 16)
    return {
        "part": group // 4,
        "z": group % 4,
        "row": helper // 4,
        "col": (helper // 2) % 2,
        "core": helper % 2,
    }


def number(at):
    return (at["part"] * 4 + at["z"]) * 16 + at["row"] * 4 + at["col"] * 2 + at["core"]


def pairs(col=0, row=0, core=0, cluster=0):
    out = []
    for source in range(128):
        at = place(source)
        step = at["part"] * 4 + at["z"] + cluster
        flip = 1 if step // 4 != at["part"] else 0
        at["part"], at["z"] = (step // 4) % 2, step % 4
        at["col"] = (at["col"] + col + flip) % 2
        at["row"] = (at["row"] + row) % 4
        at["core"] = (at["core"] + core) % 2
        out.append((source, number(at)))
    return out


def send(name, value, **shift):
    with jax.named_scope(name):
        return lax.ppermute(value, AXES, pairs(**shift))


def after(value, *others):
    return lax.optimization_barrier((value, *others))[0]


def inner(keys, queries):
    return lax.dot_general(
        keys, queries, (((1,), (1,)), ((), ())), preferred_element_type=jnp.float32
    )


PARTS = 4
PACK_MIB = 56
LONG = 10**8


def own_count(sizes_ref, step=0):
    return sizes_ref[lax.rem(lax.axis_index("group") + step, lax.axis_size("group"))]


def pack_kernel(sizes_hbm, rows_hbm, rank_hbm, pay_hbm, a_hbm, b_hbm, rows_ref, rank_ref, pay_ref, sizes_ref, sem, out_sem):
    part = 2 * HALF // PARTS
    copies = [
        pltpu.make_async_copy(rows_hbm.at[pl.ds(i * part, part)], rows_ref.at[pl.ds(i * part, part)], sem.at[i])
        for i in range(PARTS)
    ]
    rank_copy = pltpu.make_async_copy(rank_hbm, rank_ref, sem.at[PARTS])
    sizes_copy = pltpu.make_async_copy(sizes_hbm, sizes_ref, sem.at[PARTS + 1])
    for copy in [rank_copy, sizes_copy, *copies]:
        copy.start()
    rank_copy.wait()
    sizes_copy.wait()
    left = own_count(sizes_ref) - lax.axis_index("helper") * 2 * HALF
    outs = []
    for half, half_hbm in enumerate((a_hbm, b_hbm)):
        rank = rank_ref[:, half * HALF : (half + 1) * HALF]
        position = lax.broadcasted_iota(jnp.int32, (1, HALF), 1) + half * HALF
        real = position < left
        high = jnp.where(real, rank // BASE, int(FAR) // BASE).astype(jnp.float32)
        low = jnp.where(real, rank % BASE, 0).astype(jnp.float32)
        row = jnp.concatenate([high, low, jnp.zeros((1, D - 2 * HALF), jnp.float32)], axis=1)
        pay_ref[half, HALF:, :] = jnp.broadcast_to(row, (EXTRA, D)).astype(jnp.bfloat16)
        for i in range(half * PARTS // 2, (half + 1) * PARTS // 2):
            copies[i].wait()
            rows = rows_ref[i * part : (i + 1) * part, :]
            scale = lax.rsqrt(jnp.mean(rows * rows, axis=-1, keepdims=True) + 1e-06) / math.sqrt(D)
            at = i * part - half * HALF
            pay_ref[half, at : at + part, :] = (rows * scale).astype(jnp.bfloat16)
        outs.append(pltpu.make_async_copy(pay_ref.at[half], pay_hbm.at[half], out_sem.at[2 * half]))
        outs.append(pltpu.make_async_copy(pay_ref.at[half], half_hbm, out_sem.at[2 * half + 1]))
        for out in outs[2 * half :]:
            out.start()
    for out in outs:
        out.wait()


def packed(rows, ranks, sizes):
    half = jax.ShapeDtypeStruct((PAY, D), jnp.bfloat16)
    return pl.pallas_call(
        pack_kernel,
        in_specs=[pl.BlockSpec(memory_space=pltpu.HBM)] * 3,
        out_specs=[pl.BlockSpec(memory_space=pltpu.HBM)] * 3,
        out_shape=[jax.ShapeDtypeStruct((2, PAY, D), jnp.bfloat16), half, half],
        scratch_shapes=[
            pltpu.VMEM((2 * HALF, D), jnp.float32),
            pltpu.VMEM((1, 2 * HALF), jnp.int32),
            pltpu.VMEM((2, PAY, D), jnp.bfloat16),
            pltpu.SMEM(sizes.shape, jnp.int32),
            pltpu.SemaphoreType.DMA((PARTS + 2,)),
            pltpu.SemaphoreType.DMA((4,)),
        ],
        name="pack",
        compiler_params=pltpu.CompilerParams(vmem_limit_bytes=PACK_MIB * 2**20),
        cost_estimate=pl.CostEstimate(flops=4 * 512 * D, bytes_accessed=4 * 2**20, transcendentals=512),
    )(sizes, rows, ranks)


def rank_row(tail):
    tail = tail[0:1, :].astype(jnp.float32)
    return tail[:, :HALF] * BASE + tail[:, HALF:]


def rank_column(tail):
    return jnp.transpose(jnp.broadcast_to(rank_row(tail), (128, HALF)))


def split(ref):
    return [ref.at[0], ref.at[1]]


def tops(scores):
    return jnp.max(scores.reshape(HALF // 8, 8, 128), axis=0)


def pieces(scores):
    return [scores[:, c : c + 128] for c in range(0, HALF, 128)]


def keep(row_ref, places, best):
    for at, value in zip(places, best):
        value = jnp.max(value, axis=0, keepdims=True)
        row_ref[at : at + 1, :] = jnp.maximum(row_ref[at : at + 1, :], value)


def lowest(queries):
    return [jnp.full((8, HALF), LOW, jnp.float32) for _ in queries]


ALL = lambda k, q: True
SHARE = {(0, 0), (1, 0), (1, 1), (2, 0), (2, 1), (3, 1)}


def pair_job(row_ref, ranks, keys, queries, q_at, k_at, wanted=ALL):
    q_rank = [rank_row(query[HALF:, : 2 * HALF]) for query in queries]
    best, sides = lowest(queries), []
    for n, key_ref in enumerate(keys):
        key, k_rank, side = key_ref[:HALF, :], ranks[n][...], None
        for i, query in enumerate(queries):
            if not wanted(n, i):
                continue
            parts = []
            for c, piece in enumerate(pieces(inner(key, query[:HALF, :]))):
                earlier = k_rank < q_rank[i][:, c * 128 : c * 128 + 128]
                parts.append(tops(jnp.where(earlier, piece, LOW)))
                if k_at is not None:
                    other = jnp.where(earlier, LOW, piece)
                    side = other if side is None else jnp.maximum(side, other)
            best[i] = jnp.maximum(best[i], jnp.concatenate(parts, axis=1))
        if side is not None:
            sides.append((k_at[n], side))
    keep(row_ref, q_at, best)
    for at, side in sides:
        keep(row_ref, [at], [jnp.transpose(side)])


def real_job(row_ref, limits, keys, queries, q_at):
    best = lowest(queries)
    position = lax.broadcasted_iota(jnp.int32, (HALF, 128), 0).astype(jnp.float32)
    for n, key_ref in enumerate(keys):
        key = key_ref[:HALF, :]
        real = position < row_ref[limits[n] : limits[n] + 1, :128]
        for i, query in enumerate(queries):
            parts = [tops(jnp.where(real, piece, LOW)) for piece in pieces(inner(key, query[:HALF, :]))]
            best[i] = jnp.maximum(best[i], jnp.concatenate(parts, axis=1))
    keep(row_ref, q_at, best)


def put_ranks(rank_ref, halves):
    for n, half in enumerate(halves):
        rank_ref[n] = rank_column(half[HALF:, : 2 * HALF])


def rank_shape(halves):
    return jax.ShapeDtypeStruct((halves, HALF, 128), jnp.float32)


def kernel_call(name, body, tasks, rows, arrays, extra_out=(), scalars=()):
    n = len(arrays) + len(scalars)

    def kernel(rows_in, *refs):
        row_ref = refs[n]
        row_ref[...] = rows_in[...]
        body(row_ref, *refs[:n], *refs[n + 1 :])

    out = pl.pallas_call(
        kernel,
        in_specs=[VMEM] * (1 + len(arrays)) + [SMEM] * len(scalars),
        out_specs=[VMEM] * (1 + len(extra_out)),
        out_shape=[jax.ShapeDtypeStruct((N_ROWS, HALF), jnp.float32), *extra_out],
        name=name,
        compiler_params=pltpu.CompilerParams(vmem_limit_bytes=14 * 2**20),
        cost_estimate=pl.CostEstimate(flops=int(tasks * 1024) if tasks == LONG else 0, bytes_accessed=0, transcendentals=0),
    )(rows, *arrays, *scalars)
    return out if extra_out else out[0]


W00, A00, KOWN, W03, A03, W10, A10 = 0, 2, 4, 6, 8, 10, 12
W13, A13, W01, A01, K01, PRV, KOWNX, K01X, PRVX = 14, 16, 18, 20, 22, 24, 26, 28, 30
REAL, FLOOR = 32, 34
L_NXT, L_NXTX, L_03, L_10, L_13 = 40, 42, 44, 46, 48
N_ROWS = 56


def both(at):
    return [at, at + 1]


def real_rows(sizes_ref, col, row, other=0, cluster=0):
    helper = lax.axis_index("helper")
    flip = jnp.where(lax.axis_index("group") % 4 == 3, cluster, 0)
    row = (helper // 4 + row) % 4
    col = (helper // 2 + col + flip) % 2
    start = own_count(sizes_ref, cluster) - (row * 4 + col * 2 + (helper + other) % 2) * 2 * HALF
    return [start, start - HALF]


def self_kernel(row_ref, own, ownx, sizes_ref, ranks):
    keys = split(own) + split(ownx)
    put_ranks(ranks, keys)
    row_ref[...] = jnp.full(row_ref.shape, LOW, jnp.float32)
    left = own_count(sizes_ref) - lax.axis_index("helper") * 2 * HALF
    for h in range(2):
        position = lax.broadcasted_iota(jnp.int32, (1, HALF), 1) + h * HALF
        row_ref[REAL + h : REAL + h + 1, :] = jnp.where(position < left, 1.0, 0.0)
    floor = jnp.where(own_count(sizes_ref, 1) < 2 * HALF * lax.axis_size("helper"), -1.0, LOW)
    row_ref[FLOOR : FLOOR + 1, :] = jnp.full((1, HALF), floor, jnp.float32)
    limits = [(L_NXT, real_rows(sizes_ref, 0, 0, 0, 1)), (L_NXTX, real_rows(sizes_ref, 0, 0, 1, 1))]
    limits += [(L_03, real_rows(sizes_ref, 0, -1)), (L_10, real_rows(sizes_ref, 1, 0)), (L_13, real_rows(sizes_ref, 1, -1))]
    for at, counts in limits:
        for h, count in enumerate(counts):
            row_ref[at + h : at + h + 1, :] = jnp.full((1, HALF), count, jnp.int32).astype(jnp.float32)
    pair_job(row_ref, [ranks.at[n] for n in range(4)], keys, split(own), both(W00), None)


def own_job(row_ref, own, ownx, ranks, queries, places, wanted=ALL):
    keys = split(own) + split(ownx)
    pair_job(row_ref, [ranks.at[n] for n in range(4)], keys, queries, places, both(KOWN) + both(KOWNX), wanted)


def first_kernel(row_ref, own, ownx, ranks, b01a):
    own_job(row_ref, own, ownx, ranks, [b01a], [W01])


def bundle_kernel(b01a, b01b, nxt, prva, bundle, nxta, nxtb):
    nxta[...] = nxt[0, :HALF, :]
    nxtb[...] = nxt[1, :HALF, :]
    for n, half in enumerate([b01a, b01b, prva]):
        bundle[n] = half[...]


def same_kernel(row_ref, own, ownx, own_ranks, b01a, b01b, b03, b10, nxt, prva, ranks):
    places = [W01 + 1, W10, W10 + 1]
    own_job(row_ref, own, ownx, own_ranks, [b01b, *split(b10)], places, lambda k, q: q == 0 or (k, q - 1) in SHARE)
    queries = [*split(own), b01a, b01b, *split(b03), *split(b10)]
    places = both(A00) + both(A01) + both(A03) + both(A10)
    real_job(row_ref, both(L_NXT), split(nxt), queries, places)
    put_ranks(ranks, [b01a, b01b])
    pair_job(
        row_ref, [ranks.at[0], ranks.at[1]], [b01a, b01b], split(b03), both(W03), both(K01),
        lambda k, q: (k, q) in SHARE,
    )
    limits = both(L_03) + both(L_10)
    real_job(row_ref, limits, split(b03) + split(b10), [prva], [PRV])


def half_kernel(h, row_ref, own, ownx, ranks, b01a, b01b, ranks1, nxt, prva, b13):
    own_job(row_ref, own, ownx, ranks, [b13], [W13 + h])
    pair_job(
        row_ref, [ranks1.at[0], ranks1.at[1]], [b01a, b01b], [b13], [W13 + h], both(K01), lambda k, q: (k, h) in SHARE
    )
    real_job(row_ref, both(L_NXT), split(nxt), [b13], [A13 + h])
    real_job(row_ref, [L_13 + h], [b13], [prva], [PRV])


def other_kernel(row_ref, own, b01a, b01b, b03, b10, nxtax, nxtbx):
    queries = [*split(own), b01a, b01b, *split(b03), *split(b10)]
    places = both(A00) + both(A01) + both(A03) + both(A10)
    real_job(row_ref, both(L_NXTX), [nxtax, nxtbx], queries, places)


def cross_kernel(row_ref, b03, b13a, b13b, nxtax, nxtbx, cross):
    b13 = [b13a, b13b]
    real_job(row_ref, both(L_NXTX), [nxtax, nxtbx], b13, both(A13))
    one = [cross.at[0], cross.at[1]]
    ranks = [rank_column(half[HALF:, : 2 * HALF]) for half in one]
    pair_job(
        row_ref, ranks, one, split(b03) + b13, both(W03) + both(W13), both(K01X),
        lambda k, q: (2 + k, q % 2) in SHARE,
    )


def prev_kernel(row_ref, b03, b10, b13a, b13b, cross, prvbx):
    limits = both(L_03) + both(L_10) + both(L_13)
    real_job(row_ref, limits, [*split(b03), *split(b10), b13a, b13b], [cross.at[2], prvbx], both(PRVX))


def end_kernel(row_ref, b03, b10, b13a, b13b, prvb):
    limits = both(L_13) + both(L_03) + both(L_10)
    real_job(row_ref, limits, [b13a, b13b, *split(b03), *split(b10)], [prvb], [PRV + 1])


def gather_kernel(rows_ref, swapped_ref, side_ref, kept_ref, to03_ref, to01_ref, prv_ref):
    within = jnp.maximum(rows_ref[W00 : W00 + 2, :], rows_ref[KOWN : KOWN + 2, :])
    within = jnp.maximum(within, jnp.maximum(swapped_ref[0:2, :], side_ref[0:2, :]))
    kept_ref[0:2, :] = jnp.maximum(within, -1.0)
    kept_ref[2:4, :] = jnp.maximum(jnp.maximum(rows_ref[A00 : A00 + 2, :], side_ref[2:4, :]), rows_ref[FLOOR : FLOOR + 1, :])
    kept_ref[4:6, :] = rows_ref[REAL : REAL + 2, :]
    kept_ref[6:8, :] = rows_ref[REAL : REAL + 2, :]
    to03_ref[...] = jnp.maximum(rows_ref[W03 : W03 + 4, :], side_ref[4:8, :])
    to01_ref[0:4, :] = rows_ref[W01 : W01 + 4, :]
    to01_ref[4:6, :] = jnp.maximum(rows_ref[K01 : K01 + 2, :], swapped_ref[2:4, :])
    prv_ref[0:2, :] = jnp.maximum(rows_ref[PRV : PRV + 2, :], swapped_ref[4:6, :])
    prv_ref[2:8, :] = rows_ref[0:6, :]


def final_kernel(kept, b03, b01, bprv, within_ref, adjacent_ref):
    for h in range(2):
        row = lambda ref, at: ref[at + h : at + h + 1, :]
        within = [row(kept, 0), row(b03, 0), row(b01, 0), row(b01, 4)]
        adjacent = [row(kept, 2), row(b03, 2), row(b01, 2), row(bprv, 0)]
        real = row(kept, 4) > 0
        place = slice(h * HALF, (h + 1) * HALF)
        within_ref[:, place] = jnp.where(real, functools.reduce(jnp.maximum, within), 0.0)
        adjacent_ref[:, place] = jnp.where(real, functools.reduce(jnp.maximum, adjacent), 0.0)


def small_call(name, body, shapes, arrays):
    return pl.pallas_call(
        body,
        in_specs=[VMEM] * len(arrays),
        out_specs=[VMEM] * len(shapes),
        out_shape=[jax.ShapeDtypeStruct(shape, jnp.float32) for shape in shapes],
        name=name,
        compiler_params=pltpu.CompilerParams(vmem_limit_bytes=2 * 2**20),
    )(*arrays)


def on_device(embeddings, sizes, ranks):
    rows = embeddings.shape[1]
    own, own_a, own_b = packed(embeddings[0], ranks, sizes)

    b01a = send("b01a", own_a, row=-1)
    b03 = send("b03", own, row=1)
    nxt = send("nxt", own, cluster=-1)
    b10 = send("b10", own, col=1)
    ownx = send("ownx", own, core=1)
    b01b = send("b01b", after(own_b, ownx), row=-1)
    empty = jnp.zeros((N_ROWS, HALF), jnp.float32)
    state, own_ranks = kernel_call("self", self_kernel, 1, empty, [own, ownx], [rank_shape(4)], [sizes])
    prva = send("prva", after(b01a, state), cluster=1)
    state = kernel_call("first", first_kernel, 0.5, state, [own, ownx, own_ranks, b01a])

    prvb = send("prvb", after(b01b, state), cluster=1)
    b03, b10, state = lax.optimization_barrier((b03, b10, state))
    nxt, b01b, prva, state = lax.optimization_barrier((nxt, b01b, prva, state))
    b13a = send("b13a", b03[0], col=1)
    b13b = send("b13b", b10[1], row=1)
    half = jax.ShapeDtypeStruct((HALF, D), jnp.bfloat16)
    bundle, nxta, nxtb = pl.pallas_call(
        bundle_kernel,
        in_specs=[VMEM] * 4,
        out_specs=[VMEM] * 3,
        out_shape=[jax.ShapeDtypeStruct((3, PAY, D), jnp.bfloat16), half, half],
        name="bundle",
        compiler_params=pltpu.CompilerParams(vmem_limit_bytes=8 * 2**20),
    )(b01a, b01b, nxt, prva)
    nxtax = send("nxtax", nxta, core=1)
    nxtbx = send("nxtbx", nxtb, core=1)
    state, ranks1 = kernel_call(
        "same", same_kernel, 4.5, state,
        [own, ownx, own_ranks, b01a, b01b, b03, b10, nxt, prva], [rank_shape(2)],
    )
    state = kernel_call("other", other_kernel, 0, state, [own, b01a, b01b, b03, b10, nxtax, nxtbx])
    cross = send("cross", after(bundle, state), core=1)
    kept = [own, ownx, own_ranks, b01a, b01b, ranks1, nxt, prva]
    state = kernel_call("left", functools.partial(half_kernel, 0), 1, state, [*kept, b13a])
    prvb, state = lax.optimization_barrier((prvb, state))
    state = kernel_call("right", functools.partial(half_kernel, 1), LONG, state, [*kept, b13b])
    prvbx = send("prvbx", prvb, core=1)
    state = kernel_call("cross", cross_kernel, 0, state, [b03, b13a, b13b, nxtax, nxtbx, cross])

    side = send("side", state[W10 : W10 + 8], col=1)
    state = kernel_call("prev", prev_kernel, 0, state, [b03, b10, b13a, b13b, cross, prvbx])
    swapped = send("swapped", state[KOWNX : KOWNX + 6], core=1)
    state = kernel_call("end", end_kernel, 1, state, [b03, b10, b13a, b13b, prvb])
    shapes = [(8, HALF), (4, HALF), (6, HALF), (8, HALF)]
    kept, to_03, to_01, to_prv = small_call("gather", gather_kernel, shapes, [state, swapped, side])
    back_prv = send("back_prv", to_prv, cluster=-1, row=1)
    back_01 = send("back_01", to_01, row=1)
    back_03 = send("back_03", to_03, row=-1)
    return tuple(small_call("final", final_kernel, [(1, rows)] * 2, [kept, back_03, back_01, back_prv]))


def solution(mesh):
    in_specs = (P("group", "helper", None), P(), P("group", "helper"))
    out_specs = (P("group", "helper"), P("group", "helper"))
    return jax.shard_map(
        on_device, mesh=mesh, in_specs=in_specs, out_specs=out_specs, check_vma=False
    )
```

```python
import functools
import math

import jax
import jax.numpy as jnp
from jax import lax
from jax.experimental import pallas as pl
from jax.experimental.pallas import tpu as pltpu
from jax.sharding import PartitionSpec as P

D = 1024
HALF = 256
EXTRA = 16
PAY = HALF + EXTRA
BASE = 64
FAR = 8192.0
LOW = -4.0
AXES = ("group", "helper")
VMEM = pl.BlockSpec(memory_space=pltpu.VMEM)
SMEM = pl.BlockSpec(memory_space=pltpu.SMEM)


def place(index):
    group, helper = divmod(index, 16)
    return {
        "part": group // 4,
        "z": group % 4,
        "row": helper // 4,
        "col": (helper // 2) % 2,
        "core": helper % 2,
    }


def number(at):
    return (at["part"] * 4 + at["z"]) * 16 + at["row"] * 4 + at["col"] * 2 + at["core"]


def pairs(col=0, row=0, core=0, cluster=0):
    out = []
    for source in range(128):
        at = place(source)
        step = at["part"] * 4 + at["z"] + cluster
        flip = 1 if step // 4 != at["part"] else 0
        at["part"], at["z"] = (step // 4) % 2, step % 4
        at["col"] = (at["col"] + col + flip) % 2
        at["row"] = (at["row"] + row) % 4
        at["core"] = (at["core"] + core) % 2
        out.append((source, number(at)))
    return out


def send(name, value, **shift):
    with jax.named_scope(name):
        return lax.ppermute(value, AXES, pairs(**shift))


def after(value, *others):
    return lax.optimization_barrier((value, *others))[0]


def inner(keys, queries):
    return lax.dot_general(
        keys, queries, (((1,), (1,)), ((), ())), preferred_element_type=jnp.float32
    )


PARTS = 4
PACK_MIB = 56
LONG = 10**8


def own_count(sizes_ref, step=0):
    return sizes_ref[lax.rem(lax.axis_index("group") + step, lax.axis_size("group"))]


def pack_kernel(sizes_hbm, rows_hbm, rank_hbm, pay_hbm, a_hbm, b_hbm, rows_ref, rank_ref, pay_ref, sizes_ref, sem, out_sem):
    part = 2 * HALF // PARTS
    copies = [
        pltpu.make_async_copy(rows_hbm.at[pl.ds(i * part, part)], rows_ref.at[pl.ds(i * part, part)], sem.at[i])
        for i in range(PARTS)
    ]
    rank_copy = pltpu.make_async_copy(rank_hbm, rank_ref, sem.at[PARTS])
    sizes_copy = pltpu.make_async_copy(sizes_hbm, sizes_ref, sem.at[PARTS + 1])
    for copy in [rank_copy, sizes_copy, *copies]:
        copy.start()
    rank_copy.wait()
    sizes_copy.wait()
    left = own_count(sizes_ref) - lax.axis_index("helper") * 2 * HALF
    outs = []
    for half, half_hbm in enumerate((a_hbm, b_hbm)):
        rank = rank_ref[:, half * HALF : (half + 1) * HALF]
        position = lax.broadcasted_iota(jnp.int32, (1, HALF), 1) + half * HALF
        real = position < left
        high = jnp.where(real, rank // BASE, int(FAR) // BASE).astype(jnp.float32)
        low = jnp.where(real, rank % BASE, 0).astype(jnp.float32)
        row = jnp.concatenate([high, low, jnp.zeros((1, D - 2 * HALF), jnp.float32)], axis=1)
        pay_ref[half, HALF:, :] = jnp.broadcast_to(row, (EXTRA, D)).astype(jnp.bfloat16)
        for i in range(half * PARTS // 2, (half + 1) * PARTS // 2):
            copies[i].wait()
            rows = rows_ref[i * part : (i + 1) * part, :]
            scale = lax.rsqrt(jnp.mean(rows * rows, axis=-1, keepdims=True) + 1e-06) / math.sqrt(D)
            at = i * part - half * HALF
            pay_ref[half, at : at + part, :] = (rows * scale).astype(jnp.bfloat16)
        outs.append(pltpu.make_async_copy(pay_ref.at[half], pay_hbm.at[half], out_sem.at[2 * half]))
        outs.append(pltpu.make_async_copy(pay_ref.at[half], half_hbm, out_sem.at[2 * half + 1]))
        for out in outs[2 * half :]:
            out.start()
    for out in outs:
        out.wait()


def packed(rows, ranks, sizes):
    half = jax.ShapeDtypeStruct((PAY, D), jnp.bfloat16)
    return pl.pallas_call(
        pack_kernel,
        in_specs=[pl.BlockSpec(memory_space=pltpu.HBM)] * 3,
        out_specs=[pl.BlockSpec(memory_space=pltpu.HBM)] * 3,
        out_shape=[jax.ShapeDtypeStruct((2, PAY, D), jnp.bfloat16), half, half],
        scratch_shapes=[
            pltpu.VMEM((2 * HALF, D), jnp.float32),
            pltpu.VMEM((1, 2 * HALF), jnp.int32),
            pltpu.VMEM((2, PAY, D), jnp.bfloat16),
            pltpu.SMEM(sizes.shape, jnp.int32),
            pltpu.SemaphoreType.DMA((PARTS + 2,)),
            pltpu.SemaphoreType.DMA((4,)),
        ],
        name="pack",
        compiler_params=pltpu.CompilerParams(vmem_limit_bytes=PACK_MIB * 2**20),
        cost_estimate=pl.CostEstimate(flops=4 * 512 * D, bytes_accessed=4 * 2**20, transcendentals=512),
    )(sizes, rows, ranks)


def rank_row(tail):
    tail = tail[0:1, :].astype(jnp.float32)
    return tail[:, :HALF] * BASE + tail[:, HALF:]


def rank_column(tail):
    return jnp.transpose(jnp.broadcast_to(rank_row(tail), (128, HALF)))


def split(ref):
    return [ref.at[0], ref.at[1]]


def tops(scores):
    return jnp.max(scores.reshape(HALF // 8, 8, 128), axis=0)


def pieces(scores):
    return [scores[:, c : c + 128] for c in range(0, HALF, 128)]


def keep(row_ref, places, best):
    for at, value in zip(places, best):
        value = jnp.max(value, axis=0, keepdims=True)
        row_ref[at : at + 1, :] = jnp.maximum(row_ref[at : at + 1, :], value)


def lowest(queries):
    return [jnp.full((8, HALF), LOW, jnp.float32) for _ in queries]


ALL = lambda k, q: True
SHARE = {(0, 0), (1, 0), (1, 1), (2, 0), (2, 1), (3, 1)}


def pair_job(row_ref, ranks, keys, queries, q_at, k_at, wanted=ALL):
    q_rank = [rank_row(query[HALF:, : 2 * HALF]) for query in queries]
    best, sides = lowest(queries), []
    for n, key_ref in enumerate(keys):
        key, k_rank, side = key_ref[:HALF, :], ranks[n][...], None
        for i, query in enumerate(queries):
            if not wanted(n, i):
                continue
            parts = []
            for c, piece in enumerate(pieces(inner(key, query[:HALF, :]))):
                earlier = k_rank < q_rank[i][:, c * 128 : c * 128 + 128]
                parts.append(tops(jnp.where(earlier, piece, LOW)))
                if k_at is not None:
                    other = jnp.where(earlier, LOW, piece)
                    side = other if side is None else jnp.maximum(side, other)
            best[i] = jnp.maximum(best[i], jnp.concatenate(parts, axis=1))
        if side is not None:
            sides.append((k_at[n], side))
    keep(row_ref, q_at, best)
    for at, side in sides:
        keep(row_ref, [at], [jnp.transpose(side)])


def real_job(row_ref, limits, keys, queries, q_at):
    best = lowest(queries)
    position = lax.broadcasted_iota(jnp.int32, (HALF, 128), 0).astype(jnp.float32)
    for n, key_ref in enumerate(keys):
        key = key_ref[:HALF, :]
        real = position < row_ref[limits[n] : limits[n] + 1, :128]
        for i, query in enumerate(queries):
            parts = [tops(jnp.where(real, piece, LOW)) for piece in pieces(inner(key, query[:HALF, :]))]
            best[i] = jnp.maximum(best[i], jnp.concatenate(parts, axis=1))
    keep(row_ref, q_at, best)


def put_ranks(rank_ref, halves):
    for n, half in enumerate(halves):
        rank_ref[n] = rank_column(half[HALF:, : 2 * HALF])


def rank_shape(halves):
    return jax.ShapeDtypeStruct((halves, HALF, 128), jnp.float32)


def kernel_call(name, body, tasks, rows, arrays, extra_out=(), scalars=()):
    n = len(arrays) + len(scalars)

    def kernel(rows_in, *refs):
        row_ref = refs[n]
        row_ref[...] = rows_in[...]
        body(row_ref, *refs[:n], *refs[n + 1 :])

    out = pl.pallas_call(
        kernel,
        in_specs=[VMEM] * (1 + len(arrays)) + [SMEM] * len(scalars),
        out_specs=[VMEM] * (1 + len(extra_out)),
        out_shape=[jax.ShapeDtypeStruct((N_ROWS, HALF), jnp.float32), *extra_out],
        name=name,
        compiler_params=pltpu.CompilerParams(vmem_limit_bytes=14 * 2**20),
        cost_estimate=pl.CostEstimate(flops=int(tasks * 1024) if tasks == LONG else 0, bytes_accessed=0, transcendentals=0),
    )(rows, *arrays, *scalars)
    return out if extra_out else out[0]


W00, A00, KOWN, W03, A03, W10, A10 = 0, 2, 4, 6, 8, 10, 12
W13, A13, W01, A01, K01, PRV, KOWNX, K01X, PRVX = 14, 16, 18, 20, 22, 24, 26, 28, 30
REAL, FLOOR = 32, 34
L_NXT, L_NXTX, L_03, L_10, L_13 = 40, 42, 44, 46, 48
N_ROWS = 56


def both(at):
    return [at, at + 1]


def real_rows(sizes_ref, col, row, other=0, cluster=0):
    helper = lax.axis_index("helper")
    flip = jnp.where(lax.axis_index("group") % 4 == 3, cluster, 0)
    row = (helper // 4 + row) % 4
    col = (helper // 2 + col + flip) % 2
    start = own_count(sizes_ref, cluster) - (row * 4 + col * 2 + (helper + other) % 2) * 2 * HALF
    return [start, start - HALF]


def self_kernel(row_ref, own, ownx, sizes_ref, ranks):
    keys = split(own) + split(ownx)
    put_ranks(ranks, keys)
    row_ref[...] = jnp.full(row_ref.shape, LOW, jnp.float32)
    left = own_count(sizes_ref) - lax.axis_index("helper") * 2 * HALF
    for h in range(2):
        position = lax.broadcasted_iota(jnp.int32, (1, HALF), 1) + h * HALF
        row_ref[REAL + h : REAL + h + 1, :] = jnp.where(position < left, 1.0, 0.0)
    floor = jnp.where(own_count(sizes_ref, 1) < 2 * HALF * lax.axis_size("helper"), -1.0, LOW)
    row_ref[FLOOR : FLOOR + 1, :] = jnp.full((1, HALF), floor, jnp.float32)
    limits = [(L_NXT, real_rows(sizes_ref, 0, 0, 0, 1)), (L_NXTX, real_rows(sizes_ref, 0, 0, 1, 1))]
    limits += [(L_03, real_rows(sizes_ref, 0, -1)), (L_10, real_rows(sizes_ref, 1, 0)), (L_13, real_rows(sizes_ref, 1, -1))]
    for at, counts in limits:
        for h, count in enumerate(counts):
            row_ref[at + h : at + h + 1, :] = jnp.full((1, HALF), count, jnp.int32).astype(jnp.float32)
    pair_job(row_ref, [ranks.at[n] for n in range(4)], keys, split(own), both(W00), None)


def own_job(row_ref, own, ownx, ranks, queries, places, wanted=ALL):
    keys = split(own) + split(ownx)
    pair_job(row_ref, [ranks.at[n] for n in range(4)], keys, queries, places, both(KOWN) + both(KOWNX), wanted)


def first_kernel(row_ref, own, ownx, ranks, b01a):
    own_job(row_ref, own, ownx, ranks, [b01a], [W01])


def bundle_kernel(b01a, b01b, nxt, prva, bundle, nxta, nxtb):
    nxta[...] = nxt[0, :HALF, :]
    nxtb[...] = nxt[1, :HALF, :]
    for n, half in enumerate([b01a, b01b, prva]):
        bundle[n] = half[...]


def same_kernel(row_ref, own, ownx, own_ranks, b01a, b01b, b03, b10, nxt, prva, ranks):
    places = [W01 + 1, W10, W10 + 1]
    own_job(row_ref, own, ownx, own_ranks, [b01b, *split(b10)], places, lambda k, q: q == 0 or (k, q - 1) in SHARE)
    queries = [*split(own), b01a, b01b, *split(b03), *split(b10)]
    places = both(A00) + both(A01) + both(A03) + both(A10)
    real_job(row_ref, both(L_NXT), split(nxt), queries, places)
    put_ranks(ranks, [b01a, b01b])
    pair_job(
        row_ref, [ranks.at[0], ranks.at[1]], [b01a, b01b], split(b03), both(W03), both(K01),
        lambda k, q: (k, q) in SHARE,
    )
    limits = both(L_03) + both(L_10)
    real_job(row_ref, limits, split(b03) + split(b10), [prva], [PRV])


def half_kernel(h, row_ref, own, ownx, ranks, b01a, b01b, ranks1, nxt, prva, b13):
    own_job(row_ref, own, ownx, ranks, [b13], [W13 + h])
    pair_job(
        row_ref, [ranks1.at[0], ranks1.at[1]], [b01a, b01b], [b13], [W13 + h], both(K01), lambda k, q: (k, h) in SHARE
    )
    real_job(row_ref, both(L_NXT), split(nxt), [b13], [A13 + h])
    real_job(row_ref, [L_13 + h], [b13], [prva], [PRV])


def other_kernel(row_ref, own, b01a, b01b, b03, b10, nxtax, nxtbx):
    queries = [*split(own), b01a, b01b, *split(b03), *split(b10)]
    places = both(A00) + both(A01) + both(A03) + both(A10)
    real_job(row_ref, both(L_NXTX), [nxtax, nxtbx], queries, places)


def cross_kernel(row_ref, b03, b13a, b13b, nxtax, nxtbx, cross):
    b13 = [b13a, b13b]
    real_job(row_ref, both(L_NXTX), [nxtax, nxtbx], b13, both(A13))
    one = [cross.at[0], cross.at[1]]
    ranks = [rank_column(half[HALF:, : 2 * HALF]) for half in one]
    pair_job(
        row_ref, ranks, one, split(b03) + b13, both(W03) + both(W13), both(K01X),
        lambda k, q: (2 + k, q % 2) in SHARE,
    )


def prev_kernel(row_ref, b03, b10, b13a, b13b, cross, prvbx):
    limits = both(L_03) + both(L_10) + both(L_13)
    real_job(row_ref, limits, [*split(b03), *split(b10), b13a, b13b], [cross.at[2], prvbx], both(PRVX))


def end_kernel(row_ref, b03, b10, b13a, b13b, prvb):
    limits = both(L_13) + both(L_03) + both(L_10)
    real_job(row_ref, limits, [b13a, b13b, *split(b03), *split(b10)], [prvb], [PRV + 1])


def gather_kernel(rows_ref, swapped_ref, side_ref, kept_ref, to03_ref, to01_ref, prv_ref):
    within = jnp.maximum(rows_ref[W00 : W00 + 2, :], rows_ref[KOWN : KOWN + 2, :])
    within = jnp.maximum(within, jnp.maximum(swapped_ref[0:2, :], side_ref[0:2, :]))
    kept_ref[0:2, :] = jnp.maximum(within, -1.0)
    kept_ref[2:4, :] = jnp.maximum(jnp.maximum(rows_ref[A00 : A00 + 2, :], side_ref[2:4, :]), rows_ref[FLOOR : FLOOR + 1, :])
    kept_ref[4:6, :] = rows_ref[REAL : REAL + 2, :]
    kept_ref[6:8, :] = rows_ref[REAL : REAL + 2, :]
    to03_ref[...] = jnp.maximum(rows_ref[W03 : W03 + 4, :], side_ref[4:8, :])
    to01_ref[0:4, :] = rows_ref[W01 : W01 + 4, :]
    to01_ref[4:6, :] = jnp.maximum(rows_ref[K01 : K01 + 2, :], swapped_ref[2:4, :])
    prv_ref[0:2, :] = jnp.maximum(rows_ref[PRV : PRV + 2, :], swapped_ref[4:6, :])
    prv_ref[2:8, :] = rows_ref[0:6, :]


def final_kernel(kept, b03, b01, bprv, within_ref, adjacent_ref):
    for h in range(2):
        row = lambda ref, at: ref[at + h : at + h + 1, :]
        within = [row(kept, 0), row(b03, 0), row(b01, 0), row(b01, 4)]
        adjacent = [row(kept, 2), row(b03, 2), row(b01, 2), row(bprv, 0)]
        real = row(kept, 4) > 0
        place = slice(h * HALF, (h + 1) * HALF)
        within_ref[:, place] = jnp.where(real, functools.reduce(jnp.maximum, within), 0.0)
        adjacent_ref[:, place] = jnp.where(real, functools.reduce(jnp.maximum, adjacent), 0.0)


def small_call(name, body, shapes, arrays):
    return pl.pallas_call(
        body,
        in_specs=[VMEM] * len(arrays),
        out_specs=[VMEM] * len(shapes),
        out_shape=[jax.ShapeDtypeStruct(shape, jnp.float32) for shape in shapes],
        name=name,
        compiler_params=pltpu.CompilerParams(vmem_limit_bytes=2 * 2**20),
    )(*arrays)


def on_device(embeddings, sizes, ranks):
    rows = embeddings.shape[1]
    own, own_a, own_b = packed(embeddings[0], ranks, sizes)

    b01a = send("b01a", own_a, row=-1)
    b03 = send("b03", own, row=1)
    nxt = send("nxt", own, cluster=-1)
    b10 = send("b10", own, col=1)
    ownx = send("ownx", own, core=1)
    b01b = send("b01b", after(own_b, ownx), row=-1)
    empty = jnp.zeros((N_ROWS, HALF), jnp.float32)
    state, own_ranks = kernel_call("self", self_kernel, 1, empty, [own, ownx], [rank_shape(4)], [sizes])
    prva = send("prva", after(b01a, state), cluster=1)
    state = kernel_call("first", first_kernel, 0.5, state, [own, ownx, own_ranks, b01a])

    prvb = send("prvb", after(b01b, state), cluster=1)
    b03, b10, state = lax.optimization_barrier((b03, b10, state))
    nxt, b01b, prva, state = lax.optimization_barrier((nxt, b01b, prva, state))
    b13a = send("b13a", b03[0], col=1)
    b13b = send("b13b", b10[1], row=1)
    half = jax.ShapeDtypeStruct((HALF, D), jnp.bfloat16)
    bundle, nxta, nxtb = pl.pallas_call(
        bundle_kernel,
        in_specs=[VMEM] * 4,
        out_specs=[VMEM] * 3,
        out_shape=[jax.ShapeDtypeStruct((3, PAY, D), jnp.bfloat16), half, half],
        name="bundle",
        compiler_params=pltpu.CompilerParams(vmem_limit_bytes=8 * 2**20),
    )(b01a, b01b, nxt, prva)
    nxtax = send("nxtax", nxta, core=1)
    nxtbx = send("nxtbx", nxtb, core=1)
    state, ranks1 = kernel_call(
        "same", same_kernel, 4.5, state,
        [own, ownx, own_ranks, b01a, b01b, b03, b10, nxt, prva], [rank_shape(2)],
    )
    state = kernel_call("other", other_kernel, 0, state, [own, b01a, b01b, b03, b10, nxtax, nxtbx])
    cross = send("cross", after(bundle, state), core=1)
    kept = [own, ownx, own_ranks, b01a, b01b, ranks1, nxt, prva]
    state = kernel_call("left", functools.partial(half_kernel, 0), 1, state, [*kept, b13a])
    prvb, state = lax.optimization_barrier((prvb, state))
    state = kernel_call("right", functools.partial(half_kernel, 1), LONG, state, [*kept, b13b])
    prvbx = send("prvbx", prvb, core=1)
    state = kernel_call("cross", cross_kernel, 0, state, [b03, b13a, b13b, nxtax, nxtbx, cross])

    side = send("side", state[W10 : W10 + 8], col=1)
    state = kernel_call("prev", prev_kernel, 0, state, [b03, b10, b13a, b13b, cross, prvbx])
    swapped = send("swapped", state[KOWNX : KOWNX + 6], core=1)
    state = kernel_call("end", end_kernel, 1, state, [b03, b10, b13a, b13b, prvb])
    shapes = [(8, HALF), (4, HALF), (6, HALF), (8, HALF)]
    kept, to_03, to_01, to_prv = small_call("gather", gather_kernel, shapes, [state, swapped, side])
    back_prv = send("back_prv", to_prv, cluster=-1, row=1)
    back_01 = send("back_01", to_01, row=1)
    back_03 = send("back_03", to_03, row=-1)
    return tuple(small_call("final", final_kernel, [(1, rows)] * 2, [kept, back_03, back_01, back_prv]))


def solution(mesh):
    in_specs = (P("group", "helper", None), P(), P("group", "helper"))
    out_specs = (P("group", "helper"), P("group", "helper"))
    return jax.shard_map(
        on_device, mesh=mesh, in_specs=in_specs, out_specs=out_specs, check_vma=False
    )
```

```python
import functools
import math

import jax
import jax.numpy as jnp
from jax import lax
from jax.experimental import pallas as pl
from jax.experimental.pallas import tpu as pltpu
from jax.sharding import PartitionSpec as P

D = 1024
HALF = 256
EXTRA = 8
PAY = HALF + EXTRA
BASE = 64
FAR = 8192.0
LOW = -4.0
AXES = ("group", "helper")
VMEM = pl.BlockSpec(memory_space=pltpu.VMEM)
SMEM = pl.BlockSpec(memory_space=pltpu.SMEM)


def place(index):
    group, helper = divmod(index, 16)
    return {
        "part": group // 4,
        "z": group % 4,
        "row": helper // 4,
        "col": (helper // 2) % 2,
        "core": helper % 2,
    }


def number(at):
    return (at["part"] * 4 + at["z"]) * 16 + at["row"] * 4 + at["col"] * 2 + at["core"]


def pairs(col=0, row=0, core=0, cluster=0):
    out = []
    for source in range(128):
        at = place(source)
        step = at["part"] * 4 + at["z"] + cluster
        flip = 1 if step // 4 != at["part"] else 0
        at["part"], at["z"] = (step // 4) % 2, step % 4
        at["col"] = (at["col"] + col + flip) % 2
        at["row"] = (at["row"] + row) % 4
        at["core"] = (at["core"] + core) % 2
        out.append((source, number(at)))
    return out


def send(name, value, **shift):
    with jax.named_scope(name):
        return lax.ppermute(value, AXES, pairs(**shift))


def after(value, *others):
    return lax.optimization_barrier((value, *others))[0]


def inner(keys, queries):
    return lax.dot_general(
        keys, queries, (((1,), (1,)), ((), ())), preferred_element_type=jnp.float32
    )


PARTS = 4
PACK_MIB = 60
LONG = 10**8


def own_count(sizes_ref, step=0):
    return sizes_ref[lax.rem(lax.axis_index("group") + step, lax.axis_size("group"))]


def pack_kernel(sizes_hbm, rows_hbm, rank_hbm, pay_ref, a_ref, b_ref, rows_ref, rank_ref, sizes_ref, sem):
    part = 2 * HALF // PARTS
    copies = [
        pltpu.make_async_copy(rows_hbm.at[pl.ds(i * part, part)], rows_ref.at[pl.ds(i * part, part)], sem.at[i])
        for i in range(PARTS)
    ]
    rank_copy = pltpu.make_async_copy(rank_hbm, rank_ref, sem.at[PARTS])
    sizes_copy = pltpu.make_async_copy(sizes_hbm, sizes_ref, sem.at[PARTS + 1])
    for copy in [*copies, rank_copy, sizes_copy]:
        copy.start()
    for i, copy in enumerate(copies):
        copy.wait()
        half, at = divmod(i * part, HALF)
        rows = rows_ref[i * part : (i + 1) * part, :]
        scale = lax.rsqrt(jnp.mean(rows * rows, axis=-1, keepdims=True) + 1e-06) / math.sqrt(D)
        unit = (rows * scale).astype(jnp.bfloat16)
        pay_ref[half, at : at + part, :] = unit
        (a_ref, b_ref)[half][at : at + part, :] = unit
    rank_copy.wait()
    sizes_copy.wait()
    left = own_count(sizes_ref) - lax.axis_index("helper") * 2 * HALF
    for half, half_ref in enumerate((a_ref, b_ref)):
        rank = rank_ref[:, half * HALF : (half + 1) * HALF]
        position = lax.broadcasted_iota(jnp.int32, (1, HALF), 1) + half * HALF
        real = position < left
        high = jnp.where(real, rank // BASE, int(FAR) // BASE).astype(jnp.float32)
        low = jnp.where(real, rank % BASE, 0).astype(jnp.float32)
        both = jnp.concatenate([high, low, jnp.zeros((1, D - 2 * HALF), jnp.float32)], axis=1)
        tail = jnp.broadcast_to(both, (EXTRA, D)).astype(jnp.bfloat16)
        pay_ref[half, HALF:, :] = tail
        half_ref[HALF:, :] = tail


def packed(rows, ranks, sizes):
    half = jax.ShapeDtypeStruct((PAY, D), jnp.bfloat16)
    return pl.pallas_call(
        pack_kernel,
        in_specs=[pl.BlockSpec(memory_space=pltpu.HBM)] * 3,
        out_specs=[VMEM] * 3,
        out_shape=[jax.ShapeDtypeStruct((2, PAY, D), jnp.bfloat16), half, half],
        scratch_shapes=[
            pltpu.VMEM((2 * HALF, D), jnp.float32),
            pltpu.VMEM((1, 2 * HALF), jnp.int32),
            pltpu.SMEM(sizes.shape, jnp.int32),
            pltpu.SemaphoreType.DMA((PARTS + 2,)),
        ],
        name="pack",
        compiler_params=pltpu.CompilerParams(vmem_limit_bytes=PACK_MIB * 2**20),
        cost_estimate=pl.CostEstimate(flops=4 * 512 * D, bytes_accessed=4 * 2**20, transcendentals=512),
    )(sizes, rows, ranks)


def rank_row(tail):
    tail = tail[0:1, :].astype(jnp.float32)
    return tail[:, :HALF] * BASE + tail[:, HALF:]


def rank_column(tail):
    return jnp.transpose(jnp.broadcast_to(rank_row(tail), (128, HALF)))


def split(ref):
    return [ref.at[0], ref.at[1]]


def tops(scores):
    return jnp.max(scores.reshape(HALF // 8, 8, 128), axis=0)


def pieces(scores):
    return [scores[:, c : c + 128] for c in range(0, HALF, 128)]


def keep(row_ref, places, best):
    for at, value in zip(places, best):
        value = jnp.max(value, axis=0, keepdims=True)
        row_ref[at : at + 1, :] = jnp.maximum(row_ref[at : at + 1, :], value)


def lowest(queries):
    return [jnp.full((8, HALF), LOW, jnp.float32) for _ in queries]


ALL = lambda k, q: True
SHARE = {(0, 0), (1, 0), (1, 1), (2, 0), (2, 1), (3, 1)}


def pair_job(row_ref, ranks, keys, queries, q_at, k_at, wanted=ALL):
    q_rank = [rank_row(query[HALF:, : 2 * HALF]) for query in queries]
    best, sides = lowest(queries), []
    for n, key_ref in enumerate(keys):
        key, k_rank, side = key_ref[:HALF, :], ranks[n][...], None
        for i, query in enumerate(queries):
            if not wanted(n, i):
                continue
            parts = []
            for c, piece in enumerate(pieces(inner(key, query[:HALF, :]))):
                earlier = k_rank < q_rank[i][:, c * 128 : c * 128 + 128]
                parts.append(tops(jnp.where(earlier, piece, LOW)))
                if k_at is not None:
                    other = jnp.where(earlier, LOW, piece)
                    side = other if side is None else jnp.maximum(side, other)
            best[i] = jnp.maximum(best[i], jnp.concatenate(parts, axis=1))
        if side is not None:
            sides.append((k_at[n], side))
    keep(row_ref, q_at, best)
    for at, side in sides:
        keep(row_ref, [at], [jnp.transpose(side)])


def real_job(row_ref, limits, keys, queries, q_at):
    best = lowest(queries)
    position = lax.broadcasted_iota(jnp.int32, (HALF, 128), 0).astype(jnp.float32)
    for n, key_ref in enumerate(keys):
        key = key_ref[:HALF, :]
        real = position < row_ref[limits[n] : limits[n] + 1, :128]
        for i, query in enumerate(queries):
            parts = [tops(jnp.where(real, piece, LOW)) for piece in pieces(inner(key, query[:HALF, :]))]
            best[i] = jnp.maximum(best[i], jnp.concatenate(parts, axis=1))
    keep(row_ref, q_at, best)


def put_ranks(rank_ref, halves):
    for n, half in enumerate(halves):
        rank_ref[n] = rank_column(half[HALF:, : 2 * HALF])


def rank_shape(halves):
    return jax.ShapeDtypeStruct((halves, HALF, 128), jnp.float32)


def kernel_call(name, body, tasks, rows, arrays, extra_out=(), scalars=()):
    n = len(arrays) + len(scalars)

    def kernel(rows_in, *refs):
        row_ref = refs[n]
        row_ref[...] = rows_in[...]
        body(row_ref, *refs[:n], *refs[n + 1 :])

    out = pl.pallas_call(
        kernel,
        in_specs=[VMEM] * (1 + len(arrays)) + [SMEM] * len(scalars),
        out_specs=[VMEM] * (1 + len(extra_out)),
        out_shape=[jax.ShapeDtypeStruct((N_ROWS, HALF), jnp.float32), *extra_out],
        name=name,
        compiler_params=pltpu.CompilerParams(vmem_limit_bytes=14 * 2**20),
        cost_estimate=pl.CostEstimate(flops=int(tasks * 1024) if tasks == LONG else 0, bytes_accessed=0, transcendentals=0),
    )(rows, *arrays, *scalars)
    return out if extra_out else out[0]


W00, A00, KOWN, W03, A03, W10, A10 = 0, 2, 4, 6, 8, 10, 12
W13, A13, W01, A01, K01, PRV, KOWNX, K01X, PRVX = 14, 16, 18, 20, 22, 24, 26, 28, 30
REAL, FLOOR = 32, 34
L_NXT, L_NXTX, L_03, L_10, L_13 = 40, 42, 44, 46, 48
N_ROWS = 56


def both(at):
    return [at, at + 1]


def real_rows(sizes_ref, col, row, other=0, cluster=0):
    helper = lax.axis_index("helper")
    flip = jnp.where(lax.axis_index("group") % 4 == 3, cluster, 0)
    row = (helper // 4 + row) % 4
    col = (helper // 2 + col + flip) % 2
    start = own_count(sizes_ref, cluster) - (row * 4 + col * 2 + (helper + other) % 2) * 2 * HALF
    return [start, start - HALF]


def self_kernel(row_ref, own, ownx, sizes_ref, ranks):
    keys = split(own) + split(ownx)
    put_ranks(ranks, keys)
    row_ref[...] = jnp.full(row_ref.shape, LOW, jnp.float32)
    left = own_count(sizes_ref) - lax.axis_index("helper") * 2 * HALF
    for h in range(2):
        position = lax.broadcasted_iota(jnp.int32, (1, HALF), 1) + h * HALF
        row_ref[REAL + h : REAL + h + 1, :] = jnp.where(position < left, 1.0, 0.0)
    floor = jnp.where(own_count(sizes_ref, 1) < 2 * HALF * lax.axis_size("helper"), -1.0, LOW)
    row_ref[FLOOR : FLOOR + 1, :] = jnp.full((1, HALF), floor, jnp.float32)
    limits = [(L_NXT, real_rows(sizes_ref, 0, 0, 0, 1)), (L_NXTX, real_rows(sizes_ref, 0, 0, 1, 1))]
    limits += [(L_03, real_rows(sizes_ref, 0, -1)), (L_10, real_rows(sizes_ref, 1, 0)), (L_13, real_rows(sizes_ref, 1, -1))]
    for at, counts in limits:
        for h, count in enumerate(counts):
            row_ref[at + h : at + h + 1, :] = jnp.full((1, HALF), count, jnp.int32).astype(jnp.float32)
    pair_job(row_ref, [ranks.at[n] for n in range(4)], keys, split(own), both(W00), None)


def own_job(row_ref, own, ownx, ranks, queries, places, wanted=ALL):
    keys = split(own) + split(ownx)
    pair_job(row_ref, [ranks.at[n] for n in range(4)], keys, queries, places, both(KOWN) + both(KOWNX), wanted)


def first_kernel(row_ref, own, ownx, ranks, b01a):
    own_job(row_ref, own, ownx, ranks, [b01a], [W01])


def bundle_kernel(b01a, b01b, nxt, prva, bundle, nxta, nxtb):
    nxta[...] = nxt[0, :HALF, :]
    nxtb[...] = nxt[1, :HALF, :]
    for n, half in enumerate([b01a, b01b, prva]):
        bundle[n] = half[...]


def same_kernel(row_ref, own, ownx, own_ranks, b01a, b01b, b03, b10, nxt, prva, ranks):
    places = [W01 + 1, W10, W10 + 1]
    own_job(row_ref, own, ownx, own_ranks, [b01b, *split(b10)], places, lambda k, q: q == 0 or (k, q - 1) in SHARE)
    queries = [*split(own), b01a, b01b, *split(b03), *split(b10)]
    places = both(A00) + both(A01) + both(A03) + both(A10)
    real_job(row_ref, both(L_NXT), split(nxt), queries, places)
    put_ranks(ranks, [b01a, b01b])
    pair_job(
        row_ref, [ranks.at[0], ranks.at[1]], [b01a, b01b], split(b03), both(W03), both(K01),
        lambda k, q: (k, q) in SHARE,
    )
    limits = both(L_03) + both(L_10)
    real_job(row_ref, limits, split(b03) + split(b10), [prva], [PRV])


def half_kernel(h, row_ref, own, ownx, ranks, b01a, b01b, ranks1, nxt, prva, b13):
    own_job(row_ref, own, ownx, ranks, [b13], [W13 + h])
    pair_job(
        row_ref, [ranks1.at[0], ranks1.at[1]], [b01a, b01b], [b13], [W13 + h], both(K01), lambda k, q: (k, h) in SHARE
    )
    real_job(row_ref, both(L_NXT), split(nxt), [b13], [A13 + h])
    real_job(row_ref, [L_13 + h], [b13], [prva], [PRV])


def other_kernel(row_ref, own, b01a, b01b, b03, b10, nxtax, nxtbx):
    queries = [*split(own), b01a, b01b, *split(b03), *split(b10)]
    places = both(A00) + both(A01) + both(A03) + both(A10)
    real_job(row_ref, both(L_NXTX), [nxtax, nxtbx], queries, places)


def cross_kernel(row_ref, b03, b13a, b13b, nxtax, nxtbx, cross):
    b13 = [b13a, b13b]
    real_job(row_ref, both(L_NXTX), [nxtax, nxtbx], b13, both(A13))
    one = [cross.at[0], cross.at[1]]
    ranks = [rank_column(half[HALF:, : 2 * HALF]) for half in one]
    pair_job(
        row_ref, ranks, one, split(b03) + b13, both(W03) + both(W13), both(K01X),
        lambda k, q: (2 + k, q % 2) in SHARE,
    )


def prev_kernel(row_ref, b03, b10, b13a, b13b, cross, prvbx):
    limits = both(L_03) + both(L_10) + both(L_13)
    real_job(row_ref, limits, [*split(b03), *split(b10), b13a, b13b], [cross.at[2], prvbx], both(PRVX))


def end_kernel(row_ref, b03, b10, b13a, b13b, prvb):
    limits = both(L_13) + both(L_03) + both(L_10)
    real_job(row_ref, limits, [b13a, b13b, *split(b03), *split(b10)], [prvb], [PRV + 1])


def gather_kernel(rows_ref, swapped_ref, side_ref, kept_ref, to03_ref, to01_ref, prv_ref):
    within = jnp.maximum(rows_ref[W00 : W00 + 2, :], rows_ref[KOWN : KOWN + 2, :])
    within = jnp.maximum(within, jnp.maximum(swapped_ref[0:2, :], side_ref[0:2, :]))
    kept_ref[0:2, :] = jnp.maximum(within, -1.0)
    kept_ref[2:4, :] = jnp.maximum(jnp.maximum(rows_ref[A00 : A00 + 2, :], side_ref[2:4, :]), rows_ref[FLOOR : FLOOR + 1, :])
    kept_ref[4:6, :] = rows_ref[REAL : REAL + 2, :]
    kept_ref[6:8, :] = rows_ref[REAL : REAL + 2, :]
    to03_ref[...] = jnp.maximum(rows_ref[W03 : W03 + 4, :], side_ref[4:8, :])
    to01_ref[0:4, :] = rows_ref[W01 : W01 + 4, :]
    to01_ref[4:6, :] = jnp.maximum(rows_ref[K01 : K01 + 2, :], swapped_ref[2:4, :])
    prv_ref[0:2, :] = jnp.maximum(rows_ref[PRV : PRV + 2, :], swapped_ref[4:6, :])
    prv_ref[2:8, :] = rows_ref[0:6, :]


def final_kernel(kept, b03, b01, bprv, within_ref, adjacent_ref):
    for h in range(2):
        row = lambda ref, at: ref[at + h : at + h + 1, :]
        within = [row(kept, 0), row(b03, 0), row(b01, 0), row(b01, 4)]
        adjacent = [row(kept, 2), row(b03, 2), row(b01, 2), row(bprv, 0)]
        real = row(kept, 4) > 0
        place = slice(h * HALF, (h + 1) * HALF)
        within_ref[:, place] = jnp.where(real, functools.reduce(jnp.maximum, within), 0.0)
        adjacent_ref[:, place] = jnp.where(real, functools.reduce(jnp.maximum, adjacent), 0.0)


def small_call(name, body, shapes, arrays):
    return pl.pallas_call(
        body,
        in_specs=[VMEM] * len(arrays),
        out_specs=[VMEM] * len(shapes),
        out_shape=[jax.ShapeDtypeStruct(shape, jnp.float32) for shape in shapes],
        name=name,
        compiler_params=pltpu.CompilerParams(vmem_limit_bytes=2 * 2**20),
    )(*arrays)


def on_device(embeddings, sizes, ranks):
    rows = embeddings.shape[1]
    own, own_a, own_b = packed(embeddings[0], ranks, sizes)

    b01a = send("b01a", own_a, row=-1)
    b03 = send("b03", own, row=1)
    nxt = send("nxt", own, cluster=-1)
    b10 = send("b10", own, col=1)
    ownx = send("ownx", own, core=1)
    b01b = send("b01b", after(own_b, ownx), row=-1)
    empty = jnp.zeros((N_ROWS, HALF), jnp.float32)
    state, own_ranks = kernel_call("self", self_kernel, 1, empty, [own, ownx], [rank_shape(4)], [sizes])
    prva = send("prva", after(b01a, state), cluster=1)
    state = kernel_call("first", first_kernel, 0.5, state, [own, ownx, own_ranks, b01a])

    prvb = send("prvb", after(b01b, state), cluster=1)
    b03, b10, state = lax.optimization_barrier((b03, b10, state))
    nxt, b01b, prva, state = lax.optimization_barrier((nxt, b01b, prva, state))
    b13a = send("b13a", b03[0], col=1)
    b13b = send("b13b", b10[1], row=1)
    half = jax.ShapeDtypeStruct((HALF, D), jnp.bfloat16)
    bundle, nxta, nxtb = pl.pallas_call(
        bundle_kernel,
        in_specs=[VMEM] * 4,
        out_specs=[VMEM] * 3,
        out_shape=[jax.ShapeDtypeStruct((3, PAY, D), jnp.bfloat16), half, half],
        name="bundle",
        compiler_params=pltpu.CompilerParams(vmem_limit_bytes=8 * 2**20),
    )(b01a, b01b, nxt, prva)
    nxtax = send("nxtax", nxta, core=1)
    nxtbx = send("nxtbx", nxtb, core=1)
    state, ranks1 = kernel_call(
        "same", same_kernel, 4.5, state,
        [own, ownx, own_ranks, b01a, b01b, b03, b10, nxt, prva], [rank_shape(2)],
    )
    state = kernel_call("other", other_kernel, 0, state, [own, b01a, b01b, b03, b10, nxtax, nxtbx])
    cross = send("cross", after(bundle, state), core=1)
    kept = [own, ownx, own_ranks, b01a, b01b, ranks1, nxt, prva]
    state = kernel_call("left", functools.partial(half_kernel, 0), 1, state, [*kept, b13a])
    prvb, state = lax.optimization_barrier((prvb, state))
    state = kernel_call("right", functools.partial(half_kernel, 1), LONG, state, [*kept, b13b])
    prvbx = send("prvbx", prvb, core=1)
    state = kernel_call("cross", cross_kernel, 0, state, [b03, b13a, b13b, nxtax, nxtbx, cross])

    side = send("side", state[W10 : W10 + 8], col=1)
    state = kernel_call("prev", prev_kernel, 0, state, [b03, b10, b13a, b13b, cross, prvbx])
    swapped = send("swapped", state[KOWNX : KOWNX + 6], core=1)
    state = kernel_call("end", end_kernel, 1, state, [b03, b10, b13a, b13b, prvb])
    shapes = [(8, HALF), (4, HALF), (6, HALF), (8, HALF)]
    kept, to_03, to_01, to_prv = small_call("gather", gather_kernel, shapes, [state, swapped, side])
    back_prv = send("back_prv", to_prv, cluster=-1, row=1)
    back_01 = send("back_01", to_01, row=1)
    back_03 = send("back_03", to_03, row=-1)
    return tuple(small_call("final", final_kernel, [(1, rows)] * 2, [kept, back_03, back_01, back_prv]))


def solution(mesh):
    in_specs = (P("group", "helper", None), P(), P("group", "helper"))
    out_specs = (P("group", "helper"), P("group", "helper"))
    return jax.shard_map(
        on_device, mesh=mesh, in_specs=in_specs, out_specs=out_specs, check_vma=False
    )
```

```python
import functools
import math

import jax
import jax.numpy as jnp
from jax import lax
from jax.experimental import pallas as pl
from jax.experimental.pallas import tpu as pltpu
from jax.sharding import PartitionSpec as P

D = 1024
HALF = 256
EXTRA = 8
PAY = HALF + EXTRA
BASE = 64
FAR = 8192.0
LOW = -4.0
AXES = ("group", "helper")
VMEM = pl.BlockSpec(memory_space=pltpu.VMEM)
SMEM = pl.BlockSpec(memory_space=pltpu.SMEM)


def place(index):
    group, helper = divmod(index, 16)
    return {
        "part": group // 4,
        "z": group % 4,
        "row": helper // 4,
        "col": (helper // 2) % 2,
        "core": helper % 2,
    }


def number(at):
    return (at["part"] * 4 + at["z"]) * 16 + at["row"] * 4 + at["col"] * 2 + at["core"]


def pairs(col=0, row=0, core=0, cluster=0):
    out = []
    for source in range(128):
        at = place(source)
        step = at["part"] * 4 + at["z"] + cluster
        flip = 1 if step // 4 != at["part"] else 0
        at["part"], at["z"] = (step // 4) % 2, step % 4
        at["col"] = (at["col"] + col + flip) % 2
        at["row"] = (at["row"] + row) % 4
        at["core"] = (at["core"] + core) % 2
        out.append((source, number(at)))
    return out


def send(name, value, **shift):
    with jax.named_scope(name):
        return lax.ppermute(value, AXES, pairs(**shift))


def after(value, *others):
    return lax.optimization_barrier((value, *others))[0]


def inner(keys, queries):
    return lax.dot_general(
        keys, queries, (((1,), (1,)), ((), ())), preferred_element_type=jnp.float32
    )


PARTS = 4
PACK_MIB = 60
LONG = 10**8


def own_count(sizes_ref, step=0):
    return sizes_ref[lax.rem(lax.axis_index("group") + step, lax.axis_size("group"))]


def pack_kernel(sizes_hbm, rows_hbm, rank_hbm, pay_ref, a_ref, b_ref, rows_ref, rank_ref, sizes_ref, sem):
    part = 2 * HALF // PARTS
    copies = [
        pltpu.make_async_copy(rows_hbm.at[pl.ds(i * part, part)], rows_ref.at[pl.ds(i * part, part)], sem.at[i])
        for i in range(PARTS)
    ]
    rank_copy = pltpu.make_async_copy(rank_hbm, rank_ref, sem.at[PARTS])
    sizes_copy = pltpu.make_async_copy(sizes_hbm, sizes_ref, sem.at[PARTS + 1])
    for copy in [*copies, rank_copy, sizes_copy]:
        copy.start()
    for i, copy in enumerate(copies):
        copy.wait()
        half, at = divmod(i * part, HALF)
        rows = rows_ref[i * part : (i + 1) * part, :]
        scale = lax.rsqrt(jnp.mean(rows * rows, axis=-1, keepdims=True) + 1e-06) / math.sqrt(D)
        unit = (rows * scale).astype(jnp.bfloat16)
        pay_ref[half, at : at + part, :] = unit
        (a_ref, b_ref)[half][at : at + part, :] = unit
    rank_copy.wait()
    sizes_copy.wait()
    left = own_count(sizes_ref) - lax.axis_index("helper") * 2 * HALF
    for half, half_ref in enumerate((a_ref, b_ref)):
        rank = rank_ref[:, half * HALF : (half + 1) * HALF]
        position = lax.broadcasted_iota(jnp.int32, (1, HALF), 1) + half * HALF
        real = position < left
        high = jnp.where(real, rank // BASE, int(FAR) // BASE).astype(jnp.float32)
        low = jnp.where(real, rank % BASE, 0).astype(jnp.float32)
        both = jnp.concatenate([high, low, jnp.zeros((1, D - 2 * HALF), jnp.float32)], axis=1)
        tail = jnp.broadcast_to(both, (EXTRA, D)).astype(jnp.bfloat16)
        pay_ref[half, HALF:, :] = tail
        half_ref[HALF:, :] = tail


def packed(rows, ranks, sizes):
    half = jax.ShapeDtypeStruct((PAY, D), jnp.bfloat16)
    return pl.pallas_call(
        pack_kernel,
        in_specs=[pl.BlockSpec(memory_space=pltpu.HBM)] * 3,
        out_specs=[VMEM] * 3,
        out_shape=[jax.ShapeDtypeStruct((2, PAY, D), jnp.bfloat16), half, half],
        scratch_shapes=[
            pltpu.VMEM((2 * HALF, D), jnp.float32),
            pltpu.VMEM((1, 2 * HALF), jnp.int32),
            pltpu.SMEM(sizes.shape, jnp.int32),
            pltpu.SemaphoreType.DMA((PARTS + 2,)),
        ],
        name="pack",
        compiler_params=pltpu.CompilerParams(vmem_limit_bytes=PACK_MIB * 2**20),
        cost_estimate=pl.CostEstimate(flops=4 * 512 * D, bytes_accessed=4 * 2**20, transcendentals=512),
    )(sizes, rows, ranks)


def rank_row(tail):
    tail = tail[0:1, :].astype(jnp.float32)
    return tail[:, :HALF] * BASE + tail[:, HALF:]


def rank_column(tail):
    return jnp.transpose(jnp.broadcast_to(rank_row(tail), (128, HALF)))


def split(ref):
    return [ref.at[0], ref.at[1]]


def tops(scores):
    return jnp.max(scores.reshape(HALF // 8, 8, 128), axis=0)


def pieces(scores):
    return [scores[:, c : c + 128] for c in range(0, HALF, 128)]


def keep(row_ref, places, best):
    for at, value in zip(places, best):
        value = jnp.max(value, axis=0, keepdims=True)
        row_ref[at : at + 1, :] = jnp.maximum(row_ref[at : at + 1, :], value)


def lowest(queries):
    return [jnp.full((8, HALF), LOW, jnp.float32) for _ in queries]


ALL = lambda k, q: True
SHARE = {(0, 0), (1, 0), (1, 1), (2, 0), (2, 1), (3, 1)}


def pair_job(row_ref, ranks, keys, queries, q_at, k_at, wanted=ALL):
    q_rank = [rank_row(query[HALF:, : 2 * HALF]) for query in queries]
    best, sides = lowest(queries), []
    for n, key_ref in enumerate(keys):
        key, k_rank, side = key_ref[:HALF, :], ranks[n][...], None
        for i, query in enumerate(queries):
            if not wanted(n, i):
                continue
            parts = []
            for c, piece in enumerate(pieces(inner(key, query[:HALF, :]))):
                earlier = k_rank < q_rank[i][:, c * 128 : c * 128 + 128]
                parts.append(tops(jnp.where(earlier, piece, LOW)))
                if k_at is not None:
                    other = jnp.where(earlier, LOW, piece)
                    side = other if side is None else jnp.maximum(side, other)
            best[i] = jnp.maximum(best[i], jnp.concatenate(parts, axis=1))
        if side is not None:
            sides.append((k_at[n], side))
    keep(row_ref, q_at, best)
    for at, side in sides:
        keep(row_ref, [at], [jnp.transpose(side)])


def real_job(row_ref, limits, keys, queries, q_at):
    best = lowest(queries)
    position = lax.broadcasted_iota(jnp.int32, (HALF, 128), 0).astype(jnp.float32)
    for n, key_ref in enumerate(keys):
        key = key_ref[:HALF, :]
        real = position < row_ref[limits[n] : limits[n] + 1, :128]
        for i, query in enumerate(queries):
            parts = [tops(jnp.where(real, piece, LOW)) for piece in pieces(inner(key, query[:HALF, :]))]
            best[i] = jnp.maximum(best[i], jnp.concatenate(parts, axis=1))
    keep(row_ref, q_at, best)


def put_ranks(rank_ref, halves):
    for n, half in enumerate(halves):
        rank_ref[n] = rank_column(half[HALF:, : 2 * HALF])


def rank_shape(halves):
    return jax.ShapeDtypeStruct((halves, HALF, 128), jnp.float32)


def kernel_call(name, body, tasks, rows, arrays, extra_out=(), scalars=()):
    n = len(arrays) + len(scalars)

    def kernel(rows_in, *refs):
        row_ref = refs[n]
        row_ref[...] = rows_in[...]
        body(row_ref, *refs[:n], *refs[n + 1 :])

    out = pl.pallas_call(
        kernel,
        in_specs=[VMEM] * (1 + len(arrays)) + [SMEM] * len(scalars),
        out_specs=[VMEM] * (1 + len(extra_out)),
        out_shape=[jax.ShapeDtypeStruct((N_ROWS, HALF), jnp.float32), *extra_out],
        name=name,
        compiler_params=pltpu.CompilerParams(vmem_limit_bytes=14 * 2**20),
        cost_estimate=pl.CostEstimate(flops=int(tasks * 1024) if tasks == LONG else 0, bytes_accessed=0, transcendentals=0),
    )(rows, *arrays, *scalars)
    return out if extra_out else out[0]


W00, A00, KOWN, W03, A03, W10, A10 = 0, 2, 4, 6, 8, 10, 12
W13, A13, W01, A01, K01, PRV, KOWNX, K01X, PRVX = 14, 16, 18, 20, 22, 24, 26, 28, 30
REAL, FLOOR = 32, 34
L_NXT, L_NXTX, L_03, L_10, L_13 = 40, 42, 44, 46, 48
N_ROWS = 56


def both(at):
    return [at, at + 1]


def real_rows(sizes_ref, col, row, other=0, cluster=0):
    helper = lax.axis_index("helper")
    flip = jnp.where(lax.axis_index("group") % 4 == 3, cluster, 0)
    row = (helper // 4 + row) % 4
    col = (helper // 2 + col + flip) % 2
    start = own_count(sizes_ref, cluster) - (row * 4 + col * 2 + (helper + other) % 2) * 2 * HALF
    return [start, start - HALF]


def self_kernel(row_ref, own, ownx, sizes_ref, ranks):
    keys = split(own) + split(ownx)
    put_ranks(ranks, keys)
    row_ref[...] = jnp.full(row_ref.shape, LOW, jnp.float32)
    left = own_count(sizes_ref) - lax.axis_index("helper") * 2 * HALF
    for h in range(2):
        position = lax.broadcasted_iota(jnp.int32, (1, HALF), 1) + h * HALF
        row_ref[REAL + h : REAL + h + 1, :] = jnp.where(position < left, 1.0, 0.0)
    floor = jnp.where(own_count(sizes_ref, 1) < 2 * HALF * lax.axis_size("helper"), -1.0, LOW)
    row_ref[FLOOR : FLOOR + 1, :] = jnp.full((1, HALF), floor, jnp.float32)
    limits = [(L_NXT, real_rows(sizes_ref, 0, 0, 0, 1)), (L_NXTX, real_rows(sizes_ref, 0, 0, 1, 1))]
    limits += [(L_03, real_rows(sizes_ref, 0, -1)), (L_10, real_rows(sizes_ref, 1, 0)), (L_13, real_rows(sizes_ref, 1, -1))]
    for at, counts in limits:
        for h, count in enumerate(counts):
            row_ref[at + h : at + h + 1, :] = jnp.full((1, HALF), count, jnp.int32).astype(jnp.float32)
    pair_job(row_ref, [ranks.at[n] for n in range(4)], keys, split(own), both(W00), None)


def own_job(row_ref, own, ownx, ranks, queries, places, wanted=ALL):
    keys = split(own) + split(ownx)
    pair_job(row_ref, [ranks.at[n] for n in range(4)], keys, queries, places, both(KOWN) + both(KOWNX), wanted)


def first_kernel(row_ref, own, ownx, ranks, b01a):
    own_job(row_ref, own, ownx, ranks, [b01a], [W01])


def bundle_kernel(b01a, b01b, nxt, prva, bundle, nxta, nxtb):
    nxta[...] = nxt[0, :HALF, :]
    nxtb[...] = nxt[1, :HALF, :]
    for n, half in enumerate([b01a, b01b, prva]):
        bundle[n] = half[...]


def same_kernel(row_ref, own, ownx, own_ranks, b01a, b01b, b03, b10, nxt, prva, ranks):
    places = [W01 + 1, W10, W10 + 1]
    own_job(row_ref, own, ownx, own_ranks, [b01b, *split(b10)], places, lambda k, q: q == 0 or (k, q - 1) in SHARE)
    queries = [*split(own), b01a, b01b, *split(b03), *split(b10)]
    places = both(A00) + both(A01) + both(A03) + both(A10)
    real_job(row_ref, both(L_NXT), split(nxt), queries, places)
    put_ranks(ranks, [b01a, b01b])
    pair_job(
        row_ref, [ranks.at[0], ranks.at[1]], [b01a, b01b], split(b03), both(W03), both(K01),
        lambda k, q: (k, q) in SHARE,
    )
    limits = both(L_03) + both(L_10)
    real_job(row_ref, limits, split(b03) + split(b10), [prva], [PRV])


def half_kernel(h, row_ref, own, ownx, ranks, b01a, b01b, ranks1, nxt, prva, b13):
    own_job(row_ref, own, ownx, ranks, [b13], [W13 + h])
    pair_job(
        row_ref, [ranks1.at[0], ranks1.at[1]], [b01a, b01b], [b13], [W13 + h], both(K01), lambda k, q: (k, h) in SHARE
    )
    real_job(row_ref, both(L_NXT), split(nxt), [b13], [A13 + h])
    real_job(row_ref, [L_13 + h], [b13], [prva], [PRV])


def other_kernel(row_ref, own, b01a, b01b, b03, b10, nxtax, nxtbx):
    queries = [*split(own), b01a, b01b, *split(b03), *split(b10)]
    places = both(A00) + both(A01) + both(A03) + both(A10)
    real_job(row_ref, both(L_NXTX), [nxtax, nxtbx], queries, places)


def cross_kernel(row_ref, b03, b13a, b13b, nxtax, nxtbx, cross):
    b13 = [b13a, b13b]
    real_job(row_ref, both(L_NXTX), [nxtax, nxtbx], b13, both(A13))
    one = [cross.at[0], cross.at[1]]
    ranks = [rank_column(half[HALF:, : 2 * HALF]) for half in one]
    pair_job(
        row_ref, ranks, one, split(b03) + b13, both(W03) + both(W13), both(K01X),
        lambda k, q: (2 + k, q % 2) in SHARE,
    )


def prev_kernel(row_ref, b03, b10, b13a, b13b, cross, prvbx):
    limits = both(L_03) + both(L_10) + both(L_13)
    real_job(row_ref, limits, [*split(b03), *split(b10), b13a, b13b], [cross.at[2], prvbx], both(PRVX))


def end_kernel(row_ref, b03, b10, b13a, b13b, prvb):
    limits = both(L_13) + both(L_03) + both(L_10)
    real_job(row_ref, limits, [b13a, b13b, *split(b03), *split(b10)], [prvb], [PRV + 1])


def gather_kernel(rows_ref, swapped_ref, side_ref, kept_ref, to03_ref, to01_ref, prv_ref):
    within = jnp.maximum(rows_ref[W00 : W00 + 2, :], rows_ref[KOWN : KOWN + 2, :])
    within = jnp.maximum(within, jnp.maximum(swapped_ref[0:2, :], side_ref[0:2, :]))
    kept_ref[0:2, :] = jnp.maximum(within, -1.0)
    kept_ref[2:4, :] = jnp.maximum(jnp.maximum(rows_ref[A00 : A00 + 2, :], side_ref[2:4, :]), rows_ref[FLOOR : FLOOR + 1, :])
    kept_ref[4:6, :] = rows_ref[REAL : REAL + 2, :]
    kept_ref[6:8, :] = rows_ref[REAL : REAL + 2, :]
    to03_ref[...] = jnp.maximum(rows_ref[W03 : W03 + 4, :], side_ref[4:8, :])
    to01_ref[0:4, :] = rows_ref[W01 : W01 + 4, :]
    to01_ref[4:6, :] = jnp.maximum(rows_ref[K01 : K01 + 2, :], swapped_ref[2:4, :])
    prv_ref[0:2, :] = jnp.maximum(rows_ref[PRV : PRV + 2, :], swapped_ref[4:6, :])
    prv_ref[2:8, :] = rows_ref[0:6, :]


def final_kernel(kept, b03, b01, bprv, within_ref, adjacent_ref):
    for h in range(2):
        row = lambda ref, at: ref[at + h : at + h + 1, :]
        within = [row(kept, 0), row(b03, 0), row(b01, 0), row(b01, 4)]
        adjacent = [row(kept, 2), row(b03, 2), row(b01, 2), row(bprv, 0)]
        real = row(kept, 4) > 0
        place = slice(h * HALF, (h + 1) * HALF)
        within_ref[:, place] = jnp.where(real, functools.reduce(jnp.maximum, within), 0.0)
        adjacent_ref[:, place] = jnp.where(real, functools.reduce(jnp.maximum, adjacent), 0.0)


def small_call(name, body, shapes, arrays):
    return pl.pallas_call(
        body,
        in_specs=[VMEM] * len(arrays),
        out_specs=[VMEM] * len(shapes),
        out_shape=[jax.ShapeDtypeStruct(shape, jnp.float32) for shape in shapes],
        name=name,
        compiler_params=pltpu.CompilerParams(vmem_limit_bytes=2 * 2**20),
    )(*arrays)


def on_device(embeddings, sizes, ranks):
    rows = embeddings.shape[1]
    own, own_a, own_b = packed(embeddings[0], ranks, sizes)

    b01a = send("b01a", own_a, row=-1)
    b03 = send("b03", own, row=1)
    nxt = send("nxt", own, cluster=-1)
    b10 = send("b10", own, col=1)
    ownx = send("ownx", own, core=1)
    b01b = send("b01b", after(own_b, ownx), row=-1)
    empty = jnp.zeros((N_ROWS, HALF), jnp.float32)
    state, own_ranks = kernel_call("self", self_kernel, 1, empty, [own, ownx], [rank_shape(4)], [sizes])
    prva = send("prva", after(b01a, state), cluster=1)
    state = kernel_call("first", first_kernel, 0.5, state, [own, ownx, own_ranks, b01a])

    prvb = send("prvb", after(b01b, state), cluster=1)
    b03, b10, state = lax.optimization_barrier((b03, b10, state))
    nxt, b01b, prva, state = lax.optimization_barrier((nxt, b01b, prva, state))
    b13a = send("b13a", b03[0], col=1)
    b13b = send("b13b", b10[1], row=1)
    half = jax.ShapeDtypeStruct((HALF, D), jnp.bfloat16)
    bundle, nxta, nxtb = pl.pallas_call(
        bundle_kernel,
        in_specs=[VMEM] * 4,
        out_specs=[VMEM] * 3,
        out_shape=[jax.ShapeDtypeStruct((3, PAY, D), jnp.bfloat16), half, half],
        name="bundle",
        compiler_params=pltpu.CompilerParams(vmem_limit_bytes=8 * 2**20),
    )(b01a, b01b, nxt, prva)
    nxtax = send("nxtax", nxta, core=1)
    nxtbx = send("nxtbx", nxtb, core=1)
    state, ranks1 = kernel_call(
        "same", same_kernel, 4.5, state,
        [own, ownx, own_ranks, b01a, b01b, b03, b10, nxt, prva], [rank_shape(2)],
    )
    state = kernel_call("other", other_kernel, 0, state, [own, b01a, b01b, b03, b10, nxtax, nxtbx])
    cross = send("cross", after(bundle, state), core=1)
    kept = [own, ownx, own_ranks, b01a, b01b, ranks1, nxt, prva]
    state = kernel_call("left", functools.partial(half_kernel, 1), 1, state, [*kept, b13b])
    prvb, state = lax.optimization_barrier((prvb, state))
    state = kernel_call("right", functools.partial(half_kernel, 0), LONG, state, [*kept, b13a])
    prvbx = send("prvbx", prvb, core=1)
    state = kernel_call("cross", cross_kernel, 0, state, [b03, b13a, b13b, nxtax, nxtbx, cross])

    side = send("side", state[W10 : W10 + 8], col=1)
    state = kernel_call("prev", prev_kernel, 0, state, [b03, b10, b13a, b13b, cross, prvbx])
    swapped = send("swapped", state[KOWNX : KOWNX + 6], core=1)
    state = kernel_call("end", end_kernel, 1, state, [b03, b10, b13a, b13b, prvb])
    shapes = [(8, HALF), (4, HALF), (6, HALF), (8, HALF)]
    kept, to_03, to_01, to_prv = small_call("gather", gather_kernel, shapes, [state, swapped, side])
    back_prv = send("back_prv", to_prv, cluster=-1, row=1)
    back_01 = send("back_01", to_01, row=1)
    back_03 = send("back_03", to_03, row=-1)
    return tuple(small_call("final", final_kernel, [(1, rows)] * 2, [kept, back_03, back_01, back_prv]))


def solution(mesh):
    in_specs = (P("group", "helper", None), P(), P("group", "helper"))
    out_specs = (P("group", "helper"), P("group", "helper"))
    return jax.shard_map(
        on_device, mesh=mesh, in_specs=in_specs, out_specs=out_specs, check_vma=False
    )
```

```python
import functools
import math

import jax
import jax.numpy as jnp
from jax import lax
from jax.experimental import pallas as pl
from jax.experimental.pallas import tpu as pltpu
from jax.sharding import PartitionSpec as P

D = 1024
HALF = 256
EXTRA = 8
PAY = HALF + EXTRA
BASE = 64
FAR = 8192.0
LOW = -4.0
AXES = ("group", "helper")
VMEM = pl.BlockSpec(memory_space=pltpu.VMEM)
SMEM = pl.BlockSpec(memory_space=pltpu.SMEM)


def place(index):
    group, helper = divmod(index, 16)
    return {
        "part": group // 4,
        "z": group % 4,
        "row": helper // 4,
        "col": (helper // 2) % 2,
        "core": helper % 2,
    }


def number(at):
    return (at["part"] * 4 + at["z"]) * 16 + at["row"] * 4 + at["col"] * 2 + at["core"]


def pairs(col=0, row=0, core=0, cluster=0):
    out = []
    for source in range(128):
        at = place(source)
        step = at["part"] * 4 + at["z"] + cluster
        flip = 1 if step // 4 != at["part"] else 0
        at["part"], at["z"] = (step // 4) % 2, step % 4
        at["col"] = (at["col"] + col + flip) % 2
        at["row"] = (at["row"] + row) % 4
        at["core"] = (at["core"] + core) % 2
        out.append((source, number(at)))
    return out


def send(name, value, **shift):
    with jax.named_scope(name):
        return lax.ppermute(value, AXES, pairs(**shift))


def after(value, *others):
    return lax.optimization_barrier((value, *others))[0]


def inner(keys, queries):
    return lax.dot_general(
        keys, queries, (((1,), (1,)), ((), ())), preferred_element_type=jnp.float32
    )


PARTS = 4
PACK_MIB = 60
LONG = 10**8


def own_count(sizes_ref, step=0):
    return sizes_ref[lax.rem(lax.axis_index("group") + step, lax.axis_size("group"))]


def pack_kernel(sizes_hbm, rows_hbm, rank_hbm, pay_ref, a_ref, b_ref, rows_ref, rank_ref, sizes_ref, sem):
    part = 2 * HALF // PARTS
    copies = [
        pltpu.make_async_copy(rows_hbm.at[pl.ds(i * part, part)], rows_ref.at[pl.ds(i * part, part)], sem.at[i])
        for i in range(PARTS)
    ]
    rank_copy = pltpu.make_async_copy(rank_hbm, rank_ref, sem.at[PARTS])
    sizes_copy = pltpu.make_async_copy(sizes_hbm, sizes_ref, sem.at[PARTS + 1])
    for copy in [*copies, rank_copy, sizes_copy]:
        copy.start()
    for i, copy in enumerate(copies):
        copy.wait()
        half, at = divmod(i * part, HALF)
        rows = rows_ref[i * part : (i + 1) * part, :]
        scale = lax.rsqrt(jnp.mean(rows * rows, axis=-1, keepdims=True) + 1e-06) / math.sqrt(D)
        unit = (rows * scale).astype(jnp.bfloat16)
        pay_ref[half, at : at + part, :] = unit
        (a_ref, b_ref)[half][at : at + part, :] = unit
    rank_copy.wait()
    sizes_copy.wait()
    left = own_count(sizes_ref) - lax.axis_index("helper") * 2 * HALF
    for half, half_ref in enumerate((a_ref, b_ref)):
        rank = rank_ref[:, half * HALF : (half + 1) * HALF]
        position = lax.broadcasted_iota(jnp.int32, (1, HALF), 1) + half * HALF
        real = position < left
        high = jnp.where(real, rank // BASE, int(FAR) // BASE).astype(jnp.float32)
        low = jnp.where(real, rank % BASE, 0).astype(jnp.float32)
        both = jnp.concatenate([high, low, jnp.zeros((1, D - 2 * HALF), jnp.float32)], axis=1)
        tail = jnp.broadcast_to(both, (EXTRA, D)).astype(jnp.bfloat16)
        pay_ref[half, HALF:, :] = tail
        half_ref[HALF:, :] = tail


def packed(rows, ranks, sizes):
    half = jax.ShapeDtypeStruct((PAY, D), jnp.bfloat16)
    return pl.pallas_call(
        pack_kernel,
        in_specs=[pl.BlockSpec(memory_space=pltpu.HBM)] * 3,
        out_specs=[VMEM] * 3,
        out_shape=[jax.ShapeDtypeStruct((2, PAY, D), jnp.bfloat16), half, half],
        scratch_shapes=[
            pltpu.VMEM((2 * HALF, D), jnp.float32),
            pltpu.VMEM((1, 2 * HALF), jnp.int32),
            pltpu.SMEM(sizes.shape, jnp.int32),
            pltpu.SemaphoreType.DMA((PARTS + 2,)),
        ],
        name="pack",
        compiler_params=pltpu.CompilerParams(vmem_limit_bytes=PACK_MIB * 2**20),
        cost_estimate=pl.CostEstimate(flops=4 * 512 * D, bytes_accessed=4 * 2**20, transcendentals=512),
    )(sizes, rows, ranks)


def rank_row(tail):
    tail = tail[0:1, :].astype(jnp.float32)
    return tail[:, :HALF] * BASE + tail[:, HALF:]


def rank_column(tail):
    return jnp.transpose(jnp.broadcast_to(rank_row(tail), (128, HALF)))


def split(ref):
    return [ref.at[0], ref.at[1]]


def tops(scores):
    return jnp.max(scores.reshape(HALF // 8, 8, 128), axis=0)


def pieces(scores):
    return [scores[:, c : c + 128] for c in range(0, HALF, 128)]


def keep(row_ref, places, best):
    for at, value in zip(places, best):
        value = jnp.max(value, axis=0, keepdims=True)
        row_ref[at : at + 1, :] = jnp.maximum(row_ref[at : at + 1, :], value)


def lowest(queries):
    return [jnp.full((8, HALF), LOW, jnp.float32) for _ in queries]


ALL = lambda k, q: True
SHARE = {(0, 0), (1, 0), (1, 1), (2, 0), (2, 1), (3, 1)}


def pair_job(row_ref, ranks, keys, queries, q_at, k_at, wanted=ALL):
    q_rank = [rank_row(query[HALF:, : 2 * HALF]) for query in queries]
    best, sides = lowest(queries), []
    for n, key_ref in enumerate(keys):
        key, k_rank, side = key_ref[:HALF, :], ranks[n][...], None
        for i, query in enumerate(queries):
            if not wanted(n, i):
                continue
            parts = []
            for c, piece in enumerate(pieces(inner(key, query[:HALF, :]))):
                earlier = k_rank < q_rank[i][:, c * 128 : c * 128 + 128]
                parts.append(tops(jnp.where(earlier, piece, LOW)))
                if k_at is not None:
                    other = jnp.where(earlier, LOW, piece)
                    side = other if side is None else jnp.maximum(side, other)
            best[i] = jnp.maximum(best[i], jnp.concatenate(parts, axis=1))
        if side is not None:
            sides.append((k_at[n], side))
    keep(row_ref, q_at, best)
    for at, side in sides:
        keep(row_ref, [at], [jnp.transpose(side)])


def real_job(row_ref, limits, keys, queries, q_at):
    best = lowest(queries)
    position = lax.broadcasted_iota(jnp.int32, (HALF, 128), 0).astype(jnp.float32)
    for n, key_ref in enumerate(keys):
        key = key_ref[:HALF, :]
        real = position < row_ref[limits[n] : limits[n] + 1, :128]
        for i, query in enumerate(queries):
            parts = [tops(jnp.where(real, piece, LOW)) for piece in pieces(inner(key, query[:HALF, :]))]
            best[i] = jnp.maximum(best[i], jnp.concatenate(parts, axis=1))
    keep(row_ref, q_at, best)


def put_ranks(rank_ref, halves):
    for n, half in enumerate(halves):
        rank_ref[n] = rank_column(half[HALF:, : 2 * HALF])


def rank_shape(halves):
    return jax.ShapeDtypeStruct((halves, HALF, 128), jnp.float32)


def kernel_call(name, body, tasks, rows, arrays, extra_out=(), scalars=()):
    n = len(arrays) + len(scalars)

    def kernel(rows_in, *refs):
        row_ref = refs[n]
        row_ref[...] = rows_in[...]
        body(row_ref, *refs[:n], *refs[n + 1 :])

    out = pl.pallas_call(
        kernel,
        in_specs=[VMEM] * (1 + len(arrays)) + [SMEM] * len(scalars),
        out_specs=[VMEM] * (1 + len(extra_out)),
        out_shape=[jax.ShapeDtypeStruct((N_ROWS, HALF), jnp.float32), *extra_out],
        name=name,
        compiler_params=pltpu.CompilerParams(vmem_limit_bytes=14 * 2**20),
        cost_estimate=pl.CostEstimate(flops=int(tasks * 1024) if tasks == LONG else 0, bytes_accessed=0, transcendentals=0),
    )(rows, *arrays, *scalars)
    return out if extra_out else out[0]


W00, A00, KOWN, W03, A03, W10, A10 = 0, 2, 4, 6, 8, 10, 12
W13, A13, W01, A01, K01, PRV, KOWNX, K01X, PRVX = 14, 16, 18, 20, 22, 24, 26, 28, 30
REAL, FLOOR = 32, 34
L_NXT, L_NXTX, L_03, L_10, L_13 = 40, 42, 44, 46, 48
N_ROWS = 56


def both(at):
    return [at, at + 1]


def real_rows(sizes_ref, col, row, other=0, cluster=0):
    helper = lax.axis_index("helper")
    flip = jnp.where(lax.axis_index("group") % 4 == 3, cluster, 0)
    row = (helper // 4 + row) % 4
    col = (helper // 2 + col + flip) % 2
    start = own_count(sizes_ref, cluster) - (row * 4 + col * 2 + (helper + other) % 2) * 2 * HALF
    return [start, start - HALF]


def self_kernel(row_ref, own, ownx, sizes_ref, ranks):
    keys = split(own) + split(ownx)
    put_ranks(ranks, keys)
    row_ref[...] = jnp.full(row_ref.shape, LOW, jnp.float32)
    left = own_count(sizes_ref) - lax.axis_index("helper") * 2 * HALF
    for h in range(2):
        position = lax.broadcasted_iota(jnp.int32, (1, HALF), 1) + h * HALF
        row_ref[REAL + h : REAL + h + 1, :] = jnp.where(position < left, 1.0, 0.0)
    floor = jnp.where(own_count(sizes_ref, 1) < 2 * HALF * lax.axis_size("helper"), -1.0, LOW)
    row_ref[FLOOR : FLOOR + 1, :] = jnp.full((1, HALF), floor, jnp.float32)
    limits = [(L_NXT, real_rows(sizes_ref, 0, 0, 0, 1)), (L_NXTX, real_rows(sizes_ref, 0, 0, 1, 1))]
    limits += [(L_03, real_rows(sizes_ref, 0, -1)), (L_10, real_rows(sizes_ref, 1, 0)), (L_13, real_rows(sizes_ref, 1, -1))]
    for at, counts in limits:
        for h, count in enumerate(counts):
            row_ref[at + h : at + h + 1, :] = jnp.full((1, HALF), count, jnp.int32).astype(jnp.float32)
    pair_job(row_ref, [ranks.at[n] for n in range(4)], keys, split(own), both(W00), None)


def own_job(row_ref, own, ownx, ranks, queries, places, wanted=ALL):
    keys = split(own) + split(ownx)
    pair_job(row_ref, [ranks.at[n] for n in range(4)], keys, queries, places, both(KOWN) + both(KOWNX), wanted)


def first_kernel(row_ref, own, ownx, ranks, b01a):
    own_job(row_ref, own, ownx, ranks, [b01a], [W01])


def bundle_kernel(b01a, b01b, nxt, prva, bundle, nxta, nxtb):
    nxta[...] = nxt[0, :HALF, :]
    nxtb[...] = nxt[1, :HALF, :]
    for n, half in enumerate([b01a, b01b, prva]):
        bundle[n] = half[...]


def same_kernel(row_ref, own, ownx, own_ranks, b01a, b01b, b03, b10, nxt, prva, ranks):
    places = [W01 + 1, W10, W10 + 1]
    own_job(row_ref, own, ownx, own_ranks, [b01b, *split(b10)], places, lambda k, q: q == 0 or (k, q - 1) in SHARE)
    queries = [*split(own), b01a, b01b, *split(b03), *split(b10)]
    places = both(A00) + both(A01) + both(A03) + both(A10)
    real_job(row_ref, both(L_NXT), split(nxt), queries, places)
    put_ranks(ranks, [b01a, b01b])
    pair_job(
        row_ref, [ranks.at[0], ranks.at[1]], [b01a, b01b], split(b03), both(W03), both(K01),
        lambda k, q: (k, q) in SHARE,
    )
    limits = both(L_03) + both(L_10)
    real_job(row_ref, limits, split(b03) + split(b10), [prva], [PRV])


def half_kernel(h, row_ref, own, ownx, ranks, b01a, b01b, ranks1, nxt, prva, b13):
    own_job(row_ref, own, ownx, ranks, [b13], [W13 + h])
    pair_job(
        row_ref, [ranks1.at[0], ranks1.at[1]], [b01a, b01b], [b13], [W13 + h], both(K01), lambda k, q: (k, h) in SHARE
    )
    real_job(row_ref, both(L_NXT), split(nxt), [b13], [A13 + h])
    real_job(row_ref, [L_13 + h], [b13], [prva], [PRV])


def other_kernel(row_ref, own, b01a, b01b, b03, b10, nxtax, nxtbx):
    queries = [*split(own), b01a, b01b, *split(b03), *split(b10)]
    places = both(A00) + both(A01) + both(A03) + both(A10)
    real_job(row_ref, both(L_NXTX), [nxtax, nxtbx], queries, places)


def cross_kernel(row_ref, b03, b13a, b13b, nxtax, nxtbx, cross):
    b13 = [b13a, b13b]
    real_job(row_ref, both(L_NXTX), [nxtax, nxtbx], b13, both(A13))
    one = [cross.at[0], cross.at[1]]
    ranks = [rank_column(half[HALF:, : 2 * HALF]) for half in one]
    pair_job(
        row_ref, ranks, one, split(b03) + b13, both(W03) + both(W13), both(K01X),
        lambda k, q: (2 + k, q % 2) in SHARE,
    )


def prev_kernel(row_ref, b03, b10, b13a, b13b, cross, prvbx):
    limits = both(L_03) + both(L_10) + both(L_13)
    real_job(row_ref, limits, [*split(b03), *split(b10), b13a, b13b], [cross.at[2], prvbx], both(PRVX))


def end_kernel(row_ref, b03, b10, b13a, b13b, prvb):
    limits = both(L_13) + both(L_03) + both(L_10)
    real_job(row_ref, limits, [b13a, b13b, *split(b03), *split(b10)], [prvb], [PRV + 1])


def gather_kernel(rows_ref, swapped_ref, side_ref, kept_ref, to03_ref, to01_ref, prv_ref):
    within = jnp.maximum(rows_ref[W00 : W00 + 2, :], rows_ref[KOWN : KOWN + 2, :])
    within = jnp.maximum(within, jnp.maximum(swapped_ref[0:2, :], side_ref[0:2, :]))
    kept_ref[0:2, :] = jnp.maximum(within, -1.0)
    kept_ref[2:4, :] = jnp.maximum(jnp.maximum(rows_ref[A00 : A00 + 2, :], side_ref[2:4, :]), rows_ref[FLOOR : FLOOR + 1, :])
    kept_ref[4:6, :] = rows_ref[REAL : REAL + 2, :]
    kept_ref[6:8, :] = rows_ref[REAL : REAL + 2, :]
    to03_ref[...] = jnp.maximum(rows_ref[W03 : W03 + 4, :], side_ref[4:8, :])
    to01_ref[0:4, :] = rows_ref[W01 : W01 + 4, :]
    to01_ref[4:6, :] = jnp.maximum(rows_ref[K01 : K01 + 2, :], swapped_ref[2:4, :])
    prv_ref[0:2, :] = jnp.maximum(rows_ref[PRV : PRV + 2, :], swapped_ref[4:6, :])
    prv_ref[2:8, :] = rows_ref[0:6, :]


def final_kernel(kept, b03, b01, bprv, within_ref, adjacent_ref):
    for h in range(2):
        row = lambda ref, at: ref[at + h : at + h + 1, :]
        within = [row(kept, 0), row(b03, 0), row(b01, 0), row(b01, 4)]
        adjacent = [row(kept, 2), row(b03, 2), row(b01, 2), row(bprv, 0)]
        real = row(kept, 4) > 0
        place = slice(h * HALF, (h + 1) * HALF)
        within_ref[:, place] = jnp.where(real, functools.reduce(jnp.maximum, within), 0.0)
        adjacent_ref[:, place] = jnp.where(real, functools.reduce(jnp.maximum, adjacent), 0.0)


def small_call(name, body, shapes, arrays):
    return pl.pallas_call(
        body,
        in_specs=[VMEM] * len(arrays),
        out_specs=[VMEM] * len(shapes),
        out_shape=[jax.ShapeDtypeStruct(shape, jnp.float32) for shape in shapes],
        name=name,
        compiler_params=pltpu.CompilerParams(vmem_limit_bytes=2 * 2**20),
    )(*arrays)


def on_device(embeddings, sizes, ranks):
    rows = embeddings.shape[1]
    own, own_a, own_b = packed(embeddings[0], ranks, sizes)

    b01a = send("b01a", own_a, row=-1)
    b10 = send("b10", own, col=1)
    nxt = send("nxt", own, cluster=-1)
    b03 = send("b03", own, row=1)
    ownx = send("ownx", own, core=1)
    b01b = send("b01b", after(own_b, ownx), row=-1)
    empty = jnp.zeros((N_ROWS, HALF), jnp.float32)
    state, own_ranks = kernel_call("self", self_kernel, 1, empty, [own, ownx], [rank_shape(4)], [sizes])
    prva = send("prva", after(b01a, state), cluster=1)
    state = kernel_call("first", first_kernel, 0.5, state, [own, ownx, own_ranks, b01a])

    prvb = send("prvb", after(b01b, state), cluster=1)
    b10, b03, state = lax.optimization_barrier((b10, b03, state))
    nxt, b01b, prva, state = lax.optimization_barrier((nxt, b01b, prva, state))
    b13a = send("b13a", b03[0], col=1)
    b13b = send("b13b", b10[1], row=1)
    half = jax.ShapeDtypeStruct((HALF, D), jnp.bfloat16)
    bundle, nxta, nxtb = pl.pallas_call(
        bundle_kernel,
        in_specs=[VMEM] * 4,
        out_specs=[VMEM] * 3,
        out_shape=[jax.ShapeDtypeStruct((3, PAY, D), jnp.bfloat16), half, half],
        name="bundle",
        compiler_params=pltpu.CompilerParams(vmem_limit_bytes=8 * 2**20),
    )(b01a, b01b, nxt, prva)
    nxtax = send("nxtax", nxta, core=1)
    nxtbx = send("nxtbx", nxtb, core=1)
    state, ranks1 = kernel_call(
        "same", same_kernel, 4.5, state,
        [own, ownx, own_ranks, b01a, b01b, b03, b10, nxt, prva], [rank_shape(2)],
    )
    state = kernel_call("other", other_kernel, 0, state, [own, b01a, b01b, b03, b10, nxtax, nxtbx])
    cross = send("cross", after(bundle, state), core=1)
    kept = [own, ownx, own_ranks, b01a, b01b, ranks1, nxt, prva]
    state = kernel_call("left", functools.partial(half_kernel, 0), 1, state, [*kept, b13a])
    prvb, state = lax.optimization_barrier((prvb, state))
    state = kernel_call("right", functools.partial(half_kernel, 1), LONG, state, [*kept, b13b])
    prvbx = send("prvbx", prvb, core=1)
    state = kernel_call("cross", cross_kernel, 0, state, [b03, b13a, b13b, nxtax, nxtbx, cross])

    side = send("side", state[W10 : W10 + 8], col=1)
    state = kernel_call("prev", prev_kernel, 0, state, [b03, b10, b13a, b13b, cross, prvbx])
    swapped = send("swapped", state[KOWNX : KOWNX + 6], core=1)
    state = kernel_call("end", end_kernel, 1, state, [b03, b10, b13a, b13b, prvb])
    shapes = [(8, HALF), (4, HALF), (6, HALF), (8, HALF)]
    kept, to_03, to_01, to_prv = small_call("gather", gather_kernel, shapes, [state, swapped, side])
    back_prv = send("back_prv", to_prv, cluster=-1, row=1)
    back_01 = send("back_01", to_01, row=1)
    back_03 = send("back_03", to_03, row=-1)
    return tuple(small_call("final", final_kernel, [(1, rows)] * 2, [kept, back_03, back_01, back_prv]))


def solution(mesh):
    in_specs = (P("group", "helper", None), P(), P("group", "helper"))
    out_specs = (P("group", "helper"), P("group", "helper"))
    return jax.shard_map(
        on_device, mesh=mesh, in_specs=in_specs, out_specs=out_specs, check_vma=False
    )
```
